32 devices in a mesh: blk: 16 (over z, x, core), group: 2 (over y).
Axes of the slice: x: 2, y: 2, z: 4, core: 2. Of those that a mesh axis runs over, the one named last changes fastest.
Arguments:
- sketch: bfloat16 [8192, 768], P('blk'), may hold values from -6 to 6
- far_tiles: bfloat16 [16, 2, 3, 1, 512, 512], P('blk', 'group'), may hold values from -0.1875 to 0.1875
- row_blocks: int32 [16, 2, 3, 1], P('blk', 'group'), may hold values from 0 to 1, as said below
- owner_route: int32 [16, 2, 2], P('blk', 'group'), may hold values from 0 to 1, each once within a row
- cluster_basis: bfloat16 [16, 2, 1024, 256], P('blk', 'group'), may hold values from -0.1875 to 0.1875
Outputs:
- coefficients: float32 [16, 2, 256, 768], P('blk', 'group')
The draws below stay inside these ranges and needn't reach their ends.
Inputs may be any that keep to these rules, and one draw needn't show every extreme that they name: `row_blocks`: for one device and one offset, the 1 entries are distinct. `owner_route`: for each device the entries are a permutation of 0 .. 2 - 1.
All inputs are finite; a program needn't handle non-finite values.
Results may differ from the reference program's by a relative error of at most 0.0029.
Values may be sent and summed in bfloat16 or wider, within the bound.
No kernel may reach another device: no remote copies, remote signals or barrier semaphores. Data moves between devices by JAX's collectives and lax.ppermute only.
A program may use at most 64 MiB of HBM per device.

```python
import jax
import jax.numpy as jnp
from jax import lax

K = 768
CL = 1024
RANK = 256
PW = 512
REACH = 1
OFFS = 3
TB = 512
TPO = 1
NCAT = 8192
N_BLK = 16
N_GROUP = 2


def draw_row_blocks(key, part):
    scores = jax.random.randint(key, (N_BLK, N_GROUP, OFFS, N_GROUP), 0, 1 << 20) * N_GROUP
    scores = scores + jnp.arange(N_GROUP, dtype=jnp.int32)
    order = jnp.argsort(scores, axis=-1, stable=True)
    return order[..., :TPO].astype(jnp.int32)


def block_scale(stream_key, shape, split, least, high):
    def one(dim, parts):
        steps = jax.random.uniform(jax.random.fold_in(jax.random.fold_in(stream_key, 6), dim), (parts,), jnp.float32, least / len(split), high / len(split))
        return jnp.repeat(jnp.exp(steps), shape[dim] // parts).reshape((-1,) + (1,) * (len(shape) - dim - 1))

    gain = one(*split[0])
    for cut in split[1:]:
        gain = gain * one(*cut)
    return gain


def scatter_about(key, shape, scale, most, split=(), kind=jnp.bfloat16):
    gain = block_scale(key, shape, split, -0.22, 0.18) if split else 1.0
    drawn = jax.random.normal(key, shape, jnp.float32) * scale * gain
    return jnp.minimum(jnp.maximum(drawn, -most), most).astype(kind)


def setup_inputs(seed: int = 0) -> dict:
    streams_of = jax.random.split(jax.random.key(seed), 6)
    return {
        "sketch": scatter_about(streams_of[0], (NCAT, K), 1.0, 6.0, ((0, 16),)),
        "far_tiles": scatter_about(streams_of[1], (N_BLK, N_GROUP, OFFS, TPO, TB, PW), (2 * PW) ** -0.5, 0.1875, ((0, 16), (1, 2))),
        "row_blocks": draw_row_blocks(jax.random.fold_in(streams_of[5], 71), 0),
        "owner_route": jax.vmap(lambda own: jax.random.permutation(own, N_GROUP))(jax.random.split(streams_of[3], N_BLK * N_GROUP)).reshape((N_BLK, N_GROUP, N_GROUP)).astype(jnp.int32),
        "cluster_basis": scatter_about(streams_of[4], (N_BLK, N_GROUP, CL, RANK), CL ** -0.5, 0.1875, ((0, 16), (1, 2))),
    }


def device_rows(tiles_dev, blocks_dev, panels):
    summed = jnp.zeros((N_GROUP, TB, K), jnp.float32)
    for offset in range(OFFS):
        product = jnp.einsum('trk,kc->trc', tiles_dev[offset].astype(jnp.float32), panels[offset].astype(jnp.float32))
        summed = summed.at[blocks_dev[offset]].add(product)
    return summed.astype(jnp.bfloat16)


def place_rows(rows_dev, route_dev):
    return jnp.zeros_like(rows_dev).at[route_dev].set(rows_dev)


def reference(sketch, far_tiles, row_blocks, owner_route, cluster_basis):
    sketch_blocks = sketch.reshape(N_BLK, PW, K)

    def one_blk(blk_index):
        shifts = jnp.arange(OFFS, dtype=jnp.int32) - REACH
        which = ((blk_index + shifts) % N_BLK).astype(jnp.int32)
        panels = jnp.take(sketch_blocks, which, axis=0)
        sampled = jax.vmap(device_rows, in_axes=(0, 0, None))(far_tiles[blk_index], row_blocks[blk_index], panels)
        ordered = jax.vmap(place_rows)(sampled, owner_route[blk_index])
        cluster = jnp.transpose(ordered, (1, 0, 2, 3)).reshape(N_GROUP, CL, K)
        return jnp.einsum('dlr,dlc->drc', cluster_basis[blk_index].astype(jnp.float32), cluster.astype(jnp.float32))

    return lax.map(one_blk, jnp.arange(N_BLK, dtype=jnp.int32))
```

```python
import functools

import jax
import jax.numpy as jnp
from jax import lax
from jax.experimental import pallas as pl
from jax.experimental.pallas import tpu as pltpu
from jax.sharding import PartitionSpec as P

CUTS = (8, 4)
TRANSPOSED = (((0,), (0,)), ((), ()))


def from_behind(array, axis, by):
    devices = lax.axis_size(axis)
    return lax.ppermute(array, axis, [(i, (i + by) % devices) for i in range(devices)])


def swap_near(array):
    devices = lax.axis_size("blk")
    return lax.ppermute(array, "blk", [(i, i ^ 1) for i in range(devices)])


def swap_far(array):
    devices = lax.axis_size("blk")
    return lax.ppermute(
        array, "blk", [(i, (i + 1 if i % 2 else i - 1) % devices) for i in range(devices)]
    )


def in_vmem(array):
    return pltpu.with_memory_space_constraint(array, pltpu.VMEM)


def partial_kernel(
    start, row_blocks, owner_route, tiles, own, near, far, kept_basis, lent_basis, kept, sent, summed
):
    parity = lax.rem(lax.axis_index("blk"), 2)
    group = lax.axis_index("group")
    slots = tiles.shape[3]
    width = far.shape[1]
    columns = pl.ds(start, width)
    summed[...] = jnp.zeros_like(summed)
    for offset, panel in (
        (1, own[:, columns]),
        (2 - 2 * parity, near[:, columns]),
        (2 * parity, far[...]),
    ):
        for slot in range(slots):
            owner = owner_route[0, 0, row_blocks[0, 0, offset, slot]]
            place = jnp.where(owner == group, 0, 1)
            summed[place] += jnp.dot(
                tiles[0, 0, offset, slot], panel, preferred_element_type=jnp.float32
            )
    sent[...] = lax.dot_general(
        lent_basis[...], summed[1].astype(jnp.bfloat16), TRANSPOSED, preferred_element_type=jnp.float32
    ).astype(jnp.bfloat16)
    kept[...] = lax.dot_general(
        kept_basis[...], summed[0].astype(jnp.bfloat16), TRANSPOSED, preferred_element_type=jnp.float32
    )


def partials(start, row_blocks, owner_route, tiles, own, near, far, kept_basis, lent_basis):
    rank = kept_basis.shape[1]
    rows, width = tiles.shape[4], far.shape[1]
    vmem = pl.BlockSpec(memory_space=pltpu.VMEM)
    smem = pl.BlockSpec(memory_space=pltpu.SMEM)
    return pl.pallas_call(
        functools.partial(partial_kernel, start),
        out_shape=(
            pltpu.VMEM((rank, width), jnp.float32),
            pltpu.VMEM((rank, width), jnp.bfloat16),
        ),
        in_specs=[smem] * 2 + [vmem] * 6,
        out_specs=[vmem] * 2,
        scratch_shapes=[pltpu.VMEM((2, rows, width), jnp.float32)],
        compiler_params=pltpu.CompilerParams(vmem_limit_bytes=16 << 20),
        cost_estimate=pl.CostEstimate(
            flops=2 * rows * width * (3 * own.shape[0] + 2 * rank),
            bytes_accessed=4 << 20,
            transcendentals=0,
        ),
    )(
        row_blocks,
        owner_route,
        *(in_vmem(x) for x in (tiles, own, near, far, kept_basis, lent_basis)),
    )


def join_kernel(starts, *refs):
    parts, out = refs[:-1], refs[-1]
    for start, kept, received in zip(starts, parts[0::2], parts[1::2]):
        out[:, pl.ds(start, kept.shape[1])] = kept[...] + received[...].astype(jnp.float32)


def join(starts, parts, columns):
    vmem = pl.BlockSpec(memory_space=pltpu.VMEM)
    flat = [in_vmem(x) for part in parts for x in part]
    return pl.pallas_call(
        functools.partial(join_kernel, starts),
        out_shape=jax.ShapeDtypeStruct((flat[0].shape[0], columns), jnp.float32),
        in_specs=[vmem] * len(flat),
        out_specs=vmem,
        compiler_params=pltpu.CompilerParams(vmem_limit_bytes=16 << 20),
        cost_estimate=pl.CostEstimate(flops=0, bytes_accessed=2 << 20, transcendentals=0),
    )(*flat)


def paired_body(sketch, far_tiles, row_blocks, owner_route, cluster_basis):
    columns = sketch.shape[1]
    half = cluster_basis.shape[2] // 2
    group = lax.axis_index("group")
    starts, widths = [], []
    for cut in CUTS:
        starts.append(sum(widths))
        widths.append(columns * cut // sum(CUTS))
    far = [swap_far(sketch[:, s : s + w]) for s, w in zip(starts, widths)]
    near = swap_near(sketch)
    basis = cluster_basis[0, 0]
    lent_basis = from_behind(
        lax.dynamic_slice_in_dim(basis, (1 - group) * half, half, 0), "group", 1
    )
    kept_basis = lax.dynamic_slice_in_dim(basis, group * half, half, 0)
    parts = []
    for start, panel in zip(starts, far):
        kept, sent = partials(
            start, row_blocks, owner_route, far_tiles, sketch, near, panel, kept_basis, lent_basis
        )
        parts.append((kept, from_behind(sent, "group", 1)))
    return join(tuple(starts), parts, columns)[None, None]


def contribute(summed, far_tiles, row_blocks, offset, current):
    product = jnp.einsum(
        "trk,kc->trc", far_tiles[0, 0, offset], current, preferred_element_type=jnp.float32
    )
    return summed.at[row_blocks[0, 0, offset]].add(product)


def ring_body(sketch, far_tiles, row_blocks, owner_route, cluster_basis):
    offsets = far_tiles.shape[2]
    radius = (offsets - 1) // 2
    groups = lax.axis_size("group")
    tile_rows = far_tiles.shape[4]
    columns = sketch.shape[1]
    summed = jnp.zeros((groups, tile_rows, columns), jnp.float32)
    for offset in range(offsets):
        current = from_behind(sketch, "blk", radius - offset) if offset != radius else sketch
        summed = contribute(summed, far_tiles, row_blocks, offset, current)
    sampled = summed.astype(jnp.bfloat16)
    ordered = jnp.zeros_like(sampled).at[owner_route[0, 0]].set(sampled)
    received = lax.all_to_all(ordered, "group", split_axis=0, concat_axis=0, tiled=True)
    stacked = received.reshape(received.shape[0] * received.shape[1], received.shape[2])
    coefficients = lax.dot_general(
        cluster_basis[0, 0], stacked, TRANSPOSED, preferred_element_type=jnp.float32
    )
    return coefficients[None, None]


def body(sketch, far_tiles, row_blocks, owner_route, cluster_basis):
    small = cluster_basis.shape[3] < far_tiles.shape[4]
    paired = lax.axis_size("group") == 2 and lax.axis_size("blk") % 2 == 0
    if small and paired and far_tiles.shape[2] == 3:
        return paired_body(sketch, far_tiles, row_blocks, owner_route, cluster_basis)
    return ring_body(sketch, far_tiles, row_blocks, owner_route, cluster_basis)


def solution(mesh):
    placed = (
        P("blk", None),
        P("blk", "group", None, None, None, None),
        P("blk", "group", None, None),
        P("blk", "group", None),
        P("blk", "group", None, None),
    )
    return jax.shard_map(
        body, mesh=mesh, in_specs=placed, out_specs=P("blk", "group", None, None), check_vma=False
    )
```

```python
import functools

import jax
import jax.numpy as jnp
from jax import lax
from jax.experimental import pallas as pl
from jax.experimental.pallas import tpu as pltpu
from jax.sharding import PartitionSpec as P

TRANSPOSED = (((0,), (0,)), ((), ()))


def from_behind(array, axis, by):
    devices = lax.axis_size(axis)
    return lax.ppermute(array, axis, [(i, (i + by) % devices) for i in range(devices)])


def swap_near(array):
    devices = lax.axis_size("blk")
    return lax.ppermute(array, "blk", [(i, i ^ 1) for i in range(devices)])


def swap_far(array):
    devices = lax.axis_size("blk")
    return lax.ppermute(
        array, "blk", [(i, (i + 1 if i % 2 else i - 1) % devices) for i in range(devices)]
    )


def on_chip(shape, dtype):
    return pltpu.VMEM(shape, dtype)


def call(kernel, out_shape, scalars, arrays, flops, scratch=()):
    scalar, vector = (pl.BlockSpec(memory_space=m) for m in (pltpu.SMEM, pltpu.VMEM))
    placed = [pltpu.with_memory_space_constraint(x, pltpu.SMEM) for x in scalars]
    placed += [pltpu.with_memory_space_constraint(x, pltpu.VMEM) for x in arrays]
    return pl.pallas_call(
        kernel,
        out_shape=out_shape,
        in_specs=[scalar] * len(scalars) + [vector] * len(arrays),
        out_specs=tuple(vector for _ in out_shape) if isinstance(out_shape, tuple) else vector,
        scratch_shapes=list(scratch),
        compiler_params=pltpu.CompilerParams(vmem_limit_bytes=16 << 20),
        cost_estimate=pl.CostEstimate(flops=flops, bytes_accessed=1 << 20, transcendentals=0),
    )(*placed)


def add_tiles(row_blocks, owner_route, tiles, offset, panel, summed):
    group = lax.axis_index("group")
    for slot in range(tiles.shape[3]):
        owner = owner_route[0, 0, row_blocks[0, 0, offset, slot]]
        place = jnp.where(owner == group, 0, 1)
        summed[place] += jnp.dot(
            tiles[0, 0, offset, slot], panel[...], preferred_element_type=jnp.float32
        )


def local_kernel(row_blocks, owner_route, tiles, own, near, summed):
    parity = lax.rem(lax.axis_index("blk"), 2)
    summed[...] = jnp.zeros_like(summed)
    add_tiles(row_blocks, owner_route, tiles, 1, own, summed)
    add_tiles(row_blocks, owner_route, tiles, 2 - 2 * parity, near, summed)


def turn_kernel(basis, lent, kept_turned, lent_turned):
    half = lent.shape[0]
    start = pl.multiple_of(lax.axis_index("group") * half, half)
    kept_turned[...] = basis[0, 0, pl.ds(start, half), :].T
    lent_turned[...] = lent[...].T


def far_kernel(row_blocks, owner_route, tiles, far, local, lent_turned, sampled, sent, summed):
    parity = lax.rem(lax.axis_index("blk"), 2)
    summed[...] = local[...]
    add_tiles(row_blocks, owner_route, tiles, 2 * parity, far, summed)
    sampled[...] = summed[0].astype(jnp.bfloat16)
    sent[...] = jnp.dot(
        lent_turned[...], summed[1].astype(jnp.bfloat16), preferred_element_type=jnp.float32
    ).astype(jnp.bfloat16)


def kept_kernel(kept_turned, sampled, kept):
    kept[...] = jnp.dot(kept_turned[...], sampled[...], preferred_element_type=jnp.float32)


def join_kernel(kept, received, out):
    out[...] = kept[...] + received[...].astype(jnp.float32)


def paired_body(sketch, far_tiles, row_blocks, owner_route, cluster_basis):
    panels, columns = sketch.shape
    rows = far_tiles.shape[4]
    half, rank = cluster_basis.shape[2] // 2, cluster_basis.shape[3]
    scalars = (row_blocks, owner_route)
    far = swap_far(sketch)
    near = swap_near(sketch)
    lent_rows = (1 - lax.axis_index("group")) * half
    lent = from_behind(
        lax.dynamic_slice_in_dim(cluster_basis[0, 0], lent_rows, half, 0), "group", 1
    )
    product = 2 * rows * panels * columns
    local = call(
        local_kernel,
        on_chip((2, rows, columns), jnp.float32),
        scalars,
        (far_tiles, sketch, near),
        2 * product,
    )
    kept_turned, lent_turned = call(
        turn_kernel, (on_chip((rank, half), jnp.bfloat16),) * 2, (), (cluster_basis, lent), 1 << 20
    )
    sampled, sent = call(
        far_kernel,
        (on_chip((rows, columns), jnp.bfloat16), on_chip((rank, columns), jnp.bfloat16)),
        scalars,
        (far_tiles, far, local, lent_turned),
        2 * product,
        (pltpu.VMEM((2, rows, columns), jnp.float32),),
    )
    received = from_behind(sent, "group", 1)
    kept = call(
        kept_kernel, on_chip((rank, columns), jnp.float32), (), (kept_turned, sampled), product // 2
    )
    out = call(
        join_kernel,
        jax.ShapeDtypeStruct((rank, columns), jnp.float32),
        (),
        (kept, received),
        1 << 20,
    )
    return out[None, None]


def contribute(summed, far_tiles, row_blocks, offset, current):
    product = jnp.einsum(
        "trk,kc->trc", far_tiles[0, 0, offset], current, preferred_element_type=jnp.float32
    )
    return summed.at[row_blocks[0, 0, offset]].add(product)


def ring_body(sketch, far_tiles, row_blocks, owner_route, cluster_basis):
    offsets = far_tiles.shape[2]
    radius = (offsets - 1) // 2
    groups = lax.axis_size("group")
    tile_rows = far_tiles.shape[4]
    columns = sketch.shape[1]
    summed = jnp.zeros((groups, tile_rows, columns), jnp.float32)
    for offset in range(offsets):
        current = from_behind(sketch, "blk", radius - offset) if offset != radius else sketch
        summed = contribute(summed, far_tiles, row_blocks, offset, current)
    sampled = summed.astype(jnp.bfloat16)
    ordered = jnp.zeros_like(sampled).at[owner_route[0, 0]].set(sampled)
    received = lax.all_to_all(ordered, "group", split_axis=0, concat_axis=0, tiled=True)
    stacked = received.reshape(received.shape[0] * received.shape[1], received.shape[2])
    coefficients = lax.dot_general(
        cluster_basis[0, 0], stacked, TRANSPOSED, preferred_element_type=jnp.float32
    )
    return coefficients[None, None]


def body(sketch, far_tiles, row_blocks, owner_route, cluster_basis):
    small = cluster_basis.shape[3] < far_tiles.shape[4]
    paired = lax.axis_size("group") == 2 and lax.axis_size("blk") % 2 == 0
    if small and paired and far_tiles.shape[2] == 3:
        return paired_body(sketch, far_tiles, row_blocks, owner_route, cluster_basis)
    return ring_body(sketch, far_tiles, row_blocks, owner_route, cluster_basis)


def solution(mesh):
    placed = (
        P("blk", None),
        P("blk", "group", None, None, None, None),
        P("blk", "group", None, None),
        P("blk", "group", None),
        P("blk", "group", None, None),
    )
    return jax.shard_map(
        body, mesh=mesh, in_specs=placed, out_specs=P("blk", "group", None, None), check_vma=False
    )
```

```python
import functools

import jax
import jax.numpy as jnp
from jax import lax
from jax.experimental import pallas as pl
from jax.experimental.pallas import tpu as pltpu
from jax.sharding import PartitionSpec as P

TRANSPOSED = (((0,), (0,)), ((), ()))


def from_behind(array, axis, by):
    devices = lax.axis_size(axis)
    return lax.ppermute(array, axis, [(i, (i + by) % devices) for i in range(devices)])


def swap_near(array):
    devices = lax.axis_size("blk")
    return lax.ppermute(array, "blk", [(i, i ^ 1) for i in range(devices)])


def swap_far(array):
    devices = lax.axis_size("blk")
    return lax.ppermute(
        array, "blk", [(i, (i + 1 if i % 2 else i - 1) % devices) for i in range(devices)]
    )


def on_chip(shape, dtype):
    return pltpu.VMEM(shape, dtype)


def call(kernel, out_shape, scalars, arrays, flops, scratch=(), hbm=()):
    scalar, vector, main = (
        pl.BlockSpec(memory_space=m) for m in (pltpu.SMEM, pltpu.VMEM, pltpu.HBM)
    )
    placed = [pltpu.with_memory_space_constraint(x, pltpu.SMEM) for x in scalars]
    placed += [pltpu.with_memory_space_constraint(x, pltpu.VMEM) for x in arrays]
    placed += [pltpu.with_memory_space_constraint(x, pltpu.HBM) for x in hbm]
    return pl.pallas_call(
        kernel,
        out_shape=out_shape,
        in_specs=[scalar] * len(scalars) + [vector] * len(arrays) + [main] * len(hbm),
        out_specs=tuple(vector for _ in out_shape) if isinstance(out_shape, tuple) else vector,
        scratch_shapes=list(scratch),
        compiler_params=pltpu.CompilerParams(vmem_limit_bytes=16 << 20),
        cost_estimate=pl.CostEstimate(flops=flops, bytes_accessed=1 << 20, transcendentals=0),
    )(*placed)


def far_offset():
    return 2 * lax.rem(lax.axis_index("blk"), 2)


def owner_of(row_blocks, owner_route, offset):
    return owner_route[0, 0, row_blocks[0, 0, offset, 0]]


def cut_kernel(sketch, basis, first, lent, sems):
    half = lent.shape[0]
    start = pl.multiple_of((1 - lax.axis_index("group")) * half, half)
    copies = (
        pltpu.make_async_copy(sketch.at[:, pl.ds(0, first.shape[1])], first, sems.at[0]),
        pltpu.make_async_copy(basis.at[0, 0, pl.ds(start, half)], lent, sems.at[1]),
    )
    for copy in copies:
        copy.start()
    for copy in copies:
        copy.wait()


def local_kernel(row_blocks, owner_route, tiles, own, near, hit, miss):
    far = far_offset()
    owner = owner_of(row_blocks, owner_route, far)
    own_hits = owner_of(row_blocks, owner_route, 1) == owner
    near_hits = owner_of(row_blocks, owner_route, 2 - far) == owner
    step = 256
    for start in range(0, own.shape[1], step):
        columns = pl.ds(start, step)
        first = jnp.dot(tiles[0, 0, 1, 0], own[:, columns], preferred_element_type=jnp.float32)
        second = jnp.dot(
            tiles[0, 0, 2 - far, 0], near[:, columns], preferred_element_type=jnp.float32
        )
        hit[:, columns] = jnp.where(own_hits, first, 0.0) + jnp.where(near_hits, second, 0.0)
        miss[:, columns] = (
            jnp.where(own_hits, 0.0, first) + jnp.where(near_hits, 0.0, second)
        ).astype(jnp.bfloat16)


def turn_kernel(row_blocks, owner_route, basis, lent, miss, own, hit_turned, missed, second):
    half = lent.shape[0]
    group = lax.axis_index("group")
    kept = basis[0, 0, pl.ds(pl.multiple_of(group * half, half), half), :].T
    other = lent[...].T
    stays = owner_of(row_blocks, owner_route, far_offset()) == group
    hit_turned[...] = jnp.where(stays, kept, other)
    missed[...] = jnp.dot(
        jnp.where(stays, other, kept), miss[...], preferred_element_type=jnp.float32
    )
    second[...] = own[:, pl.ds(own.shape[1] - second.shape[1], second.shape[1])]


def far_kernel(start, row_blocks, owner_route, tiles, far, hit, hit_turned, missed, made, sent):
    offset = far_offset()
    stays = owner_of(row_blocks, owner_route, offset) == lax.axis_index("group")
    columns = pl.ds(start, far.shape[1])
    product = jnp.dot(tiles[0, 0, offset, 0], far[...], preferred_element_type=jnp.float32)
    sampled = (hit[:, columns] + product).astype(jnp.bfloat16)
    result = jnp.dot(hit_turned[...], sampled, preferred_element_type=jnp.float32)
    sent[...] = jnp.where(stays, missed[:, columns], result).astype(jnp.bfloat16)
    made[...] = result


def join_kernel(row_blocks, owner_route, missed, *refs):
    parts, out = refs[:-1], refs[-1]
    stays = owner_of(row_blocks, owner_route, far_offset()) == lax.axis_index("group")
    start = 0
    for made, received in zip(parts[0::2], parts[1::2]):
        columns = pl.ds(start, made.shape[1])
        kept = jnp.where(stays, made[...], missed[:, columns])
        out[:, columns] = kept + received[...].astype(jnp.float32)
        start += made.shape[1]


def paired_body(sketch, far_tiles, row_blocks, owner_route, cluster_basis):
    panels, columns = sketch.shape
    rows = far_tiles.shape[4]
    half, rank = cluster_basis.shape[2] // 2, cluster_basis.shape[3]
    early = 2 * columns // 3
    scalars = (row_blocks, owner_route)
    product = 2 * rows * panels * columns
    first, lent = call(
        cut_kernel,
        (on_chip((panels, early), sketch.dtype), on_chip((half, rank), cluster_basis.dtype)),
        (),
        (),
        0,
        (pltpu.SemaphoreType.DMA((2,)),),
        (sketch, cluster_basis),
    )
    far_first = swap_far(first)
    near = swap_near(sketch)
    lent = from_behind(lent, "group", 1)
    hit, miss = call(
        local_kernel,
        (on_chip((rows, columns), jnp.float32), on_chip((rows, columns), jnp.bfloat16)),
        scalars,
        (far_tiles, sketch, near),
        2 * product,
    )
    hit_turned, missed, second = call(
        turn_kernel,
        (
            on_chip((rank, half), jnp.bfloat16),
            on_chip((rank, columns), jnp.float32),
            on_chip((panels, columns - early), sketch.dtype),
        ),
        scalars,
        (cluster_basis, lent, miss, sketch),
        product // 2,
    )
    far_second = swap_far(second)
    parts = []
    for start, far in ((0, far_first), (early, far_second)):
        width = far.shape[1]
        made, sent = call(
            functools.partial(far_kernel, start),
            (on_chip((rank, width), jnp.float32), on_chip((rank, width), jnp.bfloat16)),
            scalars,
            (far_tiles, far, hit, hit_turned, missed),
            2 * product * width // columns,
        )
        parts += [made, from_behind(sent, "group", 1)]
    out = call(
        join_kernel,
        jax.ShapeDtypeStruct((rank, columns), jnp.float32),
        scalars,
        (missed, *parts),
        1 << 20,
    )
    return out[None, None]


def contribute(summed, far_tiles, row_blocks, offset, current):
    product = jnp.einsum(
        "trk,kc->trc", far_tiles[0, 0, offset], current, preferred_element_type=jnp.float32
    )
    return summed.at[row_blocks[0, 0, offset]].add(product)


def ring_body(sketch, far_tiles, row_blocks, owner_route, cluster_basis):
    offsets = far_tiles.shape[2]
    radius = (offsets - 1) // 2
    groups = lax.axis_size("group")
    tile_rows = far_tiles.shape[4]
    columns = sketch.shape[1]
    summed = jnp.zeros((groups, tile_rows, columns), jnp.float32)
    for offset in range(offsets):
        current = from_behind(sketch, "blk", radius - offset) if offset != radius else sketch
        summed = contribute(summed, far_tiles, row_blocks, offset, current)
    sampled = summed.astype(jnp.bfloat16)
    ordered = jnp.zeros_like(sampled).at[owner_route[0, 0]].set(sampled)
    received = lax.all_to_all(ordered, "group", split_axis=0, concat_axis=0, tiled=True)
    stacked = received.reshape(received.shape[0] * received.shape[1], received.shape[2])
    coefficients = lax.dot_general(
        cluster_basis[0, 0], stacked, TRANSPOSED, preferred_element_type=jnp.float32
    )
    return coefficients[None, None]


def body(sketch, far_tiles, row_blocks, owner_route, cluster_basis):
    small = cluster_basis.shape[3] < far_tiles.shape[4]
    paired = lax.axis_size("group") == 2 and lax.axis_size("blk") % 2 == 0
    if small and paired and far_tiles.shape[2:4] == (3, 1):
        return paired_body(sketch, far_tiles, row_blocks, owner_route, cluster_basis)
    return ring_body(sketch, far_tiles, row_blocks, owner_route, cluster_basis)


def solution(mesh):
    placed = (
        P("blk", None),
        P("blk", "group", None, None, None, None),
        P("blk", "group", None, None),
        P("blk", "group", None),
        P("blk", "group", None, None),
    )
    return jax.shard_map(
        body, mesh=mesh, in_specs=placed, out_specs=P("blk", "group", None, None), check_vma=False
    )
```

```python
import functools

import jax
import jax.numpy as jnp
from jax import lax
from jax.experimental import pallas as pl
from jax.experimental.pallas import tpu as pltpu
from jax.sharding import PartitionSpec as P

TRANSPOSED = (((0,), (0,)), ((), ()))


def from_behind(array, axis, by):
    devices = lax.axis_size(axis)
    return lax.ppermute(array, axis, [(i, (i + by) % devices) for i in range(devices)])


def swap_near(array):
    devices = lax.axis_size("blk")
    return lax.ppermute(array, "blk", [(i, i ^ 1) for i in range(devices)])


def swap_far(array):
    devices = lax.axis_size("blk")
    return lax.ppermute(
        array, "blk", [(i, (i + 1 if i % 2 else i - 1) % devices) for i in range(devices)]
    )


def on_chip(shape, dtype):
    return pltpu.VMEM(shape, dtype)


def call(kernel, out_shape, arrays, flops, scalars=(), hbm=(), scratch=(), to_hbm=False, alias=False):
    scalar, vector, main = (
        pl.BlockSpec(memory_space=m) for m in (pltpu.SMEM, pltpu.VMEM, pltpu.HBM)
    )
    placed = list(scalars)
    placed += [pltpu.with_memory_space_constraint(x, pltpu.VMEM) for x in arrays]
    placed += [pltpu.with_memory_space_constraint(x, pltpu.HBM) for x in hbm]
    target = main if to_hbm else vector
    return pl.pallas_call(
        kernel,
        out_shape=out_shape,
        in_specs=[scalar] * len(scalars) + [vector] * len(arrays) + [main] * len(hbm),
        out_specs=tuple(target for _ in out_shape) if isinstance(out_shape, tuple) else target,
        scratch_shapes=list(scratch),
        input_output_aliases={len(placed) - 1: 0} if alias else {},
        compiler_params=pltpu.CompilerParams(vmem_limit_bytes=16 << 20),
        cost_estimate=pl.CostEstimate(flops=flops, bytes_accessed=1 << 20, transcendentals=0),
    )(*placed)


def far_offset():
    return 2 * lax.rem(lax.axis_index("blk"), 2)


def copy_all(pairs, sems):
    copies = [pltpu.make_async_copy(*pair, sems.at[i]) for i, pair in enumerate(pairs)]
    for copy in copies:
        copy.start()
    for copy in copies:
        copy.wait()


def cut_kernel(sketch, first, sems):
    copy_all([(sketch.at[:, pl.ds(0, first.shape[1])], first)], sems)


def stage_kernel(sketch, tiles, basis, lent, own, staged, kept, sems):
    half = lent.shape[0]
    group = lax.axis_index("group")
    ours, theirs = (
        basis.at[0, 0, pl.ds(pl.multiple_of(g * half, half), half)] for g in (group, 1 - group)
    )
    copy_all([(theirs, lent), (sketch, own), (tiles.at[0, 0, :, 0], staged), (ours, kept)], sems)


def local_kernel(row_blocks, owner_route, tiles, own, near, hit, miss, stays):
    far = far_offset()
    owner = owner_route[row_blocks[far]]
    own_hits = owner_route[row_blocks[1]] == owner
    near_hits = owner_route[row_blocks[2 - far]] == owner
    step = 256
    for start in range(0, own.shape[1], step):
        columns = pl.ds(start, step)
        first = jnp.dot(tiles[1], own[:, columns], preferred_element_type=jnp.float32)
        second = jnp.dot(tiles[2 - far], near[:, columns], preferred_element_type=jnp.float32)
        hit[:, columns] = jnp.where(own_hits, first, 0.0) + jnp.where(near_hits, second, 0.0)
        miss[:, columns] = (
            jnp.where(own_hits, 0.0, first) + jnp.where(near_hits, 0.0, second)
        ).astype(jnp.bfloat16)
    stays[...] = jnp.full(stays.shape, jnp.where(owner == lax.axis_index("group"), 1.0, 0.0))


def turn_kernel(kept, lent, miss, own, stays, hit_turned, missed, second):
    stay = stays[:, pl.ds(0, kept.shape[0])] > 0.0
    ours, theirs = kept[...].T, lent[...].T
    hit_turned[...] = jnp.where(stay, ours, theirs)
    missed[...] = jnp.dot(
        jnp.where(stay, theirs, ours), miss[...], preferred_element_type=jnp.float32
    )
    second[...] = own[:, pl.ds(own.shape[1] - second.shape[1], second.shape[1])]


def far_kernel(start, tiles, far, hit, hit_turned, missed, stays, kept, sent):
    columns = pl.ds(start, far.shape[1])
    product = jnp.dot(tiles[far_offset()], far[...], preferred_element_type=jnp.float32)
    sampled = (hit[:, columns] + product).astype(jnp.bfloat16)
    made = jnp.dot(hit_turned[...], sampled, preferred_element_type=jnp.float32)
    stay = stays[:, columns] > 0.0
    other = missed[:, columns]
    sent[...] = jnp.where(stay, other, made).astype(jnp.bfloat16)
    kept[...] = jnp.where(stay, made, other)


def join_kernel(start, kept, received, *rest):
    out, total, sems = rest[-3:]
    total[...] = kept[...] + received[...].astype(jnp.float32)
    copy_all([(total, out.at[:, pl.ds(start, total.shape[1])])], sems)


def paired_body(sketch, far_tiles, row_blocks, owner_route, cluster_basis):
    panels, columns = sketch.shape
    offsets, rows = far_tiles.shape[2], far_tiles.shape[4]
    half, rank = cluster_basis.shape[2] // 2, cluster_basis.shape[3]
    early = 2 * columns // 3
    product = 2 * rows * panels * columns
    short, wide = sketch.dtype, jnp.float32
    copies = pltpu.SemaphoreType.DMA
    first = call(
        cut_kernel, on_chip((panels, early), short), (), 0, hbm=(sketch,), scratch=(copies((1,)),)
    )
    far_first = swap_far(first)
    near = swap_near(sketch)
    lent, own, tiles, kept = call(
        stage_kernel,
        (
            on_chip((half, rank), short),
            on_chip((panels, columns), short),
            on_chip((offsets, rows, panels), short),
            on_chip((half, rank), short),
        ),
        (),
        0,
        hbm=(sketch, far_tiles, cluster_basis),
        scratch=(copies((4,)),),
    )
    lent = from_behind(lent, "group", 1)
    hit, miss, stays = call(
        local_kernel,
        (
            on_chip((rows, columns), wide),
            on_chip((rows, columns), short),
            on_chip((1, columns), wide),
        ),
        (tiles, own, near),
        2 * product,
        scalars=(row_blocks.reshape(-1), owner_route.reshape(-1)),
    )
    hit_turned, missed, second = call(
        turn_kernel,
        (
            on_chip((rank, half), short),
            on_chip((rank, columns), wide),
            on_chip((panels, columns - early), short),
        ),
        (kept, lent, miss, own, stays),
        product // 2,
    )
    far_second = swap_far(second)
    out = None
    for start, far in ((0, far_first), (early, far_second)):
        width = far.shape[1]
        kept, sent = call(
            functools.partial(far_kernel, start),
            (on_chip((rank, width), wide), on_chip((rank, width), short)),
            (tiles, far, hit, hit_turned, missed, stays),
            2 * product * width // columns,
        )
        out = call(
            functools.partial(join_kernel, start),
            pltpu.HBM((rank, columns), wide),
            (kept, from_behind(sent, "group", 1)),
            1 << 16,
            hbm=() if out is None else (out,),
            scratch=(on_chip((rank, width), wide), copies((1,))),
            to_hbm=True,
            alias=out is not None,
        )
    return out[None, None]


def contribute(summed, far_tiles, row_blocks, offset, current):
    product = jnp.einsum(
        "trk,kc->trc", far_tiles[0, 0, offset], current, preferred_element_type=jnp.float32
    )
    return summed.at[row_blocks[0, 0, offset]].add(product)


def ring_body(sketch, far_tiles, row_blocks, owner_route, cluster_basis):
    offsets = far_tiles.shape[2]
    radius = (offsets - 1) // 2
    groups = lax.axis_size("group")
    tile_rows = far_tiles.shape[4]
    columns = sketch.shape[1]
    summed = jnp.zeros((groups, tile_rows, columns), jnp.float32)
    for offset in range(offsets):
        current = from_behind(sketch, "blk", radius - offset) if offset != radius else sketch
        summed = contribute(summed, far_tiles, row_blocks, offset, current)
    sampled = summed.astype(jnp.bfloat16)
    ordered = jnp.zeros_like(sampled).at[owner_route[0, 0]].set(sampled)
    received = lax.all_to_all(ordered, "group", split_axis=0, concat_axis=0, tiled=True)
    stacked = received.reshape(received.shape[0] * received.shape[1], received.shape[2])
    coefficients = lax.dot_general(
        cluster_basis[0, 0], stacked, TRANSPOSED, preferred_element_type=jnp.float32
    )
    return coefficients[None, None]


def body(sketch, far_tiles, row_blocks, owner_route, cluster_basis):
    small = cluster_basis.shape[3] < far_tiles.shape[4]
    paired = lax.axis_size("group") == 2 and lax.axis_size("blk") % 2 == 0
    if small and paired and far_tiles.shape[2:4] == (3, 1):
        return paired_body(sketch, far_tiles, row_blocks, owner_route, cluster_basis)
    return ring_body(sketch, far_tiles, row_blocks, owner_route, cluster_basis)


def solution(mesh):
    placed = (
        P("blk", None),
        P("blk", "group", None, None, None, None),
        P("blk", "group", None, None),
        P("blk", "group", None),
        P("blk", "group", None, None),
    )
    return jax.shard_map(
        body, mesh=mesh, in_specs=placed, out_specs=P("blk", "group", None, None), check_vma=False
    )
```

```python
import functools

import jax
import jax.numpy as jnp
from jax import lax
from jax.experimental import pallas as pl
from jax.experimental.pallas import tpu as pltpu
from jax.sharding import PartitionSpec as P

TRANSPOSED = (((0,), (0,)), ((), ()))


def from_behind(array, axis, by):
    devices = lax.axis_size(axis)
    return lax.ppermute(array, axis, [(i, (i + by) % devices) for i in range(devices)])


def swap(array, wanted, partner):
    sizes = lax.axis_size("blk"), lax.axis_size("group")
    places = [(b, g) for b in range(sizes[0]) for g in range(sizes[1]) if wanted(b)]
    flat = [(b * sizes[1] + g, partner(b, g)) for b, g in places]
    pairs = [(source, b % sizes[0] * sizes[1] + g) for source, (b, g) in flat]
    return lax.ppermute(array, ("blk", "group"), pairs)


def is_late(b):
    return (b + 1) // 2 % 2 == 1


def is_early(b):
    return not is_late(b)


def every(b):
    return True


def near_of(b, g):
    return b ^ 1, g


def far_of(b, g):
    return (b + 1 if b % 2 else b - 1), g


def across(b, g):
    return b, 1 - g


def on_chip(shape, dtype):
    return pltpu.VMEM(shape, dtype)


def call(kernel, out_shape, arrays, flops, scalars=(), hbm=(), scratch=(), to_hbm=False, alias=False):
    scalar, vector, main = (
        pl.BlockSpec(memory_space=m) for m in (pltpu.SMEM, pltpu.VMEM, pltpu.HBM)
    )
    placed = list(scalars)
    placed += [pltpu.with_memory_space_constraint(x, pltpu.VMEM) for x in arrays]
    placed += [pltpu.with_memory_space_constraint(x, pltpu.HBM) for x in hbm]
    target = main if to_hbm else vector
    return pl.pallas_call(
        kernel,
        out_shape=out_shape,
        in_specs=[scalar] * len(scalars) + [vector] * len(arrays) + [main] * len(hbm),
        out_specs=tuple(target for _ in out_shape) if isinstance(out_shape, tuple) else target,
        scratch_shapes=list(scratch),
        input_output_aliases={len(placed) - 1: 0} if alias else {},
        compiler_params=pltpu.CompilerParams(vmem_limit_bytes=16 << 20),
        cost_estimate=pl.CostEstimate(flops=flops, bytes_accessed=1 << 20, transcendentals=0),
    )(*placed)


def far_offset():
    return 2 * lax.rem(lax.axis_index("blk"), 2)


def copy_all(pairs, sems):
    copies = [pltpu.make_async_copy(*pair, sems.at[i]) for i, pair in enumerate(pairs)]
    for copy in copies:
        copy.start()
    for copy in copies:
        copy.wait()


def comes_late():
    return lax.rem((lax.axis_index("blk") + 1) // 2, 2) == 1


def stage_kernel(sketch, tiles, basis, lent, first, second, own, staged, kept, sems):
    half = lent.shape[0]
    group = lax.axis_index("group")
    ours, theirs = (
        basis.at[0, 0, pl.ds(pl.multiple_of(g * half, half), half)] for g in (group, 1 - group)
    )
    width = first.shape[1]
    pairs = [
        (theirs, lent),
        (sketch.at[:, pl.ds(0, width)], first),
        (sketch.at[:, pl.ds(width, second.shape[1])], second),
        (sketch, own),
        (tiles.at[0, 0, :, 0], staged),
        (ours, kept),
    ]
    copy_all(pairs, sems)


def local_kernel(row_blocks, owner_route, tiles, own, near, hit, miss, stays):
    far = far_offset()
    owner = owner_route[row_blocks[far]]
    own_hits = owner_route[row_blocks[1]] == owner
    near_hits = owner_route[row_blocks[2 - far]] == owner
    step = 256
    for start in range(0, own.shape[1], step):
        columns = pl.ds(start, step)
        first = jnp.dot(tiles[1], own[:, columns], preferred_element_type=jnp.float32)
        second = jnp.dot(tiles[2 - far], near[:, columns], preferred_element_type=jnp.float32)
        hit[:, columns] = jnp.where(own_hits, first, 0.0) + jnp.where(near_hits, second, 0.0)
        miss[:, columns] = (
            jnp.where(own_hits, 0.0, first) + jnp.where(near_hits, 0.0, second)
        ).astype(jnp.bfloat16)
    stays[...] = jnp.full(stays.shape, jnp.where(owner == lax.axis_index("group"), 1.0, 0.0))


def turn_kernel(kept, lent, miss, stays, hit_turned, missed):
    stay = stays[:, pl.ds(0, kept.shape[0])] > 0.0
    ours, theirs = kept[...].T, lent[...].T
    hit_turned[...] = jnp.where(stay, ours, theirs)
    missed[...] = jnp.dot(
        jnp.where(stay, theirs, ours), miss[...], preferred_element_type=jnp.float32
    )


def far_kernel(late, start, tiles, far, hit, hit_turned, missed, stays, kept, sent):
    @pl.when(comes_late() == late)
    def _():
        columns = pl.ds(start, far.shape[1])
        product = jnp.dot(tiles[far_offset()], far[...], preferred_element_type=jnp.float32)
        sampled = (hit[:, columns] + product).astype(jnp.bfloat16)
        made = jnp.dot(hit_turned[...], sampled, preferred_element_type=jnp.float32)
        stay = stays[:, columns] > 0.0
        other = missed[:, columns]
        sent[...] = jnp.where(stay, other, made).astype(jnp.bfloat16)
        kept[...] = jnp.where(stay, made, other)


def join_part(kept, received, start, out, total, sems):
    width = kept.shape[1]
    part = total.at[:, pl.ds(0, width)]
    part[...] = kept[...] + received[...].astype(jnp.float32)
    copy_all([(part, out.at[:, pl.ds(start, width)])], sems)


def join_first_kernel(kept, received, out, total, sems):
    @pl.when(comes_late())
    def _():
        join_part(kept, received, 0, out, total, sems)


def join_rest_kernel(kept, received, all_kept, all_received, begun, out, total, sems):
    late = comes_late()

    @pl.when(late)
    def _():
        join_part(kept, received, out.shape[1] - kept.shape[1], out, total, sems)

    @pl.when(jnp.logical_not(late))
    def _():
        join_part(all_kept, all_received, 0, out, total, sems)


def paired_body(sketch, far_tiles, row_blocks, owner_route, cluster_basis):
    panels, columns = sketch.shape
    offsets, rows = far_tiles.shape[2], far_tiles.shape[4]
    half, rank = cluster_basis.shape[2] // 2, cluster_basis.shape[3]
    width = 2 * columns // 3
    product = 2 * rows * panels * columns
    short, wide = sketch.dtype, jnp.float32
    copies = pltpu.SemaphoreType.DMA
    far_whole = swap(sketch, is_early, far_of)
    near = swap(sketch, every, near_of)
    lent, first, second, own, tiles, kept = call(
        stage_kernel,
        (
            on_chip((half, rank), short),
            on_chip((panels, width), short),
            on_chip((panels, columns - width), short),
            on_chip((panels, columns), short),
            on_chip((offsets, rows, panels), short),
            on_chip((half, rank), short),
        ),
        (),
        0,
        hbm=(sketch, far_tiles, cluster_basis),
        scratch=(copies((6,)),),
    )
    lent = swap(lent, every, across)
    hit, miss, stays = call(
        local_kernel,
        (
            on_chip((rows, columns), wide),
            on_chip((rows, columns), short),
            on_chip((1, columns), wide),
        ),
        (tiles, own, near),
        2 * product,
        scalars=(row_blocks.reshape(-1), owner_route.reshape(-1)),
    )
    hit_turned, missed = call(
        turn_kernel,
        (on_chip((rank, half), short), on_chip((rank, columns), wide)),
        (kept, lent, miss, stays),
        product // 2,
    )
    first, second, hit_turned = lax.optimization_barrier((first, second, hit_turned))
    far_first = swap(first, is_late, far_of)
    far_second = swap(second, is_late, far_of)

    def finish(far, late, start):
        part = far.shape[1]
        kept, sent = call(
            functools.partial(far_kernel, late, start),
            (on_chip((rank, part), wide), on_chip((rank, part), short)),
            (tiles, far, hit, hit_turned, missed, stays),
            2 * product * part // columns,
        )
        return kept, swap(sent, is_late if late else is_early, across)

    whole = finish(far_whole, False, 0)
    part = finish(far_first, True, 0)
    rest = finish(far_second, True, width)
    scratch = on_chip((rank, columns), wide), copies((1,))
    target = pltpu.HBM((rank, columns), wide)
    out = call(join_first_kernel, target, part, 1 << 16, scratch=scratch, to_hbm=True)
    out = call(
        join_rest_kernel,
        target,
        (*rest, *whole),
        1 << 16,
        hbm=(out,),
        scratch=scratch,
        to_hbm=True,
        alias=True,
    )
    return out[None, None]


def contribute(summed, far_tiles, row_blocks, offset, current):
    product = jnp.einsum(
        "trk,kc->trc", far_tiles[0, 0, offset], current, preferred_element_type=jnp.float32
    )
    return summed.at[row_blocks[0, 0, offset]].add(product)


def ring_body(sketch, far_tiles, row_blocks, owner_route, cluster_basis):
    offsets = far_tiles.shape[2]
    radius = (offsets - 1) // 2
    groups = lax.axis_size("group")
    tile_rows = far_tiles.shape[4]
    columns = sketch.shape[1]
    summed = jnp.zeros((groups, tile_rows, columns), jnp.float32)
    for offset in range(offsets):
        current = from_behind(sketch, "blk", radius - offset) if offset != radius else sketch
        summed = contribute(summed, far_tiles, row_blocks, offset, current)
    sampled = summed.astype(jnp.bfloat16)
    ordered = jnp.zeros_like(sampled).at[owner_route[0, 0]].set(sampled)
    received = lax.all_to_all(ordered, "group", split_axis=0, concat_axis=0, tiled=True)
    stacked = received.reshape(received.shape[0] * received.shape[1], received.shape[2])
    coefficients = lax.dot_general(
        cluster_basis[0, 0], stacked, TRANSPOSED, preferred_element_type=jnp.float32
    )
    return coefficients[None, None]


def body(sketch, far_tiles, row_blocks, owner_route, cluster_basis):
    small = cluster_basis.shape[3] < far_tiles.shape[4]
    paired = lax.axis_size("group") == 2 and lax.axis_size("blk") % 4 == 0
    if small and paired and far_tiles.shape[2:4] == (3, 1):
        return paired_body(sketch, far_tiles, row_blocks, owner_route, cluster_basis)
    return ring_body(sketch, far_tiles, row_blocks, owner_route, cluster_basis)


def solution(mesh):
    placed = (
        P("blk", None),
        P("blk", "group", None, None, None, None),
        P("blk", "group", None, None),
        P("blk", "group", None),
        P("blk", "group", None, None),
    )
    return jax.shard_map(
        body, mesh=mesh, in_specs=placed, out_specs=P("blk", "group", None, None), check_vma=False
    )
```

```python
import functools

import jax
import jax.numpy as jnp
from jax import lax
from jax.experimental import pallas as pl
from jax.experimental.pallas import tpu as pltpu
from jax.sharding import PartitionSpec as P

TRANSPOSED = (((0,), (0,)), ((), ()))


def from_behind(array, axis, by):
    devices = lax.axis_size(axis)
    return lax.ppermute(array, axis, [(i, (i + by) % devices) for i in range(devices)])


def swap_near(array):
    devices = lax.axis_size("blk")
    return lax.ppermute(array, "blk", [(i, i ^ 1) for i in range(devices)])


def swap_far(array):
    devices = lax.axis_size("blk")
    return lax.ppermute(
        array, "blk", [(i, (i + 1 if i % 2 else i - 1) % devices) for i in range(devices)]
    )


def on_chip(shape, dtype):
    return pltpu.VMEM(shape, dtype)


def call(kernel, out_shape, arrays, flops, scalars=(), hbm=(), scratch=(), to_hbm=False, alias=False):
    scalar, vector, main = (
        pl.BlockSpec(memory_space=m) for m in (pltpu.SMEM, pltpu.VMEM, pltpu.HBM)
    )
    placed = list(scalars)
    placed += [pltpu.with_memory_space_constraint(x, pltpu.VMEM) for x in arrays]
    placed += [pltpu.with_memory_space_constraint(x, pltpu.HBM) for x in hbm]
    target = main if to_hbm else vector
    return pl.pallas_call(
        kernel,
        out_shape=out_shape,
        in_specs=[scalar] * len(scalars) + [vector] * len(arrays) + [main] * len(hbm),
        out_specs=tuple(target for _ in out_shape) if isinstance(out_shape, tuple) else target,
        scratch_shapes=list(scratch),
        input_output_aliases={len(placed) - 1: 0} if alias else {},
        compiler_params=pltpu.CompilerParams(vmem_limit_bytes=16 << 20),
        cost_estimate=pl.CostEstimate(flops=flops, bytes_accessed=1 << 20, transcendentals=0),
    )(*placed)


def far_offset():
    return 2 * lax.rem(lax.axis_index("blk"), 2)


def copy_all(pairs, sems):
    copies = [pltpu.make_async_copy(*pair, sems.at[i]) for i, pair in enumerate(pairs)]
    for copy in copies:
        copy.start()
    for copy in copies:
        copy.wait()


def cut_kernel(sketch, first, sems):
    copy_all([(sketch.at[:, pl.ds(0, first.shape[1])], first)], sems)


def stage_kernel(sketch, tiles, basis, second, lent, own, staged, kept, sems):
    half = lent.shape[0]
    group = lax.axis_index("group")
    ours, theirs = (
        basis.at[0, 0, pl.ds(pl.multiple_of(g * half, half), half)] for g in (group, 1 - group)
    )
    width = second.shape[1]
    pairs = [
        (sketch.at[:, pl.ds(sketch.shape[1] - width, width)], second),
        (theirs, lent),
        (sketch, own),
        (tiles.at[0, 0, :, 0], staged),
        (ours, kept),
    ]
    copy_all(pairs, sems)


def local_kernel(row_blocks, owner_route, tiles, own, near, hit, miss, stays):
    far = far_offset()
    owner = owner_route[row_blocks[far]]
    own_hits = owner_route[row_blocks[1]] == owner
    near_hits = owner_route[row_blocks[2 - far]] == owner
    step = 256
    for start in range(0, own.shape[1], step):
        columns = pl.ds(start, step)
        first = jnp.dot(tiles[1], own[:, columns], preferred_element_type=jnp.float32)
        second = jnp.dot(tiles[2 - far], near[:, columns], preferred_element_type=jnp.float32)
        hit[:, columns] = jnp.where(own_hits, first, 0.0) + jnp.where(near_hits, second, 0.0)
        miss[:, columns] = (
            jnp.where(own_hits, 0.0, first) + jnp.where(near_hits, 0.0, second)
        ).astype(jnp.bfloat16)
    stays[...] = jnp.full(stays.shape, jnp.where(owner == lax.axis_index("group"), 1.0, 0.0))


def turn_kernel(kept, lent, miss, stays, hit_turned, missed):
    stay = stays[:, pl.ds(0, kept.shape[0])] > 0.0
    ours, theirs = kept[...].T, lent[...].T
    hit_turned[...] = jnp.where(stay, ours, theirs)
    missed[...] = jnp.dot(
        jnp.where(stay, theirs, ours), miss[...], preferred_element_type=jnp.float32
    )


def far_kernel(start, tiles, far, hit, hit_turned, missed, stays, kept, sent):
    columns = pl.ds(start, far.shape[1])
    product = jnp.dot(tiles[far_offset()], far[...], preferred_element_type=jnp.float32)
    sampled = (hit[:, columns] + product).astype(jnp.bfloat16)
    made = jnp.dot(hit_turned[...], sampled, preferred_element_type=jnp.float32)
    stay = stays[:, columns] > 0.0
    other = missed[:, columns]
    sent[...] = jnp.where(stay, other, made).astype(jnp.bfloat16)
    kept[...] = jnp.where(stay, made, other)


def join_kernel(start, kept, received, *rest):
    out, total, sems = rest[-3:]
    total[...] = kept[...] + received[...].astype(jnp.float32)
    copy_all([(total, out.at[:, pl.ds(start, total.shape[1])])], sems)


def paired_body(sketch, far_tiles, row_blocks, owner_route, cluster_basis):
    panels, columns = sketch.shape
    offsets, rows = far_tiles.shape[2], far_tiles.shape[4]
    half, rank = cluster_basis.shape[2] // 2, cluster_basis.shape[3]
    early = 2 * columns // 3
    product = 2 * rows * panels * columns
    short, wide = sketch.dtype, jnp.float32
    copies = pltpu.SemaphoreType.DMA
    first = call(
        cut_kernel, on_chip((panels, early), short), (), 0, hbm=(sketch,), scratch=(copies((1,)),)
    )
    far_first = swap_far(first)
    second, lent, own, tiles, kept = call(
        stage_kernel,
        (
            on_chip((panels, columns - early), short),
            on_chip((half, rank), short),
            on_chip((panels, columns), short),
            on_chip((offsets, rows, panels), short),
            on_chip((half, rank), short),
        ),
        (),
        0,
        hbm=(sketch, far_tiles, cluster_basis),
        scratch=(copies((5,)),),
    )
    far_second = swap_far(second)
    lent = from_behind(lent, "group", 1)
    near = swap_near(own)
    hit, miss, stays = call(
        local_kernel,
        (
            on_chip((rows, columns), wide),
            on_chip((rows, columns), short),
            on_chip((1, columns), wide),
        ),
        (tiles, own, near),
        2 * product,
        scalars=(row_blocks.reshape(-1), owner_route.reshape(-1)),
    )
    hit_turned, missed = call(
        turn_kernel,
        (on_chip((rank, half), short), on_chip((rank, columns), wide)),
        (kept, lent, miss, stays),
        product // 2,
    )
    out = None
    for start, far in ((0, far_first), (early, far_second)):
        width = far.shape[1]
        kept, sent = call(
            functools.partial(far_kernel, start),
            (on_chip((rank, width), wide), on_chip((rank, width), short)),
            (tiles, far, hit, hit_turned, missed, stays),
            2 * product * width // columns,
        )
        out = call(
            functools.partial(join_kernel, start),
            pltpu.HBM((rank, columns), wide),
            (kept, from_behind(sent, "group", 1)),
            1 << 16,
            hbm=() if out is None else (out,),
            scratch=(on_chip((rank, width), wide), copies((1,))),
            to_hbm=True,
            alias=out is not None,
        )
    return out[None, None]


def contribute(summed, far_tiles, row_blocks, offset, current):
    product = jnp.einsum(
        "trk,kc->trc", far_tiles[0, 0, offset], current, preferred_element_type=jnp.float32
    )
    return summed.at[row_blocks[0, 0, offset]].add(product)


def ring_body(sketch, far_tiles, row_blocks, owner_route, cluster_basis):
    offsets = far_tiles.shape[2]
    radius = (offsets - 1) // 2
    groups = lax.axis_size("group")
    tile_rows = far_tiles.shape[4]
    columns = sketch.shape[1]
    summed = jnp.zeros((groups, tile_rows, columns), jnp.float32)
    for offset in range(offsets):
        current = from_behind(sketch, "blk", radius - offset) if offset != radius else sketch
        summed = contribute(summed, far_tiles, row_blocks, offset, current)
    sampled = summed.astype(jnp.bfloat16)
    ordered = jnp.zeros_like(sampled).at[owner_route[0, 0]].set(sampled)
    received = lax.all_to_all(ordered, "group", split_axis=0, concat_axis=0, tiled=True)
    stacked = received.reshape(received.shape[0] * received.shape[1], received.shape[2])
    coefficients = lax.dot_general(
        cluster_basis[0, 0], stacked, TRANSPOSED, preferred_element_type=jnp.float32
    )
    return coefficients[None, None]


def body(sketch, far_tiles, row_blocks, owner_route, cluster_basis):
    small = cluster_basis.shape[3] < far_tiles.shape[4]
    paired = lax.axis_size("group") == 2 and lax.axis_size("blk") % 2 == 0
    if small and paired and far_tiles.shape[2:4] == (3, 1):
        return paired_body(sketch, far_tiles, row_blocks, owner_route, cluster_basis)
    return ring_body(sketch, far_tiles, row_blocks, owner_route, cluster_basis)


def solution(mesh):
    placed = (
        P("blk", None),
        P("blk", "group", None, None, None, None),
        P("blk", "group", None, None),
        P("blk", "group", None),
        P("blk", "group", None, None),
    )
    return jax.shard_map(
        body, mesh=mesh, in_specs=placed, out_specs=P("blk", "group", None, None), check_vma=False
    )
```

```python
import functools

import jax
import jax.numpy as jnp
from jax import lax
from jax.experimental import pallas as pl
from jax.experimental.pallas import tpu as pltpu
from jax.sharding import PartitionSpec as P

SHARES = (3, 2, 1)
TRANSPOSED = (((0,), (0,)), ((), ()))


def from_behind(array, axis, by):
    devices = lax.axis_size(axis)
    return lax.ppermute(array, axis, [(i, (i + by) % devices) for i in range(devices)])


def swap_near(array):
    devices = lax.axis_size("blk")
    return lax.ppermute(array, "blk", [(i, i ^ 1) for i in range(devices)])


def swap_far(array):
    devices = lax.axis_size("blk")
    return lax.ppermute(
        array, "blk", [(i, (i + 1 if i % 2 else i - 1) % devices) for i in range(devices)]
    )


def on_chip(shape, dtype):
    return pltpu.VMEM(shape, dtype)


def call(kernel, out_shape, arrays, flops, scalars=(), hbm=(), scratch=(), to_hbm=False, alias=False):
    scalar, vector, main = (
        pl.BlockSpec(memory_space=m) for m in (pltpu.SMEM, pltpu.VMEM, pltpu.HBM)
    )
    placed = list(scalars)
    placed += [pltpu.with_memory_space_constraint(x, pltpu.VMEM) for x in arrays]
    placed += [pltpu.with_memory_space_constraint(x, pltpu.HBM) for x in hbm]
    target = main if to_hbm else vector
    return pl.pallas_call(
        kernel,
        out_shape=out_shape,
        in_specs=[scalar] * len(scalars) + [vector] * len(arrays) + [main] * len(hbm),
        out_specs=tuple(target for _ in out_shape) if isinstance(out_shape, tuple) else target,
        scratch_shapes=list(scratch),
        input_output_aliases={len(placed) - 1: 0} if alias else {},
        compiler_params=pltpu.CompilerParams(vmem_limit_bytes=16 << 20),
        cost_estimate=pl.CostEstimate(flops=flops, bytes_accessed=1 << 20, transcendentals=0),
    )(*placed)


def far_offset():
    return 2 * lax.rem(lax.axis_index("blk"), 2)


def copy_all(pairs, sems):
    copies = [pltpu.make_async_copy(*pair, sems.at[i]) for i, pair in enumerate(pairs)]
    for copy in copies:
        copy.start()
    for copy in copies:
        copy.wait()


def half_rows(basis, group, half):
    return basis.at[0, 0, pl.ds(pl.multiple_of(group * half, half), half)]


def cut_kernel(sketch, basis, first, lent, sems):
    theirs = half_rows(basis, 1 - lax.axis_index("group"), lent.shape[0])
    copy_all([(sketch.at[:, pl.ds(0, first.shape[1])], first), (theirs, lent)], sems)


def stage_kernel(begun, sketch, tiles, basis, *outs):
    del begun
    *parts, own, staged, kept, sems = outs
    ours = half_rows(basis, lax.axis_index("group"), kept.shape[0])
    pairs = []
    end = sketch.shape[1]
    for part in reversed(parts):
        end -= part.shape[1]
        pairs.insert(0, (sketch.at[:, pl.ds(end, part.shape[1])], part))
    copy_all([*pairs, (sketch, own), (tiles.at[0, 0, :, 0], staged), (ours, kept)], sems)


def local_kernel(row_blocks, owner_route, tiles, own, near, hit, miss, stays):
    far = far_offset()
    owner = owner_route[row_blocks[far]]
    own_hits = owner_route[row_blocks[1]] == owner
    near_hits = owner_route[row_blocks[2 - far]] == owner
    step = 256
    for start in range(0, own.shape[1], step):
        columns = pl.ds(start, step)
        first = jnp.dot(tiles[1], own[:, columns], preferred_element_type=jnp.float32)
        second = jnp.dot(tiles[2 - far], near[:, columns], preferred_element_type=jnp.float32)
        hit[:, columns] = jnp.where(own_hits, first, 0.0) + jnp.where(near_hits, second, 0.0)
        miss[:, columns] = (
            jnp.where(own_hits, 0.0, first) + jnp.where(near_hits, 0.0, second)
        ).astype(jnp.bfloat16)
    stays[...] = jnp.full(stays.shape, jnp.where(owner == lax.axis_index("group"), 1.0, 0.0))


def turn_kernel(kept, lent, miss, stays, hit_turned, missed):
    stay = stays[:, pl.ds(0, kept.shape[0])] > 0.0
    ours, theirs = kept[...].T, lent[...].T
    hit_turned[...] = jnp.where(stay, ours, theirs)
    missed[...] = jnp.dot(
        jnp.where(stay, theirs, ours), miss[...], preferred_element_type=jnp.float32
    )


def far_kernel(start, tiles, far, hit, hit_turned, missed, stays, kept, sent):
    columns = pl.ds(start, far.shape[1])
    product = jnp.dot(tiles[far_offset()], far[...], preferred_element_type=jnp.float32)
    sampled = (hit[:, columns] + product).astype(jnp.bfloat16)
    made = jnp.dot(hit_turned[...], sampled, preferred_element_type=jnp.float32)
    stay = stays[:, columns] > 0.0
    other = missed[:, columns]
    sent[...] = jnp.where(stay, other, made).astype(jnp.bfloat16)
    kept[...] = jnp.where(stay, made, other)


def join_kernel(start, kept, received, *rest):
    out, total, sems = rest[-3:]
    total[...] = kept[...] + received[...].astype(jnp.float32)
    copy_all([(total, out.at[:, pl.ds(start, total.shape[1])])], sems)


def paired_body(sketch, far_tiles, row_blocks, owner_route, cluster_basis):
    panels, columns = sketch.shape
    offsets, rows = far_tiles.shape[2], far_tiles.shape[4]
    half, rank = cluster_basis.shape[2] // 2, cluster_basis.shape[3]
    widths = [columns * share // sum(SHARES) for share in SHARES]
    starts = [sum(widths[:i]) for i in range(len(widths))]
    product = 2 * rows * panels * columns
    short, wide = sketch.dtype, jnp.float32
    copies = pltpu.SemaphoreType.DMA
    first, lent = call(
        cut_kernel,
        (on_chip((panels, widths[0]), short), on_chip((half, rank), short)),
        (),
        0,
        hbm=(sketch, cluster_basis),
        scratch=(copies((2,)),),
    )
    *later, own, tiles, kept = call(
        stage_kernel,
        (
            *(on_chip((panels, width), short) for width in widths[1:]),
            on_chip((panels, columns), short),
            on_chip((offsets, rows, panels), short),
            on_chip((half, rank), short),
        ),
        (first,),
        0,
        hbm=(sketch, far_tiles, cluster_basis),
        scratch=(copies((len(widths) + 2,)),),
    )
    lent = from_behind(lent, "group", 1)
    fars = [swap_far(part) for part in (first, *later)]
    near = swap_near(own)
    hit, miss, stays = call(
        local_kernel,
        (
            on_chip((rows, columns), wide),
            on_chip((rows, columns), short),
            on_chip((1, columns), wide),
        ),
        (tiles, own, near),
        2 * product,
        scalars=(row_blocks.reshape(-1), owner_route.reshape(-1)),
    )
    hit_turned, missed = call(
        turn_kernel,
        (on_chip((rank, half), short), on_chip((rank, columns), wide)),
        (kept, lent, miss, stays),
        product // 2,
    )
    out = None
    for start, far in zip(starts, fars):
        width = far.shape[1]
        kept, sent = call(
            functools.partial(far_kernel, start),
            (on_chip((rank, width), wide), on_chip((rank, width), short)),
            (tiles, far, hit, hit_turned, missed, stays),
            2 * product * width // columns,
        )
        out = call(
            functools.partial(join_kernel, start),
            pltpu.HBM((rank, columns), wide),
            (kept, from_behind(sent, "group", 1)),
            1 << 16,
            hbm=() if out is None else (out,),
            scratch=(on_chip((rank, width), wide), copies((1,))),
            to_hbm=True,
            alias=out is not None,
        )
    return out[None, None]


def contribute(summed, far_tiles, row_blocks, offset, current):
    product = jnp.einsum(
        "trk,kc->trc", far_tiles[0, 0, offset], current, preferred_element_type=jnp.float32
    )
    return summed.at[row_blocks[0, 0, offset]].add(product)


def ring_body(sketch, far_tiles, row_blocks, owner_route, cluster_basis):
    offsets = far_tiles.shape[2]
    radius = (offsets - 1) // 2
    groups = lax.axis_size("group")
    tile_rows = far_tiles.shape[4]
    columns = sketch.shape[1]
    summed = jnp.zeros((groups, tile_rows, columns), jnp.float32)
    for offset in range(offsets):
        current = from_behind(sketch, "blk", radius - offset) if offset != radius else sketch
        summed = contribute(summed, far_tiles, row_blocks, offset, current)
    sampled = summed.astype(jnp.bfloat16)
    ordered = jnp.zeros_like(sampled).at[owner_route[0, 0]].set(sampled)
    received = lax.all_to_all(ordered, "group", split_axis=0, concat_axis=0, tiled=True)
    stacked = received.reshape(received.shape[0] * received.shape[1], received.shape[2])
    coefficients = lax.dot_general(
        cluster_basis[0, 0], stacked, TRANSPOSED, preferred_element_type=jnp.float32
    )
    return coefficients[None, None]


def body(sketch, far_tiles, row_blocks, owner_route, cluster_basis):
    small = cluster_basis.shape[3] < far_tiles.shape[4]
    paired = lax.axis_size("group") == 2 and lax.axis_size("blk") % 2 == 0
    if small and paired and far_tiles.shape[2:4] == (3, 1):
        return paired_body(sketch, far_tiles, row_blocks, owner_route, cluster_basis)
    return ring_body(sketch, far_tiles, row_blocks, owner_route, cluster_basis)


def solution(mesh):
    placed = (
        P("blk", None),
        P("blk", "group", None, None, None, None),
        P("blk", "group", None, None),
        P("blk", "group", None),
        P("blk", "group", None, None),
    )
    return jax.shard_map(
        body, mesh=mesh, in_specs=placed, out_specs=P("blk", "group", None, None), check_vma=False
    )
```

```python
import functools

import jax
import jax.numpy as jnp
from jax import lax
from jax.experimental import pallas as pl
from jax.experimental.pallas import tpu as pltpu
from jax.sharding import PartitionSpec as P

SHARES = (3, 2, 1)
TRANSPOSED = (((0,), (0,)), ((), ()))


def from_behind(array, axis, by):
    devices = lax.axis_size(axis)
    return lax.ppermute(array, axis, [(i, (i + by) % devices) for i in range(devices)])


def swap_near(array):
    devices = lax.axis_size("blk")
    return lax.ppermute(array, "blk", [(i, i ^ 1) for i in range(devices)])


def swap_far(array):
    devices = lax.axis_size("blk")
    return lax.ppermute(
        array, "blk", [(i, (i + 1 if i % 2 else i - 1) % devices) for i in range(devices)]
    )


def on_chip(shape, dtype):
    return pltpu.VMEM(shape, dtype)


def call(kernel, out_shape, arrays, flops, scalars=(), hbm=(), scratch=(), to_hbm=False, alias=False):
    scalar, vector, main = (
        pl.BlockSpec(memory_space=m) for m in (pltpu.SMEM, pltpu.VMEM, pltpu.HBM)
    )
    placed = list(scalars)
    placed += [pltpu.with_memory_space_constraint(x, pltpu.VMEM) for x in arrays]
    placed += [pltpu.with_memory_space_constraint(x, pltpu.HBM) for x in hbm]
    target = main if to_hbm else vector
    return pl.pallas_call(
        kernel,
        out_shape=out_shape,
        in_specs=[scalar] * len(scalars) + [vector] * len(arrays) + [main] * len(hbm),
        out_specs=tuple(target for _ in out_shape) if isinstance(out_shape, tuple) else target,
        scratch_shapes=list(scratch),
        input_output_aliases={len(placed) - 1: 0} if alias else {},
        compiler_params=pltpu.CompilerParams(vmem_limit_bytes=16 << 20),
        cost_estimate=pl.CostEstimate(flops=flops, bytes_accessed=1 << 20, transcendentals=0),
    )(*placed)


def far_offset():
    return 2 * lax.rem(lax.axis_index("blk"), 2)


def copy_all(pairs, sems):
    copies = [pltpu.make_async_copy(*pair, sems.at[i]) for i, pair in enumerate(pairs)]
    for copy in copies:
        copy.start()
    for copy in copies:
        copy.wait()


def half_rows(basis, group, half):
    return basis.at[0, 0, pl.ds(pl.multiple_of(group * half, half), half)]


def cut_kernel(sketch, basis, first, lent, sems):
    theirs = half_rows(basis, 1 - lax.axis_index("group"), lent.shape[0])
    copy_all([(sketch.at[:, pl.ds(0, first.shape[1])], first), (theirs, lent)], sems)


def stage_kernel(begun, sketch, tiles, basis, *outs):
    del begun
    *parts, own, staged, kept, sems = outs
    ours = half_rows(basis, lax.axis_index("group"), kept.shape[0])
    pairs = []
    end = sketch.shape[1]
    for part in reversed(parts):
        end -= part.shape[1]
        pairs.insert(0, (sketch.at[:, pl.ds(end, part.shape[1])], part))
    copy_all([*pairs, (sketch, own), (tiles.at[0, 0, :, 0], staged), (ours, kept)], sems)


def local_kernel(row_blocks, owner_route, tiles, own, near, hit, miss, stays):
    far = far_offset()
    owner = owner_route[row_blocks[far]]
    own_hits = owner_route[row_blocks[1]] == owner
    near_hits = owner_route[row_blocks[2 - far]] == owner
    step = 256
    for start in range(0, own.shape[1], step):
        columns = pl.ds(start, step)
        first = jnp.dot(tiles[1], own[:, columns], preferred_element_type=jnp.float32)
        second = jnp.dot(tiles[2 - far], near[:, columns], preferred_element_type=jnp.float32)
        hit[:, columns] = jnp.where(own_hits, first, 0.0) + jnp.where(near_hits, second, 0.0)
        miss[:, columns] = (
            jnp.where(own_hits, 0.0, first) + jnp.where(near_hits, 0.0, second)
        ).astype(jnp.bfloat16)
    stays[...] = jnp.full(stays.shape, jnp.where(owner == lax.axis_index("group"), 1.0, 0.0))


def turn_kernel(kept, lent, miss, stays, hit_turned, missed):
    stay = stays[:, pl.ds(0, kept.shape[0])] > 0.0
    ours, theirs = kept[...].T, lent[...].T
    hit_turned[...] = jnp.where(stay, ours, theirs)
    missed[...] = jnp.dot(
        jnp.where(stay, theirs, ours), miss[...], preferred_element_type=jnp.float32
    )


def far_kernel(start, tiles, far, hit, hit_turned, missed, stays, kept, sent):
    columns = pl.ds(start, far.shape[1])
    product = jnp.dot(tiles[far_offset()], far[...], preferred_element_type=jnp.float32)
    sampled = (hit[:, columns] + product).astype(jnp.bfloat16)
    made = jnp.dot(hit_turned[...], sampled, preferred_element_type=jnp.float32)
    stay = stays[:, columns] > 0.0
    other = missed[:, columns]
    sent[...] = jnp.where(stay, other, made).astype(jnp.bfloat16)
    kept[...] = jnp.where(stay, made, other)


def join_kernel(start, kept, received, *rest):
    out, total, sems = rest[-3:]
    total[...] = kept[...] + received[...].astype(jnp.float32)
    copy_all([(total, out.at[:, pl.ds(start, total.shape[1])])], sems)


def paired_body(sketch, far_tiles, row_blocks, owner_route, cluster_basis):
    panels, columns = sketch.shape
    offsets, rows = far_tiles.shape[2], far_tiles.shape[4]
    half, rank = cluster_basis.shape[2] // 2, cluster_basis.shape[3]
    widths = [columns * share // sum(SHARES) for share in SHARES]
    starts = [sum(widths[:i]) for i in range(len(widths))]
    product = 2 * rows * panels * columns
    short, wide = sketch.dtype, jnp.float32
    copies = pltpu.SemaphoreType.DMA
    first, lent = call(
        cut_kernel,
        (on_chip((panels, widths[0]), short), on_chip((half, rank), short)),
        (),
        0,
        hbm=(sketch, cluster_basis),
        scratch=(copies((2,)),),
    )
    *later, own, tiles, kept = call(
        stage_kernel,
        (
            *(on_chip((panels, width), short) for width in widths[1:]),
            on_chip((panels, columns), short),
            on_chip((offsets, rows, panels), short),
            on_chip((half, rank), short),
        ),
        (first,),
        0,
        hbm=(sketch, far_tiles, cluster_basis),
        scratch=(copies((len(widths) + 2,)),),
    )
    lent = from_behind(lent, "group", 1)
    fars = [swap_far(part) for part in (first, *later)]
    near = swap_near(sketch)
    hit, miss, stays = call(
        local_kernel,
        (
            on_chip((rows, columns), wide),
            on_chip((rows, columns), short),
            on_chip((1, columns), wide),
        ),
        (tiles, own, near),
        2 * product,
        scalars=(row_blocks.reshape(-1), owner_route.reshape(-1)),
    )
    hit_turned, missed = call(
        turn_kernel,
        (on_chip((rank, half), short), on_chip((rank, columns), wide)),
        (kept, lent, miss, stays),
        product // 2,
    )
    out = None
    for start, far in zip(starts, fars):
        width = far.shape[1]
        kept, sent = call(
            functools.partial(far_kernel, start),
            (on_chip((rank, width), wide), on_chip((rank, width), short)),
            (tiles, far, hit, hit_turned, missed, stays),
            2 * product * width // columns,
        )
        out = call(
            functools.partial(join_kernel, start),
            pltpu.HBM((rank, columns), wide),
            (kept, from_behind(sent, "group", 1)),
            1 << 16,
            hbm=() if out is None else (out,),
            scratch=(on_chip((rank, width), wide), copies((1,))),
            to_hbm=True,
            alias=out is not None,
        )
    return out[None, None]


def contribute(summed, far_tiles, row_blocks, offset, current):
    product = jnp.einsum(
        "trk,kc->trc", far_tiles[0, 0, offset], current, preferred_element_type=jnp.float32
    )
    return summed.at[row_blocks[0, 0, offset]].add(product)


def ring_body(sketch, far_tiles, row_blocks, owner_route, cluster_basis):
    offsets = far_tiles.shape[2]
    radius = (offsets - 1) // 2
    groups = lax.axis_size("group")
    tile_rows = far_tiles.shape[4]
    columns = sketch.shape[1]
    summed = jnp.zeros((groups, tile_rows, columns), jnp.float32)
    for offset in range(offsets):
        current = from_behind(sketch, "blk", radius - offset) if offset != radius else sketch
        summed = contribute(summed, far_tiles, row_blocks, offset, current)
    sampled = summed.astype(jnp.bfloat16)
    ordered = jnp.zeros_like(sampled).at[owner_route[0, 0]].set(sampled)
    received = lax.all_to_all(ordered, "group", split_axis=0, concat_axis=0, tiled=True)
    stacked = received.reshape(received.shape[0] * received.shape[1], received.shape[2])
    coefficients = lax.dot_general(
        cluster_basis[0, 0], stacked, TRANSPOSED, preferred_element_type=jnp.float32
    )
    return coefficients[None, None]


def body(sketch, far_tiles, row_blocks, owner_route, cluster_basis):
    small = cluster_basis.shape[3] < far_tiles.shape[4]
    paired = lax.axis_size("group") == 2 and lax.axis_size("blk") % 2 == 0
    if small and paired and far_tiles.shape[2:4] == (3, 1):
        return paired_body(sketch, far_tiles, row_blocks, owner_route, cluster_basis)
    return ring_body(sketch, far_tiles, row_blocks, owner_route, cluster_basis)


def solution(mesh):
    placed = (
        P("blk", None),
        P("blk", "group", None, None, None, None),
        P("blk", "group", None, None),
        P("blk", "group", None),
        P("blk", "group", None, None),
    )
    return jax.shard_map(
        body, mesh=mesh, in_specs=placed, out_specs=P("blk", "group", None, None), check_vma=False
    )
```

```python
import functools

import jax
import jax.numpy as jnp
from jax import lax
from jax.experimental import pallas as pl
from jax.experimental.pallas import tpu as pltpu
from jax.sharding import PartitionSpec as P

SHARES = (3, 2, 1)
TRANSPOSED = (((0,), (0,)), ((), ()))


def from_behind(array, axis, by):
    devices = lax.axis_size(axis)
    return lax.ppermute(array, axis, [(i, (i + by) % devices) for i in range(devices)])


def swap_near(array):
    devices = lax.axis_size("blk")
    return lax.ppermute(array, "blk", [(i, i ^ 1) for i in range(devices)])


def swap_far(array):
    devices = lax.axis_size("blk")
    return lax.ppermute(
        array, "blk", [(i, (i + 1 if i % 2 else i - 1) % devices) for i in range(devices)]
    )


def on_chip(shape, dtype):
    return pltpu.VMEM(shape, dtype)


def call(kernel, out_shape, arrays, flops, scalars=(), hbm=(), scratch=(), to_hbm=False, alias=False):
    scalar, vector, main = (
        pl.BlockSpec(memory_space=m) for m in (pltpu.SMEM, pltpu.VMEM, pltpu.HBM)
    )
    placed = list(scalars)
    placed += [pltpu.with_memory_space_constraint(x, pltpu.VMEM) for x in arrays]
    placed += [pltpu.with_memory_space_constraint(x, pltpu.HBM) for x in hbm]
    target = main if to_hbm else vector
    return pl.pallas_call(
        kernel,
        out_shape=out_shape,
        in_specs=[scalar] * len(scalars) + [vector] * len(arrays) + [main] * len(hbm),
        out_specs=tuple(target for _ in out_shape) if isinstance(out_shape, tuple) else target,
        scratch_shapes=list(scratch),
        input_output_aliases={len(placed) - 1: 0} if alias else {},
        compiler_params=pltpu.CompilerParams(vmem_limit_bytes=16 << 20),
        cost_estimate=pl.CostEstimate(flops=flops, bytes_accessed=1 << 20, transcendentals=0),
    )(*placed)


def far_offset():
    return 2 * lax.rem(lax.axis_index("blk"), 2)


def copy_all(pairs, sems):
    copies = [pltpu.make_async_copy(*pair, sems.at[i]) for i, pair in enumerate(pairs)]
    for copy in copies:
        copy.start()
    for copy in copies:
        copy.wait()


def half_rows(basis, group, half):
    return basis.at[0, 0, pl.ds(pl.multiple_of(group * half, half), half)]


def cut_kernel(sketch, basis, lent, *rest):
    *parts, sems = rest
    theirs = half_rows(basis, 1 - lax.axis_index("group"), lent.shape[0])
    pairs = []
    start = 0
    for part in parts:
        pairs.append((sketch.at[:, pl.ds(start, part.shape[1])], part))
        start += part.shape[1]
    copy_all([*pairs, (theirs, lent)], sems)


def stage_kernel(begun, sketch, tiles, basis, own, staged, kept, sems):
    del begun
    ours = half_rows(basis, lax.axis_index("group"), kept.shape[0])
    copy_all([(sketch, own), (tiles.at[0, 0, :, 0], staged), (ours, kept)], sems)


def local_kernel(row_blocks, owner_route, tiles, own, near, hit, miss, stays, last):
    far = far_offset()
    owner = owner_route[row_blocks[far]]
    own_hits = owner_route[row_blocks[1]] == owner
    near_hits = owner_route[row_blocks[2 - far]] == owner
    last[...] = own[:, pl.ds(own.shape[1] - last.shape[1], last.shape[1])]
    step = 256
    for start in range(0, own.shape[1], step):
        columns = pl.ds(start, step)
        first = jnp.dot(tiles[1], own[:, columns], preferred_element_type=jnp.float32)
        second = jnp.dot(tiles[2 - far], near[:, columns], preferred_element_type=jnp.float32)
        hit[:, columns] = jnp.where(own_hits, first, 0.0) + jnp.where(near_hits, second, 0.0)
        miss[:, columns] = (
            jnp.where(own_hits, 0.0, first) + jnp.where(near_hits, 0.0, second)
        ).astype(jnp.bfloat16)
    stays[...] = jnp.full(stays.shape, jnp.where(owner == lax.axis_index("group"), 1.0, 0.0))


def turn_kernel(kept, lent, miss, stays, hit_turned, missed):
    stay = stays[:, pl.ds(0, kept.shape[0])] > 0.0
    ours, theirs = kept[...].T, lent[...].T
    hit_turned[...] = jnp.where(stay, ours, theirs)
    missed[...] = jnp.dot(
        jnp.where(stay, theirs, ours), miss[...], preferred_element_type=jnp.float32
    )


def far_kernel(start, tiles, far, hit, hit_turned, missed, stays, kept, sent):
    columns = pl.ds(start, far.shape[1])
    product = jnp.dot(tiles[far_offset()], far[...], preferred_element_type=jnp.float32)
    sampled = (hit[:, columns] + product).astype(jnp.bfloat16)
    made = jnp.dot(hit_turned[...], sampled, preferred_element_type=jnp.float32)
    stay = stays[:, columns] > 0.0
    other = missed[:, columns]
    sent[...] = jnp.where(stay, other, made).astype(jnp.bfloat16)
    kept[...] = jnp.where(stay, made, other)


def join_kernel(start, kept, received, *rest):
    out, total, sems = rest[-3:]
    total[...] = kept[...] + received[...].astype(jnp.float32)
    copy_all([(total, out.at[:, pl.ds(start, total.shape[1])])], sems)


def paired_body(sketch, far_tiles, row_blocks, owner_route, cluster_basis):
    panels, columns = sketch.shape
    offsets, rows = far_tiles.shape[2], far_tiles.shape[4]
    half, rank = cluster_basis.shape[2] // 2, cluster_basis.shape[3]
    widths = [columns * share // sum(SHARES) for share in SHARES]
    starts = [sum(widths[:i]) for i in range(len(widths))]
    product = 2 * rows * panels * columns
    short, wide = sketch.dtype, jnp.float32
    copies = pltpu.SemaphoreType.DMA
    lent, *parts = call(
        cut_kernel,
        (
            on_chip((half, rank), short),
            *(on_chip((panels, width), short) for width in widths[:-1]),
        ),
        (),
        0,
        hbm=(sketch, cluster_basis),
        scratch=(copies((len(widths),)),),
    )
    own, tiles, kept = call(
        stage_kernel,
        (
            on_chip((panels, columns), short),
            on_chip((offsets, rows, panels), short),
            on_chip((half, rank), short),
        ),
        (parts[0],),
        0,
        hbm=(sketch, far_tiles, cluster_basis),
        scratch=(copies((3,)),),
    )
    lent = from_behind(lent, "group", 1)
    fars = [swap_far(part) for part in parts]
    near = swap_near(sketch)
    hit, miss, stays, last = call(
        local_kernel,
        (
            on_chip((rows, columns), wide),
            on_chip((rows, columns), short),
            on_chip((1, columns), wide),
            on_chip((panels, widths[-1]), short),
        ),
        (tiles, own, near),
        2 * product,
        scalars=(row_blocks.reshape(-1), owner_route.reshape(-1)),
    )
    fars.append(swap_far(last))
    hit_turned, missed = call(
        turn_kernel,
        (on_chip((rank, half), short), on_chip((rank, columns), wide)),
        (kept, lent, miss, stays),
        product // 2,
    )
    out = None
    for start, far in zip(starts, fars):
        width = far.shape[1]
        kept, sent = call(
            functools.partial(far_kernel, start),
            (on_chip((rank, width), wide), on_chip((rank, width), short)),
            (tiles, far, hit, hit_turned, missed, stays),
            2 * product * width // columns,
        )
        out = call(
            functools.partial(join_kernel, start),
            pltpu.HBM((rank, columns), wide),
            (kept, from_behind(sent, "group", 1)),
            1 << 16,
            hbm=() if out is None else (out,),
            scratch=(on_chip((rank, width), wide), copies((1,))),
            to_hbm=True,
            alias=out is not None,
        )
    return out[None, None]


def contribute(summed, far_tiles, row_blocks, offset, current):
    product = jnp.einsum(
        "trk,kc->trc", far_tiles[0, 0, offset], current, preferred_element_type=jnp.float32
    )
    return summed.at[row_blocks[0, 0, offset]].add(product)


def ring_body(sketch, far_tiles, row_blocks, owner_route, cluster_basis):
    offsets = far_tiles.shape[2]
    radius = (offsets - 1) // 2
    groups = lax.axis_size("group")
    tile_rows = far_tiles.shape[4]
    columns = sketch.shape[1]
    summed = jnp.zeros((groups, tile_rows, columns), jnp.float32)
    for offset in range(offsets):
        current = from_behind(sketch, "blk", radius - offset) if offset != radius else sketch
        summed = contribute(summed, far_tiles, row_blocks, offset, current)
    sampled = summed.astype(jnp.bfloat16)
    ordered = jnp.zeros_like(sampled).at[owner_route[0, 0]].set(sampled)
    received = lax.all_to_all(ordered, "group", split_axis=0, concat_axis=0, tiled=True)
    stacked = received.reshape(received.shape[0] * received.shape[1], received.shape[2])
    coefficients = lax.dot_general(
        cluster_basis[0, 0], stacked, TRANSPOSED, preferred_element_type=jnp.float32
    )
    return coefficients[None, None]


def body(sketch, far_tiles, row_blocks, owner_route, cluster_basis):
    small = cluster_basis.shape[3] < far_tiles.shape[4]
    paired = lax.axis_size("group") == 2 and lax.axis_size("blk") % 2 == 0
    if small and paired and far_tiles.shape[2:4] == (3, 1):
        return paired_body(sketch, far_tiles, row_blocks, owner_route, cluster_basis)
    return ring_body(sketch, far_tiles, row_blocks, owner_route, cluster_basis)


def solution(mesh):
    placed = (
        P("blk", None),
        P("blk", "group", None, None, None, None),
        P("blk", "group", None, None),
        P("blk", "group", None),
        P("blk", "group", None, None),
    )
    return jax.shard_map(
        body, mesh=mesh, in_specs=placed, out_specs=P("blk", "group", None, None), check_vma=False
    )
```

```python
import functools

import jax
import jax.numpy as jnp
from jax import lax
from jax.experimental import pallas as pl
from jax.experimental.pallas import tpu as pltpu
from jax.sharding import PartitionSpec as P

SHARES = (3, 2, 1)
TRANSPOSED = (((0,), (0,)), ((), ()))


def from_behind(array, axis, by):
    devices = lax.axis_size(axis)
    return lax.ppermute(array, axis, [(i, (i + by) % devices) for i in range(devices)])


def swap_near(array):
    devices = lax.axis_size("blk")
    return lax.ppermute(array, "blk", [(i, i ^ 1) for i in range(devices)])


def swap_far(array):
    devices = lax.axis_size("blk")
    return lax.ppermute(
        array, "blk", [(i, (i + 1 if i % 2 else i - 1) % devices) for i in range(devices)]
    )


def on_chip(shape, dtype):
    return pltpu.VMEM(shape, dtype)


def call(kernel, out_shape, arrays, flops, scalars=(), hbm=(), scratch=(), to_hbm=False, alias=False):
    scalar, vector, main = (
        pl.BlockSpec(memory_space=m) for m in (pltpu.SMEM, pltpu.VMEM, pltpu.HBM)
    )
    placed = list(scalars)
    placed += [pltpu.with_memory_space_constraint(x, pltpu.VMEM) for x in arrays]
    placed += [pltpu.with_memory_space_constraint(x, pltpu.HBM) for x in hbm]
    target = main if to_hbm else vector
    return pl.pallas_call(
        kernel,
        out_shape=out_shape,
        in_specs=[scalar] * len(scalars) + [vector] * len(arrays) + [main] * len(hbm),
        out_specs=tuple(target for _ in out_shape) if isinstance(out_shape, tuple) else target,
        scratch_shapes=list(scratch),
        input_output_aliases={len(placed) - 1: 0} if alias else {},
        compiler_params=pltpu.CompilerParams(vmem_limit_bytes=16 << 20),
        cost_estimate=pl.CostEstimate(flops=flops, bytes_accessed=1 << 20, transcendentals=0),
    )(*placed)


def far_offset():
    return 2 * lax.rem(lax.axis_index("blk"), 2)


def copy_all(pairs, sems):
    copies = [pltpu.make_async_copy(*pair, sems.at[i]) for i, pair in enumerate(pairs)]
    for copy in copies:
        copy.start()
    for copy in copies:
        copy.wait()


def half_rows(basis, group, half):
    return basis.at[0, 0, pl.ds(pl.multiple_of(group * half, half), half)]


def cut_kernel(sketch, basis, lent, part, sems):
    theirs = half_rows(basis, 1 - lax.axis_index("group"), lent.shape[0])
    copy_all([(sketch.at[:, pl.ds(0, part.shape[1])], part), (theirs, lent)], sems)


def hand_out(own, part, start):
    part[...] = own[:, pl.ds(start, part.shape[1])]


def stage_kernel(begun, sketch, tiles, basis, own, staged, kept, sems):
    del begun
    ours = half_rows(basis, lax.axis_index("group"), kept.shape[0])
    copy_all([(sketch, own), (tiles.at[0, 0, :, 0], staged), (ours, kept)], sems)


def local_kernel(start, row_blocks, owner_route, tiles, own, near, hit, miss, stays, part):
    far = far_offset()
    owner = owner_route[row_blocks[far]]
    own_hits = owner_route[row_blocks[1]] == owner
    near_hits = owner_route[row_blocks[2 - far]] == owner
    hand_out(own, part, start)
    step = 256
    for place in range(0, own.shape[1], step):
        columns = pl.ds(place, step)
        first = jnp.dot(tiles[1], own[:, columns], preferred_element_type=jnp.float32)
        second = jnp.dot(tiles[2 - far], near[:, columns], preferred_element_type=jnp.float32)
        hit[:, columns] = jnp.where(own_hits, first, 0.0) + jnp.where(near_hits, second, 0.0)
        miss[:, columns] = (
            jnp.where(own_hits, 0.0, first) + jnp.where(near_hits, 0.0, second)
        ).astype(jnp.bfloat16)
    stays[...] = jnp.full(stays.shape, jnp.where(owner == lax.axis_index("group"), 1.0, 0.0))


def turn_kernel(kept, lent, miss, stays, hit_turned, missed):
    stay = stays[:, pl.ds(0, kept.shape[0])] > 0.0
    ours, theirs = kept[...].T, lent[...].T
    hit_turned[...] = jnp.where(stay, ours, theirs)
    missed[...] = jnp.dot(
        jnp.where(stay, theirs, ours), miss[...], preferred_element_type=jnp.float32
    )


def far_kernel(start, next_start, tiles, far, hit, hit_turned, missed, stays, own, *outs):
    kept, sent, *parts = outs
    for part in parts:
        hand_out(own, part, next_start)
    columns = pl.ds(start, far.shape[1])
    product = jnp.dot(tiles[far_offset()], far[...], preferred_element_type=jnp.float32)
    sampled = (hit[:, columns] + product).astype(jnp.bfloat16)
    made = jnp.dot(hit_turned[...], sampled, preferred_element_type=jnp.float32)
    stay = stays[:, columns] > 0.0
    other = missed[:, columns]
    sent[...] = jnp.where(stay, other, made).astype(jnp.bfloat16)
    kept[...] = jnp.where(stay, made, other)


def join_kernel(start, kept, received, *rest):
    out, total, sems = rest[-3:]
    total[...] = kept[...] + received[...].astype(jnp.float32)
    copy_all([(total, out.at[:, pl.ds(start, total.shape[1])])], sems)


def paired_body(sketch, far_tiles, row_blocks, owner_route, cluster_basis):
    panels, columns = sketch.shape
    offsets, rows = far_tiles.shape[2], far_tiles.shape[4]
    half, rank = cluster_basis.shape[2] // 2, cluster_basis.shape[3]
    widths = [columns * share // sum(SHARES) for share in SHARES]
    starts = [sum(widths[:i]) for i in range(len(widths))]
    product = 2 * rows * panels * columns
    short, wide = sketch.dtype, jnp.float32
    copies = pltpu.SemaphoreType.DMA
    lent, part = call(
        cut_kernel,
        (on_chip((half, rank), short), on_chip((panels, widths[0]), short)),
        (),
        0,
        hbm=(sketch, cluster_basis),
        scratch=(copies((2,)),),
    )
    own, tiles, kept = call(
        stage_kernel,
        (
            on_chip((panels, columns), short),
            on_chip((offsets, rows, panels), short),
            on_chip((half, rank), short),
        ),
        (part,),
        0,
        hbm=(sketch, far_tiles, cluster_basis),
        scratch=(copies((3,)),),
    )
    lent = from_behind(lent, "group", 1)
    fars = [swap_far(part)]
    near = swap_near(sketch)
    hit, miss, stays, part = call(
        functools.partial(local_kernel, starts[1]),
        (
            on_chip((rows, columns), wide),
            on_chip((rows, columns), short),
            on_chip((1, columns), wide),
            on_chip((panels, widths[1]), short),
        ),
        (tiles, own, near),
        2 * product,
        scalars=(row_blocks.reshape(-1), owner_route.reshape(-1)),
    )
    fars.append(swap_far(part))
    hit_turned, missed = call(
        turn_kernel,
        (on_chip((rank, half), short), on_chip((rank, columns), wide)),
        (kept, lent, miss, stays),
        product // 2,
    )
    out = None
    for i, (start, width) in enumerate(zip(starts, widths)):
        ahead = i + 2
        more = ahead < len(widths)
        kept, sent, *parts = call(
            functools.partial(far_kernel, start, starts[ahead] if more else None),
            (
                on_chip((rank, width), wide),
                on_chip((rank, width), short),
                *((on_chip((panels, widths[ahead]), short),) if more else ()),
            ),
            (tiles, fars[i], hit, hit_turned, missed, stays, own),
            2 * product * width // columns,
        )
        fars += [swap_far(part) for part in parts]
        out = call(
            functools.partial(join_kernel, start),
            pltpu.HBM((rank, columns), wide),
            (kept, from_behind(sent, "group", 1)),
            1 << 16,
            hbm=() if out is None else (out,),
            scratch=(on_chip((rank, width), wide), copies((1,))),
            to_hbm=True,
            alias=out is not None,
        )
    return out[None, None]


def contribute(summed, far_tiles, row_blocks, offset, current):
    product = jnp.einsum(
        "trk,kc->trc", far_tiles[0, 0, offset], current, preferred_element_type=jnp.float32
    )
    return summed.at[row_blocks[0, 0, offset]].add(product)


def ring_body(sketch, far_tiles, row_blocks, owner_route, cluster_basis):
    offsets = far_tiles.shape[2]
    radius = (offsets - 1) // 2
    groups = lax.axis_size("group")
    tile_rows = far_tiles.shape[4]
    columns = sketch.shape[1]
    summed = jnp.zeros((groups, tile_rows, columns), jnp.float32)
    for offset in range(offsets):
        current = from_behind(sketch, "blk", radius - offset) if offset != radius else sketch
        summed = contribute(summed, far_tiles, row_blocks, offset, current)
    sampled = summed.astype(jnp.bfloat16)
    ordered = jnp.zeros_like(sampled).at[owner_route[0, 0]].set(sampled)
    received = lax.all_to_all(ordered, "group", split_axis=0, concat_axis=0, tiled=True)
    stacked = received.reshape(received.shape[0] * received.shape[1], received.shape[2])
    coefficients = lax.dot_general(
        cluster_basis[0, 0], stacked, TRANSPOSED, preferred_element_type=jnp.float32
    )
    return coefficients[None, None]


def body(sketch, far_tiles, row_blocks, owner_route, cluster_basis):
    small = cluster_basis.shape[3] < far_tiles.shape[4]
    paired = lax.axis_size("group") == 2 and lax.axis_size("blk") % 2 == 0
    if small and paired and far_tiles.shape[2:4] == (3, 1):
        return paired_body(sketch, far_tiles, row_blocks, owner_route, cluster_basis)
    return ring_body(sketch, far_tiles, row_blocks, owner_route, cluster_basis)


def solution(mesh):
    placed = (
        P("blk", None),
        P("blk", "group", None, None, None, None),
        P("blk", "group", None, None),
        P("blk", "group", None),
        P("blk", "group", None, None),
    )
    return jax.shard_map(
        body, mesh=mesh, in_specs=placed, out_specs=P("blk", "group", None, None), check_vma=False
    )
```

```python
import functools

import jax
import jax.numpy as jnp
from jax import lax
from jax.experimental import pallas as pl
from jax.experimental.pallas import tpu as pltpu
from jax.sharding import PartitionSpec as P

SHARES = (2, 1)
TRANSPOSED = (((0,), (0,)), ((), ()))


def from_behind(array, axis, by):
    devices = lax.axis_size(axis)
    return lax.ppermute(array, axis, [(i, (i + by) % devices) for i in range(devices)])


def swap_near(array):
    devices = lax.axis_size("blk")
    return lax.ppermute(array, "blk", [(i, i ^ 1) for i in range(devices)])


def swap_far(array):
    devices = lax.axis_size("blk")
    return lax.ppermute(
        array, "blk", [(i, (i + 1 if i % 2 else i - 1) % devices) for i in range(devices)]
    )


def on_chip(shape, dtype):
    return pltpu.VMEM(shape, dtype)


def call(kernel, out_shape, arrays, flops, scalars=(), hbm=(), scratch=(), to_hbm=False, alias=False):
    scalar, vector, main = (
        pl.BlockSpec(memory_space=m) for m in (pltpu.SMEM, pltpu.VMEM, pltpu.HBM)
    )
    placed = list(scalars)
    placed += [pltpu.with_memory_space_constraint(x, pltpu.VMEM) for x in arrays]
    placed += [pltpu.with_memory_space_constraint(x, pltpu.HBM) for x in hbm]
    target = main if to_hbm else vector
    return pl.pallas_call(
        kernel,
        out_shape=out_shape,
        in_specs=[scalar] * len(scalars) + [vector] * len(arrays) + [main] * len(hbm),
        out_specs=tuple(target for _ in out_shape) if isinstance(out_shape, tuple) else target,
        scratch_shapes=list(scratch),
        input_output_aliases={len(placed) - 1: 0} if alias else {},
        compiler_params=pltpu.CompilerParams(vmem_limit_bytes=16 << 20),
        cost_estimate=pl.CostEstimate(flops=flops, bytes_accessed=1 << 20, transcendentals=0),
    )(*placed)


def far_offset():
    return 2 * lax.rem(lax.axis_index("blk"), 2)


def copy_all(pairs, sems):
    copies = [pltpu.make_async_copy(*pair, sems.at[i]) for i, pair in enumerate(pairs)]
    for copy in copies:
        copy.start()
    for copy in copies:
        copy.wait()


def half_rows(basis, group, half):
    return basis.at[0, 0, pl.ds(pl.multiple_of(group * half, half), half)]


def cut_kernel(sketch, basis, lent, part, sems):
    theirs = half_rows(basis, 1 - lax.axis_index("group"), lent.shape[0])
    copy_all([(sketch.at[:, pl.ds(0, part.shape[1])], part), (theirs, lent)], sems)


def stage_kernel(begun, sketch, tiles, basis, own, staged, kept, sems):
    del begun
    ours = half_rows(basis, lax.axis_index("group"), kept.shape[0])
    copy_all([(sketch, own), (tiles.at[0, 0, :, 0], staged), (ours, kept)], sems)


def local_kernel(start, row_blocks, owner_route, tiles, own, near, hit, miss, stays, part):
    far = far_offset()
    owner = owner_route[row_blocks[far]]
    own_hits = owner_route[row_blocks[1]] == owner
    near_hits = owner_route[row_blocks[2 - far]] == owner
    part[...] = own[:, pl.ds(start, part.shape[1])]
    step = 256
    for place in range(0, own.shape[1], step):
        columns = pl.ds(place, step)
        first = jnp.dot(tiles[1], own[:, columns], preferred_element_type=jnp.float32)
        second = jnp.dot(tiles[2 - far], near[:, columns], preferred_element_type=jnp.float32)
        hit[:, columns] = jnp.where(own_hits, first, 0.0) + jnp.where(near_hits, second, 0.0)
        miss[:, columns] = (
            jnp.where(own_hits, 0.0, first) + jnp.where(near_hits, 0.0, second)
        ).astype(jnp.bfloat16)
    stays[...] = jnp.full(stays.shape, jnp.where(owner == lax.axis_index("group"), 1.0, 0.0))


def turn_kernel(kept, lent, miss, stays, hit_turned, missed):
    stay = stays[:, pl.ds(0, kept.shape[0])] > 0.0
    ours, theirs = kept[...].T, lent[...].T
    hit_turned[...] = jnp.where(stay, ours, theirs)
    missed[...] = jnp.dot(
        jnp.where(stay, theirs, ours), miss[...], preferred_element_type=jnp.float32
    )


def far_kernel(start, tiles, far, hit, hit_turned, missed, stays, kept, sent):
    columns = pl.ds(start, far.shape[1])
    product = jnp.dot(tiles[far_offset()], far[...], preferred_element_type=jnp.float32)
    sampled = (hit[:, columns] + product).astype(jnp.bfloat16)
    made = jnp.dot(hit_turned[...], sampled, preferred_element_type=jnp.float32)
    stay = stays[:, columns] > 0.0
    other = missed[:, columns]
    sent[...] = jnp.where(stay, other, made).astype(jnp.bfloat16)
    kept[...] = jnp.where(stay, made, other)


def join_kernel(start, kept, received, *rest):
    out, total, sems = rest[-3:]
    total[...] = kept[...] + received[...].astype(jnp.float32)
    copy_all([(total, out.at[:, pl.ds(start, total.shape[1])])], sems)


def paired_body(sketch, far_tiles, row_blocks, owner_route, cluster_basis):
    panels, columns = sketch.shape
    offsets, rows = far_tiles.shape[2], far_tiles.shape[4]
    half, rank = cluster_basis.shape[2] // 2, cluster_basis.shape[3]
    widths = [columns * share // sum(SHARES) for share in SHARES]
    starts = [sum(widths[:i]) for i in range(len(widths))]
    product = 2 * rows * panels * columns
    short, wide = sketch.dtype, jnp.float32
    copies = pltpu.SemaphoreType.DMA
    lent, part = call(
        cut_kernel,
        (on_chip((half, rank), short), on_chip((panels, widths[0]), short)),
        (),
        0,
        hbm=(sketch, cluster_basis),
        scratch=(copies((2,)),),
    )
    own, tiles, kept = call(
        stage_kernel,
        (
            on_chip((panels, columns), short),
            on_chip((offsets, rows, panels), short),
            on_chip((half, rank), short),
        ),
        (part,),
        0,
        hbm=(sketch, far_tiles, cluster_basis),
        scratch=(copies((3,)),),
    )
    lent = from_behind(lent, "group", 1)
    fars = [swap_far(part)]
    near = swap_near(sketch)
    hit, miss, stays, part = call(
        functools.partial(local_kernel, starts[1]),
        (
            on_chip((rows, columns), wide),
            on_chip((rows, columns), short),
            on_chip((1, columns), wide),
            on_chip((panels, widths[1]), short),
        ),
        (tiles, own, near),
        2 * product,
        scalars=(row_blocks.reshape(-1), owner_route.reshape(-1)),
    )
    fars.append(swap_far(part))
    hit_turned, missed = call(
        turn_kernel,
        (on_chip((rank, half), short), on_chip((rank, columns), wide)),
        (kept, lent, miss, stays),
        product // 2,
    )
    out = None
    for i, (start, width) in enumerate(zip(starts, widths)):
        kept, sent = call(
            functools.partial(far_kernel, start),
            (on_chip((rank, width), wide), on_chip((rank, width), short)),
            (tiles, fars[i], hit, hit_turned, missed, stays),
            2 * product * width // columns,
        )
        out = call(
            functools.partial(join_kernel, start),
            pltpu.HBM((rank, columns), wide),
            (kept, from_behind(sent, "group", 1)),
            1 << 16,
            hbm=() if out is None else (out,),
            scratch=(on_chip((rank, width), wide), copies((1,))),
            to_hbm=True,
            alias=out is not None,
        )
    return out[None, None]


def contribute(summed, far_tiles, row_blocks, offset, current):
    product = jnp.einsum(
        "trk,kc->trc", far_tiles[0, 0, offset], current, preferred_element_type=jnp.float32
    )
    return summed.at[row_blocks[0, 0, offset]].add(product)


def ring_body(sketch, far_tiles, row_blocks, owner_route, cluster_basis):
    offsets = far_tiles.shape[2]
    radius = (offsets - 1) // 2
    groups = lax.axis_size("group")
    tile_rows = far_tiles.shape[4]
    columns = sketch.shape[1]
    summed = jnp.zeros((groups, tile_rows, columns), jnp.float32)
    for offset in range(offsets):
        current = from_behind(sketch, "blk", radius - offset) if offset != radius else sketch
        summed = contribute(summed, far_tiles, row_blocks, offset, current)
    sampled = summed.astype(jnp.bfloat16)
    ordered = jnp.zeros_like(sampled).at[owner_route[0, 0]].set(sampled)
    received = lax.all_to_all(ordered, "group", split_axis=0, concat_axis=0, tiled=True)
    stacked = received.reshape(received.shape[0] * received.shape[1], received.shape[2])
    coefficients = lax.dot_general(
        cluster_basis[0, 0], stacked, TRANSPOSED, preferred_element_type=jnp.float32
    )
    return coefficients[None, None]


def body(sketch, far_tiles, row_blocks, owner_route, cluster_basis):
    small = cluster_basis.shape[3] < far_tiles.shape[4]
    paired = lax.axis_size("group") == 2 and lax.axis_size("blk") % 2 == 0
    if small and paired and far_tiles.shape[2:4] == (3, 1):
        return paired_body(sketch, far_tiles, row_blocks, owner_route, cluster_basis)
    return ring_body(sketch, far_tiles, row_blocks, owner_route, cluster_basis)


def solution(mesh):
    placed = (
        P("blk", None),
        P("blk", "group", None, None, None, None),
        P("blk", "group", None, None),
        P("blk", "group", None),
        P("blk", "group", None, None),
    )
    return jax.shard_map(
        body, mesh=mesh, in_specs=placed, out_specs=P("blk", "group", None, None), check_vma=False
    )
```

```python
import functools

import jax
import jax.numpy as jnp
from jax import lax
from jax.experimental import pallas as pl
from jax.experimental.pallas import tpu as pltpu
from jax.sharding import PartitionSpec as P

SHARES = (3, 2, 1)
TRANSPOSED = (((0,), (0,)), ((), ()))


def from_behind(array, axis, by):
    devices = lax.axis_size(axis)
    return lax.ppermute(array, axis, [(i, (i + by) % devices) for i in range(devices)])


def swap_near(array):
    devices = lax.axis_size("blk")
    return lax.ppermute(array, "blk", [(i, i ^ 1) for i in range(devices)])


def swap_far(array):
    devices = lax.axis_size("blk")
    return lax.ppermute(
        array, "blk", [(i, (i + 1 if i % 2 else i - 1) % devices) for i in range(devices)]
    )


def on_chip(shape, dtype):
    return pltpu.VMEM(shape, dtype)


def call(kernel, out_shape, arrays, flops, scalars=(), hbm=(), scratch=(), to_hbm=False, alias=False):
    scalar, vector, main = (
        pl.BlockSpec(memory_space=m) for m in (pltpu.SMEM, pltpu.VMEM, pltpu.HBM)
    )
    placed = list(scalars)
    placed += [pltpu.with_memory_space_constraint(x, pltpu.VMEM) for x in arrays]
    placed += [pltpu.with_memory_space_constraint(x, pltpu.HBM) for x in hbm]
    target = main if to_hbm else vector
    return pl.pallas_call(
        kernel,
        out_shape=out_shape,
        in_specs=[scalar] * len(scalars) + [vector] * len(arrays) + [main] * len(hbm),
        out_specs=tuple(target for _ in out_shape) if isinstance(out_shape, tuple) else target,
        scratch_shapes=list(scratch),
        input_output_aliases={len(placed) - 1: 0} if alias else {},
        compiler_params=pltpu.CompilerParams(vmem_limit_bytes=16 << 20),
        cost_estimate=pl.CostEstimate(flops=flops, bytes_accessed=1 << 20, transcendentals=0),
    )(*placed)


def far_offset():
    return 2 * lax.rem(lax.axis_index("blk"), 2)


def copy_all(pairs, sems):
    copies = [pltpu.make_async_copy(*pair, sems.at[i]) for i, pair in enumerate(pairs)]
    for copy in copies:
        copy.start()
    for copy in copies:
        copy.wait()


def half_rows(basis, group, half):
    return basis.at[0, 0, pl.ds(pl.multiple_of(group * half, half), half)]


def cut_kernel(sketch, basis, lent, part, sems):
    theirs = half_rows(basis, 1 - lax.axis_index("group"), lent.shape[0])
    copy_all([(sketch.at[:, pl.ds(0, part.shape[1])], part), (theirs, lent)], sems)


def stage_kernel(begun, sketch, tiles, basis, own, staged, kept, sems):
    del begun
    ours = half_rows(basis, lax.axis_index("group"), kept.shape[0])
    copy_all([(sketch, own), (tiles.at[0, 0, :, 0], staged), (ours, kept)], sems)


def local_kernel(start, row_blocks, owner_route, tiles, own, near, hit, miss, stays, part):
    far = far_offset()
    owner = owner_route[row_blocks[far]]
    own_hits = owner_route[row_blocks[1]] == owner
    near_hits = owner_route[row_blocks[2 - far]] == owner
    part[...] = own[:, pl.ds(start, part.shape[1])]
    step = 256
    for place in range(0, own.shape[1], step):
        columns = pl.ds(place, step)
        first = jnp.dot(tiles[1], own[:, columns], preferred_element_type=jnp.float32)
        second = jnp.dot(tiles[2 - far], near[:, columns], preferred_element_type=jnp.float32)
        hit[:, columns] = jnp.where(own_hits, first, 0.0) + jnp.where(near_hits, second, 0.0)
        miss[:, columns] = (
            jnp.where(own_hits, 0.0, first) + jnp.where(near_hits, 0.0, second)
        ).astype(jnp.bfloat16)
    stays[...] = jnp.full(stays.shape, jnp.where(owner == lax.axis_index("group"), 1.0, 0.0))


def turn_kernel(start, kept, lent, miss, stays, own, hit_turned, missed, part):
    part[...] = own[:, pl.ds(start, part.shape[1])]
    stay = stays[:, pl.ds(0, kept.shape[0])] > 0.0
    ours, theirs = kept[...].T, lent[...].T
    hit_turned[...] = jnp.where(stay, ours, theirs)
    missed[...] = jnp.dot(
        jnp.where(stay, theirs, ours), miss[...], preferred_element_type=jnp.float32
    )


def far_kernel(start, tiles, far, hit, hit_turned, missed, stays, kept, sent):
    columns = pl.ds(start, far.shape[1])
    product = jnp.dot(tiles[far_offset()], far[...], preferred_element_type=jnp.float32)
    sampled = (hit[:, columns] + product).astype(jnp.bfloat16)
    made = jnp.dot(hit_turned[...], sampled, preferred_element_type=jnp.float32)
    stay = stays[:, columns] > 0.0
    other = missed[:, columns]
    sent[...] = jnp.where(stay, other, made).astype(jnp.bfloat16)
    kept[...] = jnp.where(stay, made, other)


def join_kernel(start, kept, received, *rest):
    out, total, sems = rest[-3:]
    total[...] = kept[...] + received[...].astype(jnp.float32)
    copy_all([(total, out.at[:, pl.ds(start, total.shape[1])])], sems)


def paired_body(sketch, far_tiles, row_blocks, owner_route, cluster_basis):
    panels, columns = sketch.shape
    offsets, rows = far_tiles.shape[2], far_tiles.shape[4]
    half, rank = cluster_basis.shape[2] // 2, cluster_basis.shape[3]
    widths = [columns * share // sum(SHARES) for share in SHARES]
    starts = [sum(widths[:i]) for i in range(len(widths))]
    product = 2 * rows * panels * columns
    short, wide = sketch.dtype, jnp.float32
    copies = pltpu.SemaphoreType.DMA
    lent, part = call(
        cut_kernel,
        (on_chip((half, rank), short), on_chip((panels, widths[0]), short)),
        (),
        0,
        hbm=(sketch, cluster_basis),
        scratch=(copies((2,)),),
    )
    own, tiles, kept = call(
        stage_kernel,
        (
            on_chip((panels, columns), short),
            on_chip((offsets, rows, panels), short),
            on_chip((half, rank), short),
        ),
        (part,),
        0,
        hbm=(sketch, far_tiles, cluster_basis),
        scratch=(copies((3,)),),
    )
    lent = from_behind(lent, "group", 1)
    fars = [swap_far(part)]
    near = swap_near(sketch)
    hit, miss, stays, part = call(
        functools.partial(local_kernel, starts[1]),
        (
            on_chip((rows, columns), wide),
            on_chip((rows, columns), short),
            on_chip((1, columns), wide),
            on_chip((panels, widths[1]), short),
        ),
        (tiles, own, near),
        2 * product,
        scalars=(row_blocks.reshape(-1), owner_route.reshape(-1)),
    )
    fars.append(swap_far(part))
    hit_turned, missed, part = call(
        functools.partial(turn_kernel, starts[2]),
        (
            on_chip((rank, half), short),
            on_chip((rank, columns), wide),
            on_chip((panels, widths[2]), short),
        ),
        (kept, lent, miss, stays, own),
        product // 2,
    )
    fars.append(swap_far(part))
    out = None
    for i, (start, width) in enumerate(zip(starts, widths)):
        kept, sent = call(
            functools.partial(far_kernel, start),
            (on_chip((rank, width), wide), on_chip((rank, width), short)),
            (tiles, fars[i], hit, hit_turned, missed, stays),
            2 * product * width // columns,
        )
        out = call(
            functools.partial(join_kernel, start),
            pltpu.HBM((rank, columns), wide),
            (kept, from_behind(sent, "group", 1)),
            1 << 16,
            hbm=() if out is None else (out,),
            scratch=(on_chip((rank, width), wide), copies((1,))),
            to_hbm=True,
            alias=out is not None,
        )
    return out[None, None]


def contribute(summed, far_tiles, row_blocks, offset, current):
    product = jnp.einsum(
        "trk,kc->trc", far_tiles[0, 0, offset], current, preferred_element_type=jnp.float32
    )
    return summed.at[row_blocks[0, 0, offset]].add(product)


def ring_body(sketch, far_tiles, row_blocks, owner_route, cluster_basis):
    offsets = far_tiles.shape[2]
    radius = (offsets - 1) // 2
    groups = lax.axis_size("group")
    tile_rows = far_tiles.shape[4]
    columns = sketch.shape[1]
    summed = jnp.zeros((groups, tile_rows, columns), jnp.float32)
    for offset in range(offsets):
        current = from_behind(sketch, "blk", radius - offset) if offset != radius else sketch
        summed = contribute(summed, far_tiles, row_blocks, offset, current)
    sampled = summed.astype(jnp.bfloat16)
    ordered = jnp.zeros_like(sampled).at[owner_route[0, 0]].set(sampled)
    received = lax.all_to_all(ordered, "group", split_axis=0, concat_axis=0, tiled=True)
    stacked = received.reshape(received.shape[0] * received.shape[1], received.shape[2])
    coefficients = lax.dot_general(
        cluster_basis[0, 0], stacked, TRANSPOSED, preferred_element_type=jnp.float32
    )
    return coefficients[None, None]


def body(sketch, far_tiles, row_blocks, owner_route, cluster_basis):
    small = cluster_basis.shape[3] < far_tiles.shape[4]
    paired = lax.axis_size("group") == 2 and lax.axis_size("blk") % 2 == 0
    if small and paired and far_tiles.shape[2:4] == (3, 1):
        return paired_body(sketch, far_tiles, row_blocks, owner_route, cluster_basis)
    return ring_body(sketch, far_tiles, row_blocks, owner_route, cluster_basis)


def solution(mesh):
    placed = (
        P("blk", None),
        P("blk", "group", None, None, None, None),
        P("blk", "group", None, None),
        P("blk", "group", None),
        P("blk", "group", None, None),
    )
    return jax.shard_map(
        body, mesh=mesh, in_specs=placed, out_specs=P("blk", "group", None, None), check_vma=False
    )
```

```python
import functools

import jax
import jax.numpy as jnp
from jax import lax
from jax.experimental import pallas as pl
from jax.experimental.pallas import tpu as pltpu
from jax.sharding import PartitionSpec as P

SHARES = (2, 1)
TRANSPOSED = (((0,), (0,)), ((), ()))


def from_behind(array, axis, by):
    devices = lax.axis_size(axis)
    return lax.ppermute(array, axis, [(i, (i + by) % devices) for i in range(devices)])


def swap_near(array):
    devices = lax.axis_size("blk")
    return lax.ppermute(array, "blk", [(i, i ^ 1) for i in range(devices)])


def swap_far(array):
    devices = lax.axis_size("blk")
    return lax.ppermute(
        array, "blk", [(i, (i + 1 if i % 2 else i - 1) % devices) for i in range(devices)]
    )


def on_chip(shape, dtype):
    return pltpu.VMEM(shape, dtype)


def call(kernel, out_shape, arrays, flops, scalars=(), hbm=(), scratch=(), to_hbm=False, alias=False):
    scalar, vector, main = (
        pl.BlockSpec(memory_space=m) for m in (pltpu.SMEM, pltpu.VMEM, pltpu.HBM)
    )
    placed = list(scalars)
    placed += [pltpu.with_memory_space_constraint(x, pltpu.VMEM) for x in arrays]
    placed += [pltpu.with_memory_space_constraint(x, pltpu.HBM) for x in hbm]
    target = main if to_hbm else vector
    return pl.pallas_call(
        kernel,
        out_shape=out_shape,
        in_specs=[scalar] * len(scalars) + [vector] * len(arrays) + [main] * len(hbm),
        out_specs=tuple(target for _ in out_shape) if isinstance(out_shape, tuple) else target,
        scratch_shapes=list(scratch),
        input_output_aliases={len(placed) - 1: 0} if alias else {},
        compiler_params=pltpu.CompilerParams(vmem_limit_bytes=16 << 20),
        cost_estimate=pl.CostEstimate(flops=flops, bytes_accessed=1 << 20, transcendentals=0),
    )(*placed)


def far_offset():
    return 2 * lax.rem(lax.axis_index("blk"), 2)


def copy_all(pairs, sems):
    copies = [pltpu.make_async_copy(*pair, sems.at[i]) for i, pair in enumerate(pairs)]
    for copy in copies:
        copy.start()
    for copy in copies:
        copy.wait()


def half_rows(basis, group, half):
    return basis.at[0, 0, pl.ds(pl.multiple_of(group * half, half), half)]


def cut_kernel(sketch, basis, lent, first, second, sems):
    theirs = half_rows(basis, 1 - lax.axis_index("group"), lent.shape[0])
    early, late = first.shape[1], second.shape[1]
    pairs = [
        (sketch.at[:, pl.ds(0, early)], first),
        (theirs, lent),
        (sketch.at[:, pl.ds(early, late)], second),
    ]
    copy_all(pairs, sems)


def stage_kernel(begun, sketch, tiles, basis, own, staged, kept, sems):
    del begun
    ours = half_rows(basis, lax.axis_index("group"), kept.shape[0])
    copy_all([(sketch, own), (tiles.at[0, 0, :, 0], staged), (ours, kept)], sems)


def local_kernel(row_blocks, owner_route, tiles, own, near, hit, miss, stays):
    far = far_offset()
    owner = owner_route[row_blocks[far]]
    own_hits = owner_route[row_blocks[1]] == owner
    near_hits = owner_route[row_blocks[2 - far]] == owner
    step = 256
    for place in range(0, own.shape[1], step):
        columns = pl.ds(place, step)
        first = jnp.dot(tiles[1], own[:, columns], preferred_element_type=jnp.float32)
        second = jnp.dot(tiles[2 - far], near[:, columns], preferred_element_type=jnp.float32)
        hit[:, columns] = jnp.where(own_hits, first, 0.0) + jnp.where(near_hits, second, 0.0)
        miss[:, columns] = (
            jnp.where(own_hits, 0.0, first) + jnp.where(near_hits, 0.0, second)
        ).astype(jnp.bfloat16)
    stays[...] = jnp.full(stays.shape, jnp.where(owner == lax.axis_index("group"), 1.0, 0.0))


def turn_kernel(kept, lent, miss, stays, hit_turned, missed):
    stay = stays[:, pl.ds(0, kept.shape[0])] > 0.0
    ours, theirs = kept[...].T, lent[...].T
    hit_turned[...] = jnp.where(stay, ours, theirs)
    missed[...] = jnp.dot(
        jnp.where(stay, theirs, ours), miss[...], preferred_element_type=jnp.float32
    )


def far_kernel(start, tiles, far, hit, hit_turned, missed, stays, kept, sent):
    columns = pl.ds(start, far.shape[1])
    product = jnp.dot(tiles[far_offset()], far[...], preferred_element_type=jnp.float32)
    sampled = (hit[:, columns] + product).astype(jnp.bfloat16)
    made = jnp.dot(hit_turned[...], sampled, preferred_element_type=jnp.float32)
    stay = stays[:, columns] > 0.0
    other = missed[:, columns]
    sent[...] = jnp.where(stay, other, made).astype(jnp.bfloat16)
    kept[...] = jnp.where(stay, made, other)


def join_kernel(start, kept, received, *rest):
    out, total, sems = rest[-3:]
    total[...] = kept[...] + received[...].astype(jnp.float32)
    copy_all([(total, out.at[:, pl.ds(start, total.shape[1])])], sems)


def paired_body(sketch, far_tiles, row_blocks, owner_route, cluster_basis):
    panels, columns = sketch.shape
    offsets, rows = far_tiles.shape[2], far_tiles.shape[4]
    half, rank = cluster_basis.shape[2] // 2, cluster_basis.shape[3]
    widths = [columns * share // sum(SHARES) for share in SHARES]
    starts = [sum(widths[:i]) for i in range(len(widths))]
    product = 2 * rows * panels * columns
    short, wide = sketch.dtype, jnp.float32
    copies = pltpu.SemaphoreType.DMA
    lent, *parts = call(
        cut_kernel,
        (on_chip((half, rank), short), *(on_chip((panels, width), short) for width in widths)),
        (),
        0,
        hbm=(sketch, cluster_basis),
        scratch=(copies((3,)),),
    )
    own, tiles, kept = call(
        stage_kernel,
        (
            on_chip((panels, columns), short),
            on_chip((offsets, rows, panels), short),
            on_chip((half, rank), short),
        ),
        (parts[0],),
        0,
        hbm=(sketch, far_tiles, cluster_basis),
        scratch=(copies((3,)),),
    )
    lent = from_behind(lent, "group", 1)
    fars = [swap_far(part) for part in parts]
    near = swap_near(sketch)
    hit, miss, stays = call(
        local_kernel,
        (
            on_chip((rows, columns), wide),
            on_chip((rows, columns), short),
            on_chip((1, columns), wide),
        ),
        (tiles, own, near),
        2 * product,
        scalars=(row_blocks.reshape(-1), owner_route.reshape(-1)),
    )
    hit_turned, missed = call(
        turn_kernel,
        (on_chip((rank, half), short), on_chip((rank, columns), wide)),
        (kept, lent, miss, stays),
        product // 2,
    )
    out = None
    for i, (start, width) in enumerate(zip(starts, widths)):
        kept, sent = call(
            functools.partial(far_kernel, start),
            (on_chip((rank, width), wide), on_chip((rank, width), short)),
            (tiles, fars[i], hit, hit_turned, missed, stays),
            2 * product * width // columns,
        )
        out = call(
            functools.partial(join_kernel, start),
            pltpu.HBM((rank, columns), wide),
            (kept, from_behind(sent, "group", 1)),
            1 << 16,
            hbm=() if out is None else (out,),
            scratch=(on_chip((rank, width), wide), copies((1,))),
            to_hbm=True,
            alias=out is not None,
        )
    return out[None, None]


def contribute(summed, far_tiles, row_blocks, offset, current):
    product = jnp.einsum(
        "trk,kc->trc", far_tiles[0, 0, offset], current, preferred_element_type=jnp.float32
    )
    return summed.at[row_blocks[0, 0, offset]].add(product)


def ring_body(sketch, far_tiles, row_blocks, owner_route, cluster_basis):
    offsets = far_tiles.shape[2]
    radius = (offsets - 1) // 2
    groups = lax.axis_size("group")
    tile_rows = far_tiles.shape[4]
    columns = sketch.shape[1]
    summed = jnp.zeros((groups, tile_rows, columns), jnp.float32)
    for offset in range(offsets):
        current = from_behind(sketch, "blk", radius - offset) if offset != radius else sketch
        summed = contribute(summed, far_tiles, row_blocks, offset, current)
    sampled = summed.astype(jnp.bfloat16)
    ordered = jnp.zeros_like(sampled).at[owner_route[0, 0]].set(sampled)
    received = lax.all_to_all(ordered, "group", split_axis=0, concat_axis=0, tiled=True)
    stacked = received.reshape(received.shape[0] * received.shape[1], received.shape[2])
    coefficients = lax.dot_general(
        cluster_basis[0, 0], stacked, TRANSPOSED, preferred_element_type=jnp.float32
    )
    return coefficients[None, None]


def body(sketch, far_tiles, row_blocks, owner_route, cluster_basis):
    small = cluster_basis.shape[3] < far_tiles.shape[4]
    paired = lax.axis_size("group") == 2 and lax.axis_size("blk") % 2 == 0
    if small and paired and far_tiles.shape[2:4] == (3, 1):
        return paired_body(sketch, far_tiles, row_blocks, owner_route, cluster_basis)
    return ring_body(sketch, far_tiles, row_blocks, owner_route, cluster_basis)


def solution(mesh):
    placed = (
        P("blk", None),
        P("blk", "group", None, None, None, None),
        P("blk", "group", None, None),
        P("blk", "group", None),
        P("blk", "group", None, None),
    )
    return jax.shard_map(
        body, mesh=mesh, in_specs=placed, out_specs=P("blk", "group", None, None), check_vma=False
    )
```

```python
import functools

import jax
import jax.numpy as jnp
from jax import lax
from jax.experimental import pallas as pl
from jax.experimental.pallas import tpu as pltpu
from jax.sharding import PartitionSpec as P

TRANSPOSED = (((0,), (0,)), ((), ()))


def from_behind(array, axis, by):
    devices = lax.axis_size(axis)
    return lax.ppermute(array, axis, [(i, (i + by) % devices) for i in range(devices)])


def permuted(array, target):
    blocks, groups = lax.axis_size("blk"), lax.axis_size("group")
    pairs = []
    for b in range(blocks):
        for g in range(groups):
            to_b, to_g = target(b, g)
            pairs.append((b * groups + g, to_b % blocks * groups + to_g))
    return lax.ppermute(array, ("blk", "group"), pairs)


def shares_rows(b):
    return (b + 1) // 2 % 2 == 0


def far_of(b, g):
    return (b + 1 if b % 2 else b - 1), g


def far_if_alone(b, g):
    return (b, g) if shares_rows(b) else far_of(b, g)


def other_group(b, g):
    return b, 1 - g


def other_group_if_shared(b, g):
    return other_group(b, g) if shares_rows(b) else (b, g)


def swap_near(array):
    return permuted(array, lambda b, g: (b ^ 1, g))


def on_chip(shape, dtype):
    return pltpu.VMEM(shape, dtype)


def call(kernel, out_shape, arrays, flops, scalars=(), hbm=(), scratch=(), to_hbm=False, alias=False):
    scalar, vector, main = (
        pl.BlockSpec(memory_space=m) for m in (pltpu.SMEM, pltpu.VMEM, pltpu.HBM)
    )
    placed = list(scalars)
    placed += [pltpu.with_memory_space_constraint(x, pltpu.VMEM) for x in arrays]
    placed += [pltpu.with_memory_space_constraint(x, pltpu.HBM) for x in hbm]
    target = main if to_hbm else vector
    return pl.pallas_call(
        kernel,
        out_shape=out_shape,
        in_specs=[scalar] * len(scalars) + [vector] * len(arrays) + [main] * len(hbm),
        out_specs=tuple(target for _ in out_shape) if isinstance(out_shape, tuple) else target,
        scratch_shapes=list(scratch),
        input_output_aliases={len(placed) - 1: 0} if alias else {},
        compiler_params=pltpu.CompilerParams(vmem_limit_bytes=16 << 20),
        cost_estimate=pl.CostEstimate(flops=flops, bytes_accessed=1 << 10, transcendentals=0),
    )(*placed)


def far_offset():
    return 2 * lax.rem(lax.axis_index("blk"), 2)


def copy_all(pairs, sems):
    copies = [pltpu.make_async_copy(*pair, sems.at[i]) for i, pair in enumerate(pairs)]
    for copy in copies:
        copy.start()
    for copy in copies:
        copy.wait()


def half_rows(basis, group, half):
    return basis.at[0, 0, pl.ds(pl.multiple_of(group * half, half), half)]


def shared_here():
    return lax.rem((lax.axis_index("blk") + 1) // 2, 2) == 0


def half_start(group, half):
    return pl.multiple_of(group * half, half)


def cut_kernel(sketch, basis, lent, first, last, sems):
    group = lax.axis_index("group")
    width = last.shape[1]
    half = first.shape[0] // 2
    part = [pl.ds(i * width, width) for i in range(3)]
    shared = shared_here()
    copies = [
        (sketch.at[:, part[0]], first.at[:, part[0]]),
        (half_rows(basis, 1 - group, lent.shape[0]), lent),
        (sketch.at[:, part[2]], last),
    ]
    whole = [(sketch.at[:, part[1]], first.at[:, part[1]])]
    rows = pl.ds(half_start(group, half), half)
    halves = [
        (sketch.at[rows, part[i + 1]], first.at[pl.ds(i * half, half), part[1]]) for i in range(2)
    ]

    @pl.when(shared)
    def _():
        copy_all(copies + halves, sems)

    @pl.when(jnp.logical_not(shared))
    def _():
        copy_all(copies + whole, sems)


def stage_kernel(begun, sketch, tiles, basis, own, staged, kept, sems):
    del begun
    ours = half_rows(basis, lax.axis_index("group"), kept.shape[0])
    copy_all([(sketch, own), (tiles.at[0, 0, :, 0], staged), (ours, kept)], sems)


def local_kernel(row_blocks, owner_route, tiles, own, near, hit, miss, stays):
    far = far_offset()
    owner = owner_route[row_blocks[far]]
    own_hits = owner_route[row_blocks[1]] == owner
    near_hits = owner_route[row_blocks[2 - far]] == owner
    step = 256
    for place in range(0, own.shape[1], step):
        columns = pl.ds(place, step)
        first = jnp.dot(tiles[1], own[:, columns], preferred_element_type=jnp.float32)
        second = jnp.dot(tiles[2 - far], near[:, columns], preferred_element_type=jnp.float32)
        hit[:, columns] = jnp.where(own_hits, first, 0.0) + jnp.where(near_hits, second, 0.0)
        miss[:, columns] = (
            jnp.where(own_hits, 0.0, first) + jnp.where(near_hits, 0.0, second)
        ).astype(jnp.bfloat16)
    stays[...] = jnp.full(stays.shape, jnp.where(owner == lax.axis_index("group"), 1.0, 0.0))


def turn_kernel(kept, lent, miss, stays, hit_turned, missed):
    stay = stays[:, pl.ds(0, kept.shape[0])] > 0.0
    ours, theirs = kept[...].T, lent[...].T
    hit_turned[...] = jnp.where(stay, ours, theirs)
    missed[...] = jnp.dot(
        jnp.where(stay, theirs, ours), miss[...], preferred_element_type=jnp.float32
    )


def finish(start, tiles, far, hit, hit_turned, missed, stays, kept, sent):
    columns = pl.ds(start, kept.shape[1])
    product = jnp.dot(tiles[far_offset()], far, preferred_element_type=jnp.float32)
    sampled = (hit[:, columns] + product).astype(jnp.bfloat16)
    made = jnp.dot(hit_turned[...], sampled, preferred_element_type=jnp.float32)
    stay = stays[:, columns] > 0.0
    other = missed[:, columns]
    sent[...] = jnp.where(stay, other, made).astype(jnp.bfloat16)
    kept[...] = jnp.where(stay, made, other)


def first_kernel(first, tiles, hit, hit_turned, missed, stays, kept, sent, *halves):
    width = kept.shape[1]
    for i, ours in enumerate(halves):
        rows = ours.shape[0]
        ours[...] = first[pl.ds(i * rows, rows), pl.ds(width, width)]
    finish(0, tiles, first[:, pl.ds(0, width)], hit, hit_turned, missed, stays, kept, sent)


def later_kernel(i, before, alone, ours, theirs, tiles, hit, hit_turned, missed, stays, kept, sent, far):
    del before
    half, width = ours.shape
    group = lax.axis_index("group")
    shared = shared_here()

    @pl.when(shared)
    def _():
        far[pl.ds(half_start(group, half), half), :] = ours[...]
        far[pl.ds(half_start(1 - group, half), half), :] = theirs[...]

    @pl.when(jnp.logical_not(shared))
    def _():
        far[...] = alone[:, pl.ds(alone.shape[1] - width, width)]

    finish(i * width, tiles, far[...], hit, hit_turned, missed, stays, kept, sent)


def join_kernel(start, kept, received, *rest):
    out, total, sems = rest[-3:]
    total[...] = kept[...] + received[...].astype(jnp.float32)
    copy_all([(total, out.at[:, pl.ds(start, total.shape[1])])], sems)


def paired_body(sketch, far_tiles, row_blocks, owner_route, cluster_basis):
    panels, columns = sketch.shape
    offsets, rows = far_tiles.shape[2], far_tiles.shape[4]
    half, rank = cluster_basis.shape[2] // 2, cluster_basis.shape[3]
    width = columns // 3
    product = 2 * rows * panels * columns
    short, wide = sketch.dtype, jnp.float32
    copies = pltpu.SemaphoreType.DMA
    lent, first, last = call(
        cut_kernel,
        (
            on_chip((half, rank), short),
            on_chip((panels, 2 * width), short),
            on_chip((panels, width), short),
        ),
        (),
        0,
        hbm=(sketch, cluster_basis),
        scratch=(copies((5,)),),
    )
    own, tiles, kept = call(
        stage_kernel,
        (
            on_chip((panels, columns), short),
            on_chip((offsets, rows, panels), short),
            on_chip((half, rank), short),
        ),
        (lent,),
        0,
        hbm=(sketch, far_tiles, cluster_basis),
        scratch=(copies((3,)),),
    )
    first = permuted(first, far_of)
    lent = permuted(lent, other_group)
    last = permuted(last, far_if_alone)
    near = swap_near(sketch)
    hit, miss, stays = call(
        local_kernel,
        (
            on_chip((rows, columns), wide),
            on_chip((rows, columns), short),
            on_chip((1, columns), wide),
        ),
        (tiles, own, near),
        2 * product,
        scalars=(row_blocks.reshape(-1), owner_route.reshape(-1)),
    )
    hit_turned, missed = call(
        turn_kernel,
        (on_chip((rank, half), short), on_chip((rank, columns), wide)),
        (kept, lent, miss, stays),
        product // 2,
    )
    results = on_chip((rank, width), wide), on_chip((rank, width), short)
    common = tiles, hit, hit_turned, missed, stays
    kept, sent, *ours = call(
        first_kernel,
        (*results, *(on_chip((panels // 2, width), short),) * 2),
        (first, *common),
        0,
    )
    theirs = [permuted(part, other_group_if_shared) for part in ours]
    done = [(kept, permuted(sent, other_group))]
    for i, alone in ((1, first), (2, last)):
        kept, sent = call(
            functools.partial(later_kernel, i),
            results,
            (sent, alone, ours[i - 1], theirs[i - 1], *common),
            0,
            scratch=(on_chip((panels, width), short),),
        )
        done.append((kept, permuted(sent, other_group)))
    out = None
    for i, pair in enumerate(done):
        out = call(
            functools.partial(join_kernel, i * width),
            pltpu.HBM((rank, columns), wide),
            pair,
            1 << 16,
            hbm=() if out is None else (out,),
            scratch=(on_chip((rank, width), wide), copies((1,))),
            to_hbm=True,
            alias=out is not None,
        )
    return out[None, None]


def contribute(summed, far_tiles, row_blocks, offset, current):
    product = jnp.einsum(
        "trk,kc->trc", far_tiles[0, 0, offset], current, preferred_element_type=jnp.float32
    )
    return summed.at[row_blocks[0, 0, offset]].add(product)


def ring_body(sketch, far_tiles, row_blocks, owner_route, cluster_basis):
    offsets = far_tiles.shape[2]
    radius = (offsets - 1) // 2
    groups = lax.axis_size("group")
    tile_rows = far_tiles.shape[4]
    columns = sketch.shape[1]
    summed = jnp.zeros((groups, tile_rows, columns), jnp.float32)
    for offset in range(offsets):
        current = from_behind(sketch, "blk", radius - offset) if offset != radius else sketch
        summed = contribute(summed, far_tiles, row_blocks, offset, current)
    sampled = summed.astype(jnp.bfloat16)
    ordered = jnp.zeros_like(sampled).at[owner_route[0, 0]].set(sampled)
    received = lax.all_to_all(ordered, "group", split_axis=0, concat_axis=0, tiled=True)
    stacked = received.reshape(received.shape[0] * received.shape[1], received.shape[2])
    coefficients = lax.dot_general(
        cluster_basis[0, 0], stacked, TRANSPOSED, preferred_element_type=jnp.float32
    )
    return coefficients[None, None]


def body(sketch, far_tiles, row_blocks, owner_route, cluster_basis):
    small = cluster_basis.shape[3] < far_tiles.shape[4]
    paired = lax.axis_size("group") == 2 and lax.axis_size("blk") % 4 == 0
    if small and paired and far_tiles.shape[2:4] == (3, 1):
        return paired_body(sketch, far_tiles, row_blocks, owner_route, cluster_basis)
    return ring_body(sketch, far_tiles, row_blocks, owner_route, cluster_basis)


def solution(mesh):
    placed = (
        P("blk", None),
        P("blk", "group", None, None, None, None),
        P("blk", "group", None, None),
        P("blk", "group", None),
        P("blk", "group", None, None),
    )
    return jax.shard_map(
        body, mesh=mesh, in_specs=placed, out_specs=P("blk", "group", None, None), check_vma=False
    )
```

```python
import functools

import jax
import jax.numpy as jnp
from jax import lax
from jax.experimental import pallas as pl
from jax.experimental.pallas import tpu as pltpu
from jax.sharding import PartitionSpec as P

TRANSPOSED = (((0,), (0,)), ((), ()))


def from_behind(array, axis, by):
    devices = lax.axis_size(axis)
    return lax.ppermute(array, axis, [(i, (i + by) % devices) for i in range(devices)])


def swap_near(array):
    devices = lax.axis_size("blk")
    return lax.ppermute(array, "blk", [(i, i ^ 1) for i in range(devices)])


def swap_far(array):
    devices = lax.axis_size("blk")
    return lax.ppermute(
        array, "blk", [(i, (i + 1 if i % 2 else i - 1) % devices) for i in range(devices)]
    )


def on_chip(shape, dtype):
    return pltpu.VMEM(shape, dtype)


def call(kernel, out_shape, arrays, flops, scalars=(), hbm=(), scratch=(), to_hbm=False, alias=False):
    scalar, vector, main = (
        pl.BlockSpec(memory_space=m) for m in (pltpu.SMEM, pltpu.VMEM, pltpu.HBM)
    )
    placed = list(scalars)
    placed += [pltpu.with_memory_space_constraint(x, pltpu.VMEM) for x in arrays]
    placed += [pltpu.with_memory_space_constraint(x, pltpu.HBM) for x in hbm]
    target = main if to_hbm else vector
    return pl.pallas_call(
        kernel,
        out_shape=out_shape,
        in_specs=[scalar] * len(scalars) + [vector] * len(arrays) + [main] * len(hbm),
        out_specs=tuple(target for _ in out_shape) if isinstance(out_shape, tuple) else target,
        scratch_shapes=list(scratch),
        input_output_aliases={len(placed) - 1: 0} if alias else {},
        compiler_params=pltpu.CompilerParams(vmem_limit_bytes=16 << 20),
        cost_estimate=pl.CostEstimate(flops=flops, bytes_accessed=1 << 10, transcendentals=0),
    )(*placed)


def far_offset():
    return 2 * lax.rem(lax.axis_index("blk"), 2)


def copy_all(pairs, sems):
    copies = [pltpu.make_async_copy(*pair, sems.at[i]) for i, pair in enumerate(pairs)]
    for copy in copies:
        copy.start()
    for copy in copies:
        copy.wait()


def half_rows(basis, group, half):
    return basis.at[0, 0, pl.ds(pl.multiple_of(group * half, half), half)]


def half_start(group, half):
    return pl.multiple_of(group * half, half)


def cut_kernel(sketch, basis, lent, first, last, sems):
    group = lax.axis_index("group")
    panels, width = last.shape
    half = panels // 2
    part = [pl.ds(i * width, width) for i in range(3)]
    ours = pl.ds(half_start(group, half), half)
    pairs = [
        (sketch.at[ours, part[0]], first.at[pl.ds(0, half)]),
        (sketch.at[:, part[1]], first.at[pl.ds(half, panels)]),
        (half_rows(basis, 1 - group, lent.shape[0]), lent),
        (sketch.at[:, part[2]], last),
    ]
    copy_all(pairs, sems)


def stage_kernel(begun, sketch, tiles, basis, own, staged, kept, sems):
    del begun
    ours = half_rows(basis, lax.axis_index("group"), kept.shape[0])
    copy_all([(sketch, own), (tiles.at[0, 0, :, 0], staged), (ours, kept)], sems)


def local_kernel(row_blocks, owner_route, tiles, own, near, hit, miss, stays):
    far = far_offset()
    owner = owner_route[row_blocks[far]]
    own_hits = owner_route[row_blocks[1]] == owner
    near_hits = owner_route[row_blocks[2 - far]] == owner
    step = 256
    for place in range(0, own.shape[1], step):
        columns = pl.ds(place, step)
        first = jnp.dot(tiles[1], own[:, columns], preferred_element_type=jnp.float32)
        second = jnp.dot(tiles[2 - far], near[:, columns], preferred_element_type=jnp.float32)
        hit[:, columns] = jnp.where(own_hits, first, 0.0) + jnp.where(near_hits, second, 0.0)
        miss[:, columns] = (
            jnp.where(own_hits, 0.0, first) + jnp.where(near_hits, 0.0, second)
        ).astype(jnp.bfloat16)
    stays[...] = jnp.full(stays.shape, jnp.where(owner == lax.axis_index("group"), 1.0, 0.0))


def turn_kernel(kept, lent, miss, stays, hit_turned, missed):
    stay = stays[:, pl.ds(0, kept.shape[0])] > 0.0
    ours, theirs = kept[...].T, lent[...].T
    hit_turned[...] = jnp.where(stay, ours, theirs)
    missed[...] = jnp.dot(
        jnp.where(stay, theirs, ours), miss[...], preferred_element_type=jnp.float32
    )


def hand_kernel(before, first, ours):
    del before
    ours[...] = first[pl.ds(0, ours.shape[0]), :]


def finish(start, tiles, far, hit, hit_turned, missed, stays, kept, sent):
    columns = pl.ds(start, kept.shape[1])
    product = jnp.dot(tiles[far_offset()], far, preferred_element_type=jnp.float32)
    sampled = (hit[:, columns] + product).astype(jnp.bfloat16)
    made = jnp.dot(hit_turned[...], sampled, preferred_element_type=jnp.float32)
    stay = stays[:, columns] > 0.0
    other = missed[:, columns]
    sent[...] = jnp.where(stay, other, made).astype(jnp.bfloat16)
    kept[...] = jnp.where(stay, made, other)


def whole_kernel(start, before, far, tiles, *refs):
    del before
    panels = tiles.shape[2]
    finish(start, tiles, far[pl.ds(far.shape[0] - panels, panels), :], *refs)


def shared_kernel(start, before, ours, theirs, tiles, hit, hit_turned, missed, stays, kept, sent, far):
    del before
    half = ours.shape[0]
    group = lax.axis_index("group")
    far[pl.ds(half_start(group, half), half), :] = ours[...]
    far[pl.ds(half_start(1 - group, half), half), :] = theirs[...]
    finish(start, tiles, far[...], hit, hit_turned, missed, stays, kept, sent)


def join_kernel(start, kept, received, *rest):
    out, total, sems = rest[-3:]
    total[...] = kept[...] + received[...].astype(jnp.float32)
    copy_all([(total, out.at[:, pl.ds(start, total.shape[1])])], sems)


def paired_body(sketch, far_tiles, row_blocks, owner_route, cluster_basis):
    panels, columns = sketch.shape
    offsets, rows = far_tiles.shape[2], far_tiles.shape[4]
    half, rank = cluster_basis.shape[2] // 2, cluster_basis.shape[3]
    width = columns // 3
    product = 2 * rows * panels * columns
    short, wide = sketch.dtype, jnp.float32
    copies = pltpu.SemaphoreType.DMA
    lent, first, last = call(
        cut_kernel,
        (
            on_chip((half, rank), short),
            on_chip((panels + panels // 2, width), short),
            on_chip((panels, width), short),
        ),
        (),
        0,
        hbm=(sketch, cluster_basis),
        scratch=(copies((4,)),),
    )
    own, tiles, kept = call(
        stage_kernel,
        (
            on_chip((panels, columns), short),
            on_chip((offsets, rows, panels), short),
            on_chip((half, rank), short),
        ),
        (lent,),
        0,
        hbm=(sketch, far_tiles, cluster_basis),
        scratch=(copies((3,)),),
    )
    first = swap_far(first)
    lent = from_behind(lent, "group", 1)
    last = swap_far(last)
    near = swap_near(sketch)
    hit, miss, stays = call(
        local_kernel,
        (
            on_chip((rows, columns), wide),
            on_chip((rows, columns), short),
            on_chip((1, columns), wide),
        ),
        (tiles, own, near),
        2 * product,
        scalars=(row_blocks.reshape(-1), owner_route.reshape(-1)),
    )
    hit_turned, missed = call(
        turn_kernel,
        (on_chip((rank, half), short), on_chip((rank, columns), wide)),
        (kept, lent, miss, stays),
        product // 2,
    )
    ours = call(hand_kernel, on_chip((panels // 2, width), short), (hit_turned, first), 0)
    theirs = from_behind(ours, "group", 1)
    far = on_chip((panels, width), short)
    work = (
        (width, whole_kernel, (first,), ()),
        (2 * width, whole_kernel, (last,), ()),
        (0, shared_kernel, (ours, theirs), (far,)),
    )
    out, before = None, ours
    for start, kernel, panel, scratch in work:
        kept, before = call(
            functools.partial(kernel, start),
            (on_chip((rank, width), wide), on_chip((rank, width), short)),
            (before, *panel, tiles, hit, hit_turned, missed, stays),
            0,
            scratch=scratch,
        )
        out = call(
            functools.partial(join_kernel, start),
            pltpu.HBM((rank, columns), wide),
            (kept, from_behind(before, "group", 1)),
            0,
            hbm=() if out is None else (out,),
            scratch=(on_chip((rank, width), wide), copies((1,))),
            to_hbm=True,
            alias=out is not None,
        )
    return out[None, None]


def contribute(summed, far_tiles, row_blocks, offset, current):
    product = jnp.einsum(
        "trk,kc->trc", far_tiles[0, 0, offset], current, preferred_element_type=jnp.float32
    )
    return summed.at[row_blocks[0, 0, offset]].add(product)


def ring_body(sketch, far_tiles, row_blocks, owner_route, cluster_basis):
    offsets = far_tiles.shape[2]
    radius = (offsets - 1) // 2
    groups = lax.axis_size("group")
    tile_rows = far_tiles.shape[4]
    columns = sketch.shape[1]
    summed = jnp.zeros((groups, tile_rows, columns), jnp.float32)
    for offset in range(offsets):
        current = from_behind(sketch, "blk", radius - offset) if offset != radius else sketch
        summed = contribute(summed, far_tiles, row_blocks, offset, current)
    sampled = summed.astype(jnp.bfloat16)
    ordered = jnp.zeros_like(sampled).at[owner_route[0, 0]].set(sampled)
    received = lax.all_to_all(ordered, "group", split_axis=0, concat_axis=0, tiled=True)
    stacked = received.reshape(received.shape[0] * received.shape[1], received.shape[2])
    coefficients = lax.dot_general(
        cluster_basis[0, 0], stacked, TRANSPOSED, preferred_element_type=jnp.float32
    )
    return coefficients[None, None]


def body(sketch, far_tiles, row_blocks, owner_route, cluster_basis):
    small = cluster_basis.shape[3] < far_tiles.shape[4]
    paired = lax.axis_size("group") == 2 and lax.axis_size("blk") % 2 == 0
    if small and paired and far_tiles.shape[2:4] == (3, 1):
        return paired_body(sketch, far_tiles, row_blocks, owner_route, cluster_basis)
    return ring_body(sketch, far_tiles, row_blocks, owner_route, cluster_basis)


def solution(mesh):
    placed = (
        P("blk", None),
        P("blk", "group", None, None, None, None),
        P("blk", "group", None, None),
        P("blk", "group", None),
        P("blk", "group", None, None),
    )
    return jax.shard_map(
        body, mesh=mesh, in_specs=placed, out_specs=P("blk", "group", None, None), check_vma=False
    )
```

```python
import functools

import jax
import jax.numpy as jnp
from jax import lax
from jax.experimental import pallas as pl
from jax.experimental.pallas import tpu as pltpu
from jax.sharding import PartitionSpec as P

SHARES = (2, 1)
TRANSPOSED = (((0,), (0,)), ((), ()))


def from_behind(array, axis, by):
    devices = lax.axis_size(axis)
    return lax.ppermute(array, axis, [(i, (i + by) % devices) for i in range(devices)])


def swap_near(array):
    devices = lax.axis_size("blk")
    return lax.ppermute(array, "blk", [(i, i ^ 1) for i in range(devices)])


def swap_far(array):
    devices = lax.axis_size("blk")
    return lax.ppermute(
        array, "blk", [(i, (i + 1 if i % 2 else i - 1) % devices) for i in range(devices)]
    )


def on_chip(shape, dtype):
    return pltpu.VMEM(shape, dtype)


def call(kernel, out_shape, arrays, flops, scalars=(), hbm=(), scratch=(), to_hbm=False, alias=False):
    scalar, vector, main = (
        pl.BlockSpec(memory_space=m) for m in (pltpu.SMEM, pltpu.VMEM, pltpu.HBM)
    )
    placed = list(scalars)
    placed += [pltpu.with_memory_space_constraint(x, pltpu.VMEM) for x in arrays]
    placed += [pltpu.with_memory_space_constraint(x, pltpu.HBM) for x in hbm]
    target = main if to_hbm else vector
    return pl.pallas_call(
        kernel,
        out_shape=out_shape,
        in_specs=[scalar] * len(scalars) + [vector] * len(arrays) + [main] * len(hbm),
        out_specs=tuple(target for _ in out_shape) if isinstance(out_shape, tuple) else target,
        scratch_shapes=list(scratch),
        input_output_aliases={len(placed) - 1: 0} if alias else {},
        compiler_params=pltpu.CompilerParams(vmem_limit_bytes=16 << 20),
        cost_estimate=pl.CostEstimate(flops=flops, bytes_accessed=1 << 20, transcendentals=0),
    )(*placed)


def far_offset():
    return 2 * lax.rem(lax.axis_index("blk"), 2)


def copy_all(pairs, sems):
    copies = [pltpu.make_async_copy(*pair, sems.at[i]) for i, pair in enumerate(pairs)]
    for copy in copies:
        copy.start()
    for copy in copies:
        copy.wait()


def half_rows(basis, group, half):
    return basis.at[0, 0, pl.ds(pl.multiple_of(group * half, half), half)]


def row_blocks_of(array, count=4):
    rows = array.shape[0] // count
    return [pl.ds(i * rows, rows) for i in range(count)]


def cut_kernel(sketch, basis, lent, first, second, sems):
    theirs = half_rows(basis, 1 - lax.axis_index("group"), lent.shape[0])
    early, late = pl.ds(0, first.shape[1]), pl.ds(first.shape[1], second.shape[1])
    pairs = [(sketch.at[rows, early], first.at[rows]) for rows in row_blocks_of(first)]
    pairs += [(theirs, lent), (sketch.at[:, late], second)]
    copy_all(pairs, sems)


def stage_kernel(begun, sketch, tiles, basis, own, staged, kept, sems):
    del begun
    ours = half_rows(basis, lax.axis_index("group"), kept.shape[0])
    copy_all([(sketch, own), (tiles.at[0, 0, :, 0], staged), (ours, kept)], sems)


def local_kernel(row_blocks, owner_route, tiles, own, near, hit, miss, stays):
    far = far_offset()
    owner = owner_route[row_blocks[far]]
    own_hits = owner_route[row_blocks[1]] == owner
    near_hits = owner_route[row_blocks[2 - far]] == owner
    step = 256
    for place in range(0, own.shape[1], step):
        columns = pl.ds(place, step)
        first = jnp.dot(tiles[1], own[:, columns], preferred_element_type=jnp.float32)
        second = jnp.dot(tiles[2 - far], near[:, columns], preferred_element_type=jnp.float32)
        hit[:, columns] = jnp.where(own_hits, first, 0.0) + jnp.where(near_hits, second, 0.0)
        miss[:, columns] = (
            jnp.where(own_hits, 0.0, first) + jnp.where(near_hits, 0.0, second)
        ).astype(jnp.bfloat16)
    stays[...] = jnp.full(stays.shape, jnp.where(owner == lax.axis_index("group"), 1.0, 0.0))


def turn_kernel(kept, lent, miss, stays, hit_turned, missed):
    stay = stays[:, pl.ds(0, kept.shape[0])] > 0.0
    ours, theirs = kept[...].T, lent[...].T
    hit_turned[...] = jnp.where(stay, ours, theirs)
    missed[...] = jnp.dot(
        jnp.where(stay, theirs, ours), miss[...], preferred_element_type=jnp.float32
    )


def far_kernel(start, tiles, far, hit, hit_turned, missed, stays, kept, sent):
    columns = pl.ds(start, far.shape[1])
    offset = far_offset()
    sampled = []
    for rows in row_blocks_of(hit, 2):
        product = jnp.dot(tiles[offset, rows], far[...], preferred_element_type=jnp.float32)
        sampled.append((hit[rows, columns] + product).astype(jnp.bfloat16))
    made = jnp.dot(
        hit_turned[...], jnp.concatenate(sampled), preferred_element_type=jnp.float32
    )
    stay = stays[:, columns] > 0.0
    other = missed[:, columns]
    sent[...] = jnp.where(stay, other, made).astype(jnp.bfloat16)
    kept[...] = jnp.where(stay, made, other)


def join_kernel(start, kept, received, *rest):
    out, total, sems = rest[-3:]
    columns = pl.ds(start, total.shape[1])
    under_way = []
    for i, rows in enumerate(row_blocks_of(total, 2)):
        total[rows] = kept[rows] + received[rows].astype(jnp.float32)
        copy = pltpu.make_async_copy(total.at[rows], out.at[rows, columns], sems.at[i])
        copy.start()
        under_way.append(copy)
    for copy in under_way:
        copy.wait()


def paired_body(sketch, far_tiles, row_blocks, owner_route, cluster_basis):
    panels, columns = sketch.shape
    offsets, rows = far_tiles.shape[2], far_tiles.shape[4]
    half, rank = cluster_basis.shape[2] // 2, cluster_basis.shape[3]
    widths = [columns * share // sum(SHARES) for share in SHARES]
    starts = [sum(widths[:i]) for i in range(len(widths))]
    product = 2 * rows * panels * columns
    short, wide = sketch.dtype, jnp.float32
    copies = pltpu.SemaphoreType.DMA
    lent, *parts = call(
        cut_kernel,
        (on_chip((half, rank), short), *(on_chip((panels, width), short) for width in widths)),
        (),
        0,
        hbm=(sketch, cluster_basis),
        scratch=(copies((6,)),),
    )
    own, tiles, kept = call(
        stage_kernel,
        (
            on_chip((panels, columns), short),
            on_chip((offsets, rows, panels), short),
            on_chip((half, rank), short),
        ),
        (parts[0],),
        0,
        hbm=(sketch, far_tiles, cluster_basis),
        scratch=(copies((3,)),),
    )
    lent = from_behind(lent, "group", 1)
    fars = [swap_far(part) for part in parts]
    near = swap_near(sketch)
    hit, miss, stays = call(
        local_kernel,
        (
            on_chip((rows, columns), wide),
            on_chip((rows, columns), short),
            on_chip((1, columns), wide),
        ),
        (tiles, own, near),
        2 * product,
        scalars=(row_blocks.reshape(-1), owner_route.reshape(-1)),
    )
    hit_turned, missed = call(
        turn_kernel,
        (on_chip((rank, half), short), on_chip((rank, columns), wide)),
        (kept, lent, miss, stays),
        product // 2,
    )
    out = None
    for i, (start, width) in enumerate(zip(starts, widths)):
        kept, sent = call(
            functools.partial(far_kernel, start),
            (on_chip((rank, width), wide), on_chip((rank, width), short)),
            (tiles, fars[i], hit, hit_turned, missed, stays),
            2 * product * width // columns,
        )
        out = call(
            functools.partial(join_kernel, start),
            pltpu.HBM((rank, columns), wide),
            (kept, from_behind(sent, "group", 1)),
            1 << 16,
            hbm=() if out is None else (out,),
            scratch=(on_chip((rank, width), wide), copies((2,))),
            to_hbm=True,
            alias=out is not None,
        )
    return out[None, None]


def contribute(summed, far_tiles, row_blocks, offset, current):
    product = jnp.einsum(
        "trk,kc->trc", far_tiles[0, 0, offset], current, preferred_element_type=jnp.float32
    )
    return summed.at[row_blocks[0, 0, offset]].add(product)


def ring_body(sketch, far_tiles, row_blocks, owner_route, cluster_basis):
    offsets = far_tiles.shape[2]
    radius = (offsets - 1) // 2
    groups = lax.axis_size("group")
    tile_rows = far_tiles.shape[4]
    columns = sketch.shape[1]
    summed = jnp.zeros((groups, tile_rows, columns), jnp.float32)
    for offset in range(offsets):
        current = from_behind(sketch, "blk", radius - offset) if offset != radius else sketch
        summed = contribute(summed, far_tiles, row_blocks, offset, current)
    sampled = summed.astype(jnp.bfloat16)
    ordered = jnp.zeros_like(sampled).at[owner_route[0, 0]].set(sampled)
    received = lax.all_to_all(ordered, "group", split_axis=0, concat_axis=0, tiled=True)
    stacked = received.reshape(received.shape[0] * received.shape[1], received.shape[2])
    coefficients = lax.dot_general(
        cluster_basis[0, 0], stacked, TRANSPOSED, preferred_element_type=jnp.float32
    )
    return coefficients[None, None]


def body(sketch, far_tiles, row_blocks, owner_route, cluster_basis):
    small = cluster_basis.shape[3] < far_tiles.shape[4]
    paired = lax.axis_size("group") == 2 and lax.axis_size("blk") % 2 == 0
    if small and paired and far_tiles.shape[2:4] == (3, 1):
        return paired_body(sketch, far_tiles, row_blocks, owner_route, cluster_basis)
    return ring_body(sketch, far_tiles, row_blocks, owner_route, cluster_basis)


def solution(mesh):
    placed = (
        P("blk", None),
        P("blk", "group", None, None, None, None),
        P("blk", "group", None, None),
        P("blk", "group", None),
        P("blk", "group", None, None),
    )
    return jax.shard_map(
        body, mesh=mesh, in_specs=placed, out_specs=P("blk", "group", None, None), check_vma=False
    )
```

```python
import functools

import jax
import jax.numpy as jnp
from jax import lax
from jax.experimental import pallas as pl
from jax.experimental.pallas import tpu as pltpu
from jax.sharding import PartitionSpec as P

SHARES = (1, 2)
TRANSPOSED = (((0,), (0,)), ((), ()))


def from_behind(array, axis, by):
    devices = lax.axis_size(axis)
    return lax.ppermute(array, axis, [(i, (i + by) % devices) for i in range(devices)])


def swap_near(array):
    devices = lax.axis_size("blk")
    return lax.ppermute(array, "blk", [(i, i ^ 1) for i in range(devices)])


def swap_far(array):
    devices = lax.axis_size("blk")
    return lax.ppermute(
        array, "blk", [(i, (i + 1 if i % 2 else i - 1) % devices) for i in range(devices)]
    )


def on_chip(shape, dtype):
    return pltpu.VMEM(shape, dtype)


def call(kernel, out_shape, arrays, flops, scalars=(), hbm=(), scratch=(), to_hbm=False, alias=False):
    scalar, vector, main = (
        pl.BlockSpec(memory_space=m) for m in (pltpu.SMEM, pltpu.VMEM, pltpu.HBM)
    )
    placed = list(scalars)
    placed += [pltpu.with_memory_space_constraint(x, pltpu.VMEM) for x in arrays]
    placed += [pltpu.with_memory_space_constraint(x, pltpu.HBM) for x in hbm]
    target = main if to_hbm else vector
    return pl.pallas_call(
        kernel,
        out_shape=out_shape,
        in_specs=[scalar] * len(scalars) + [vector] * len(arrays) + [main] * len(hbm),
        out_specs=tuple(target for _ in out_shape) if isinstance(out_shape, tuple) else target,
        scratch_shapes=list(scratch),
        input_output_aliases={len(placed) - 1: 0} if alias else {},
        compiler_params=pltpu.CompilerParams(vmem_limit_bytes=16 << 20),
        cost_estimate=pl.CostEstimate(flops=flops, bytes_accessed=1 << 10, transcendentals=0),
    )(*placed)


def far_offset():
    return 2 * lax.rem(lax.axis_index("blk"), 2)


def copy_all(pairs, sems):
    copies = [pltpu.make_async_copy(*pair, sems.at[i]) for i, pair in enumerate(pairs)]
    for copy in copies:
        copy.start()
    for copy in copies:
        copy.wait()


def half_rows(basis, group, half):
    return basis.at[0, 0, pl.ds(pl.multiple_of(group * half, half), half)]


def half_start(group, half):
    return pl.multiple_of(group * half, half)


def share_kernel(sketch, shared, sems):
    half, width = shared.shape
    rows = pl.ds(half_start(lax.axis_index("group"), half), half)
    copy_all([(sketch.at[rows, pl.ds(0, width)], shared)], sems)


def cut_kernel(begun, sketch, basis, lent, whole, sems):
    del begun
    theirs = half_rows(basis, 1 - lax.axis_index("group"), lent.shape[0])
    width = whole.shape[1]
    columns = pl.ds(sketch.shape[1] - width, width)
    copy_all([(sketch.at[:, columns], whole), (theirs, lent)], sems)


def stage_kernel(begun, sketch, tiles, basis, own, staged, kept, sems):
    del begun
    ours = half_rows(basis, lax.axis_index("group"), kept.shape[0])
    copy_all([(sketch, own), (tiles.at[0, 0, :, 0], staged), (ours, kept)], sems)


def local_kernel(row_blocks, owner_route, tiles, own, near, hit, miss, stays):
    far = far_offset()
    owner = owner_route[row_blocks[far]]
    own_hits = owner_route[row_blocks[1]] == owner
    near_hits = owner_route[row_blocks[2 - far]] == owner
    step = 256
    for place in range(0, own.shape[1], step):
        columns = pl.ds(place, step)
        first = jnp.dot(tiles[1], own[:, columns], preferred_element_type=jnp.float32)
        second = jnp.dot(tiles[2 - far], near[:, columns], preferred_element_type=jnp.float32)
        hit[:, columns] = jnp.where(own_hits, first, 0.0) + jnp.where(near_hits, second, 0.0)
        miss[:, columns] = (
            jnp.where(own_hits, 0.0, first) + jnp.where(near_hits, 0.0, second)
        ).astype(jnp.bfloat16)
    stays[...] = jnp.full(stays.shape, jnp.where(owner == lax.axis_index("group"), 1.0, 0.0))


def turn_kernel(kept, lent, miss, stays, hit_turned, missed):
    stay = stays[:, pl.ds(0, kept.shape[0])] > 0.0
    ours, theirs = kept[...].T, lent[...].T
    hit_turned[...] = jnp.where(stay, ours, theirs)
    missed[...] = jnp.dot(
        jnp.where(stay, theirs, ours), miss[...], preferred_element_type=jnp.float32
    )


def shared_kernel(start, tiles, ours, theirs, hit, hit_turned, missed, stays, kept, sent, far):
    half = ours.shape[0]
    group = lax.axis_index("group")
    far[pl.ds(half_start(group, half), half), :] = ours[...]
    far[pl.ds(half_start(1 - group, half), half), :] = theirs[...]
    far_kernel(start, tiles, far, hit, hit_turned, missed, stays, kept, sent)


def whole_kernel(start, before, *refs):
    del before
    far_kernel(start, *refs)


def far_kernel(start, tiles, far, hit, hit_turned, missed, stays, kept, sent):
    columns = pl.ds(start, far.shape[1])
    product = jnp.dot(tiles[far_offset()], far[...], preferred_element_type=jnp.float32)
    sampled = (hit[:, columns] + product).astype(jnp.bfloat16)
    made = jnp.dot(hit_turned[...], sampled, preferred_element_type=jnp.float32)
    stay = stays[:, columns] > 0.0
    other = missed[:, columns]
    sent[...] = jnp.where(stay, other, made).astype(jnp.bfloat16)
    kept[...] = jnp.where(stay, made, other)


def join_kernel(start, kept, received, *rest):
    out, total, sems = rest[-3:]
    total[...] = kept[...] + received[...].astype(jnp.float32)
    copy_all([(total, out.at[:, pl.ds(start, total.shape[1])])], sems)


def paired_body(sketch, far_tiles, row_blocks, owner_route, cluster_basis):
    panels, columns = sketch.shape
    offsets, rows = far_tiles.shape[2], far_tiles.shape[4]
    half, rank = cluster_basis.shape[2] // 2, cluster_basis.shape[3]
    widths = [columns * share // sum(SHARES) for share in SHARES]
    starts = [sum(widths[:i]) for i in range(len(widths))]
    product = 2 * rows * panels * columns
    short, wide = sketch.dtype, jnp.float32
    copies = pltpu.SemaphoreType.DMA
    shared = call(
        share_kernel,
        on_chip((panels // 2, widths[0]), short),
        (),
        0,
        hbm=(sketch,),
        scratch=(copies((1,)),),
    )
    lent, whole = call(
        cut_kernel,
        (on_chip((half, rank), short), on_chip((panels, widths[1]), short)),
        (shared,),
        0,
        hbm=(sketch, cluster_basis),
        scratch=(copies((2,)),),
    )
    own, tiles, kept = call(
        stage_kernel,
        (
            on_chip((panels, columns), short),
            on_chip((offsets, rows, panels), short),
            on_chip((half, rank), short),
        ),
        (lent,),
        10**10,
        hbm=(sketch, far_tiles, cluster_basis),
        scratch=(copies((3,)),),
    )
    lent = from_behind(lent, "group", 1)
    ours = swap_far(shared)
    whole = swap_far(whole)
    theirs = from_behind(ours, "group", 1)
    near = swap_near(sketch)
    hit, miss, stays = call(
        local_kernel,
        (
            on_chip((rows, columns), wide),
            on_chip((rows, columns), short),
            on_chip((1, columns), wide),
        ),
        (tiles, own, near),
        3 * 10**9,
        scalars=(row_blocks.reshape(-1), owner_route.reshape(-1)),
    )
    hit_turned, missed = call(
        turn_kernel,
        (on_chip((rank, half), short), on_chip((rank, columns), wide)),
        (kept, lent, miss, stays),
        0,
    )
    far = pltpu.VMEM((panels, widths[0]), short)
    work = (
        (0, widths[0], shared_kernel, (tiles, ours, theirs), 0, (far,)),
        (starts[1], widths[1], whole_kernel, (tiles, whole), 0, ()),
    )
    out = sent = None
    for start, width, kernel, inputs, flops, scratch in work:
        kept, sent = call(
            functools.partial(kernel, start),
            (on_chip((rank, width), wide), on_chip((rank, width), short)),
            (*(() if sent is None else (sent,)), *inputs, hit, hit_turned, missed, stays),
            flops,
            scratch=scratch,
        )
        out = call(
            functools.partial(join_kernel, start),
            pltpu.HBM((rank, columns), wide),
            (kept, from_behind(sent, "group", 1)),
            10**10 if out is None else 0,
            hbm=() if out is None else (out,),
            scratch=(on_chip((rank, width), wide), copies((1,))),
            to_hbm=True,
            alias=out is not None,
        )
    return out[None, None]


def contribute(summed, far_tiles, row_blocks, offset, current):
    product = jnp.einsum(
        "trk,kc->trc", far_tiles[0, 0, offset], current, preferred_element_type=jnp.float32
    )
    return summed.at[row_blocks[0, 0, offset]].add(product)


def ring_body(sketch, far_tiles, row_blocks, owner_route, cluster_basis):
    offsets = far_tiles.shape[2]
    radius = (offsets - 1) // 2
    groups = lax.axis_size("group")
    tile_rows = far_tiles.shape[4]
    columns = sketch.shape[1]
    summed = jnp.zeros((groups, tile_rows, columns), jnp.float32)
    for offset in range(offsets):
        current = from_behind(sketch, "blk", radius - offset) if offset != radius else sketch
        summed = contribute(summed, far_tiles, row_blocks, offset, current)
    sampled = summed.astype(jnp.bfloat16)
    ordered = jnp.zeros_like(sampled).at[owner_route[0, 0]].set(sampled)
    received = lax.all_to_all(ordered, "group", split_axis=0, concat_axis=0, tiled=True)
    stacked = received.reshape(received.shape[0] * received.shape[1], received.shape[2])
    coefficients = lax.dot_general(
        cluster_basis[0, 0], stacked, TRANSPOSED, preferred_element_type=jnp.float32
    )
    return coefficients[None, None]


def body(sketch, far_tiles, row_blocks, owner_route, cluster_basis):
    small = cluster_basis.shape[3] < far_tiles.shape[4]
    paired = lax.axis_size("group") == 2 and lax.axis_size("blk") % 2 == 0
    if small and paired and far_tiles.shape[2:4] == (3, 1):
        return paired_body(sketch, far_tiles, row_blocks, owner_route, cluster_basis)
    return ring_body(sketch, far_tiles, row_blocks, owner_route, cluster_basis)


def solution(mesh):
    placed = (
        P("blk", None),
        P("blk", "group", None, None, None, None),
        P("blk", "group", None, None),
        P("blk", "group", None),
        P("blk", "group", None, None),
    )
    return jax.shard_map(
        body, mesh=mesh, in_specs=placed, out_specs=P("blk", "group", None, None), check_vma=False
    )
```

```python
import functools

import jax
import jax.numpy as jnp
from jax import lax
from jax.experimental import pallas as pl
from jax.experimental.pallas import tpu as pltpu
from jax.sharding import PartitionSpec as P

SHARES = (3, 2, 1)
TRANSPOSED = (((0,), (0,)), ((), ()))


def from_behind(array, axis, by):
    devices = lax.axis_size(axis)
    return lax.ppermute(array, axis, [(i, (i + by) % devices) for i in range(devices)])


def swap_near(array):
    devices = lax.axis_size("blk")
    return lax.ppermute(array, "blk", [(i, i ^ 1) for i in range(devices)])


def swap_far(array):
    devices = lax.axis_size("blk")
    return lax.ppermute(
        array, "blk", [(i, (i + 1 if i % 2 else i - 1) % devices) for i in range(devices)]
    )


def on_chip(shape, dtype):
    return pltpu.VMEM(shape, dtype)


def call(kernel, out_shape, arrays, flops, scalars=(), hbm=(), scratch=(), to_hbm=False, alias=False):
    scalar, vector, main = (
        pl.BlockSpec(memory_space=m) for m in (pltpu.SMEM, pltpu.VMEM, pltpu.HBM)
    )
    placed = list(scalars)
    placed += [pltpu.with_memory_space_constraint(x, pltpu.VMEM) for x in arrays]
    placed += [pltpu.with_memory_space_constraint(x, pltpu.HBM) for x in hbm]
    target = main if to_hbm else vector
    return pl.pallas_call(
        kernel,
        out_shape=out_shape,
        in_specs=[scalar] * len(scalars) + [vector] * len(arrays) + [main] * len(hbm),
        out_specs=tuple(target for _ in out_shape) if isinstance(out_shape, tuple) else target,
        scratch_shapes=list(scratch),
        input_output_aliases={len(placed) - 1: 0} if alias else {},
        compiler_params=pltpu.CompilerParams(vmem_limit_bytes=16 << 20),
        cost_estimate=pl.CostEstimate(flops=flops, bytes_accessed=1 << 20, transcendentals=0),
    )(*placed)


def far_offset():
    return 2 * lax.rem(lax.axis_index("blk"), 2)


def copy_all(pairs, sems):
    copies = [pltpu.make_async_copy(*pair, sems.at[i]) for i, pair in enumerate(pairs)]
    for copy in copies:
        copy.start()
    for copy in copies:
        copy.wait()


def half_rows(basis, group, half):
    return basis.at[0, 0, pl.ds(pl.multiple_of(group * half, half), half)]


def cut_kernel(sketch, basis, lent, first, second, sems):
    theirs = half_rows(basis, 1 - lax.axis_index("group"), lent.shape[0])
    early, late = first.shape[1], second.shape[1]
    pairs = [
        (sketch.at[:, pl.ds(0, early)], first),
        (theirs, lent),
        (sketch.at[:, pl.ds(early, late)], second),
    ]
    copy_all(pairs, sems)


def stage_kernel(begun, sketch, tiles, basis, own, staged, kept, sems):
    del begun
    ours = half_rows(basis, lax.axis_index("group"), kept.shape[0])
    copy_all([(sketch, own), (tiles.at[0, 0, :, 0], staged), (ours, kept)], sems)


def local_kernel(row_blocks, owner_route, tiles, own, near, hit, miss, stays):
    far = far_offset()
    owner = owner_route[row_blocks[far]]
    own_hits = owner_route[row_blocks[1]] == owner
    near_hits = owner_route[row_blocks[2 - far]] == owner
    step = 256
    for place in range(0, own.shape[1], step):
        columns = pl.ds(place, step)
        first = jnp.dot(tiles[1], own[:, columns], preferred_element_type=jnp.float32)
        second = jnp.dot(tiles[2 - far], near[:, columns], preferred_element_type=jnp.float32)
        hit[:, columns] = jnp.where(own_hits, first, 0.0) + jnp.where(near_hits, second, 0.0)
        miss[:, columns] = (
            jnp.where(own_hits, 0.0, first) + jnp.where(near_hits, 0.0, second)
        ).astype(jnp.bfloat16)
    stays[...] = jnp.full(stays.shape, jnp.where(owner == lax.axis_index("group"), 1.0, 0.0))


def turn_kernel(start, kept, lent, miss, stays, own, hit_turned, missed, part):
    part[...] = own[:, pl.ds(start, part.shape[1])]
    stay = stays[:, pl.ds(0, kept.shape[0])] > 0.0
    ours, theirs = kept[...].T, lent[...].T
    hit_turned[...] = jnp.where(stay, ours, theirs)
    missed[...] = jnp.dot(
        jnp.where(stay, theirs, ours), miss[...], preferred_element_type=jnp.float32
    )


def far_kernel(start, tiles, far, hit, hit_turned, missed, stays, kept, sent):
    columns = pl.ds(start, far.shape[1])
    product = jnp.dot(tiles[far_offset()], far[...], preferred_element_type=jnp.float32)
    sampled = (hit[:, columns] + product).astype(jnp.bfloat16)
    made = jnp.dot(hit_turned[...], sampled, preferred_element_type=jnp.float32)
    stay = stays[:, columns] > 0.0
    other = missed[:, columns]
    sent[...] = jnp.where(stay, other, made).astype(jnp.bfloat16)
    kept[...] = jnp.where(stay, made, other)


def join_kernel(start, kept, received, *rest):
    out, total, sems = rest[-3:]
    total[...] = kept[...] + received[...].astype(jnp.float32)
    copy_all([(total, out.at[:, pl.ds(start, total.shape[1])])], sems)


def paired_body(sketch, far_tiles, row_blocks, owner_route, cluster_basis):
    panels, columns = sketch.shape
    offsets, rows = far_tiles.shape[2], far_tiles.shape[4]
    half, rank = cluster_basis.shape[2] // 2, cluster_basis.shape[3]
    widths = [columns * share // sum(SHARES) for share in SHARES]
    starts = [sum(widths[:i]) for i in range(len(widths))]
    product = 2 * rows * panels * columns
    short, wide = sketch.dtype, jnp.float32
    copies = pltpu.SemaphoreType.DMA
    lent, *parts = call(
        cut_kernel,
        (on_chip((half, rank), short), *(on_chip((panels, width), short) for width in widths[:2])),
        (),
        0,
        hbm=(sketch, cluster_basis),
        scratch=(copies((3,)),),
    )
    own, tiles, kept = call(
        stage_kernel,
        (
            on_chip((panels, columns), short),
            on_chip((offsets, rows, panels), short),
            on_chip((half, rank), short),
        ),
        (parts[0],),
        0,
        hbm=(sketch, far_tiles, cluster_basis),
        scratch=(copies((3,)),),
    )
    lent = from_behind(lent, "group", 1)
    fars = [swap_far(part) for part in parts]
    near = swap_near(sketch)
    hit, miss, stays = call(
        local_kernel,
        (
            on_chip((rows, columns), wide),
            on_chip((rows, columns), short),
            on_chip((1, columns), wide),
        ),
        (tiles, own, near),
        2 * product,
        scalars=(row_blocks.reshape(-1), owner_route.reshape(-1)),
    )
    hit_turned, missed, part = call(
        functools.partial(turn_kernel, starts[2]),
        (
            on_chip((rank, half), short),
            on_chip((rank, columns), wide),
            on_chip((panels, widths[2]), short),
        ),
        (kept, lent, miss, stays, own),
        product // 2,
    )
    fars.append(swap_far(part))
    out = None
    for i, (start, width) in enumerate(zip(starts, widths)):
        kept, sent = call(
            functools.partial(far_kernel, start),
            (on_chip((rank, width), wide), on_chip((rank, width), short)),
            (tiles, fars[i], hit, hit_turned, missed, stays),
            2 * product * width // columns,
        )
        out = call(
            functools.partial(join_kernel, start),
            pltpu.HBM((rank, columns), wide),
            (kept, from_behind(sent, "group", 1)),
            1 << 16,
            hbm=() if out is None else (out,),
            scratch=(on_chip((rank, width), wide), copies((1,))),
            to_hbm=True,
            alias=out is not None,
        )
    return out[None, None]


def contribute(summed, far_tiles, row_blocks, offset, current):
    product = jnp.einsum(
        "trk,kc->trc", far_tiles[0, 0, offset], current, preferred_element_type=jnp.float32
    )
    return summed.at[row_blocks[0, 0, offset]].add(product)


def ring_body(sketch, far_tiles, row_blocks, owner_route, cluster_basis):
    offsets = far_tiles.shape[2]
    radius = (offsets - 1) // 2
    groups = lax.axis_size("group")
    tile_rows = far_tiles.shape[4]
    columns = sketch.shape[1]
    summed = jnp.zeros((groups, tile_rows, columns), jnp.float32)
    for offset in range(offsets):
        current = from_behind(sketch, "blk", radius - offset) if offset != radius else sketch
        summed = contribute(summed, far_tiles, row_blocks, offset, current)
    sampled = summed.astype(jnp.bfloat16)
    ordered = jnp.zeros_like(sampled).at[owner_route[0, 0]].set(sampled)
    received = lax.all_to_all(ordered, "group", split_axis=0, concat_axis=0, tiled=True)
    stacked = received.reshape(received.shape[0] * received.shape[1], received.shape[2])
    coefficients = lax.dot_general(
        cluster_basis[0, 0], stacked, TRANSPOSED, preferred_element_type=jnp.float32
    )
    return coefficients[None, None]


def body(sketch, far_tiles, row_blocks, owner_route, cluster_basis):
    small = cluster_basis.shape[3] < far_tiles.shape[4]
    paired = lax.axis_size("group") == 2 and lax.axis_size("blk") % 2 == 0
    if small and paired and far_tiles.shape[2:4] == (3, 1):
        return paired_body(sketch, far_tiles, row_blocks, owner_route, cluster_basis)
    return ring_body(sketch, far_tiles, row_blocks, owner_route, cluster_basis)


def solution(mesh):
    placed = (
        P("blk", None),
        P("blk", "group", None, None, None, None),
        P("blk", "group", None, None),
        P("blk", "group", None),
        P("blk", "group", None, None),
    )
    return jax.shard_map(
        body, mesh=mesh, in_specs=placed, out_specs=P("blk", "group", None, None), check_vma=False
    )
```

```python
import functools

import jax
import jax.numpy as jnp
from jax import lax
from jax.experimental import pallas as pl
from jax.experimental.pallas import tpu as pltpu
from jax.sharding import PartitionSpec as P

SHARES = (2, 1)
TRANSPOSED = (((0,), (0,)), ((), ()))


def from_behind(array, axis, by):
    devices = lax.axis_size(axis)
    return lax.ppermute(array, axis, [(i, (i + by) % devices) for i in range(devices)])


def swap_near(array):
    devices = lax.axis_size("blk")
    return lax.ppermute(array, "blk", [(i, i ^ 1) for i in range(devices)])


def swap_far(array):
    devices = lax.axis_size("blk")
    return lax.ppermute(
        array, "blk", [(i, (i + 1 if i % 2 else i - 1) % devices) for i in range(devices)]
    )


def on_chip(shape, dtype):
    return pltpu.VMEM(shape, dtype)


def call(kernel, out_shape, arrays, flops, scalars=(), hbm=(), scratch=(), to_hbm=False, alias=False):
    scalar, vector, main = (
        pl.BlockSpec(memory_space=m) for m in (pltpu.SMEM, pltpu.VMEM, pltpu.HBM)
    )
    placed = list(scalars)
    placed += [pltpu.with_memory_space_constraint(x, pltpu.VMEM) for x in arrays]
    placed += [pltpu.with_memory_space_constraint(x, pltpu.HBM) for x in hbm]
    target = main if to_hbm else vector
    return pl.pallas_call(
        kernel,
        out_shape=out_shape,
        in_specs=[scalar] * len(scalars) + [vector] * len(arrays) + [main] * len(hbm),
        out_specs=tuple(target for _ in out_shape) if isinstance(out_shape, tuple) else target,
        scratch_shapes=list(scratch),
        input_output_aliases={len(placed) - 1: 0} if alias else {},
        compiler_params=pltpu.CompilerParams(vmem_limit_bytes=16 << 20),
        cost_estimate=pl.CostEstimate(flops=flops, bytes_accessed=1 << 20, transcendentals=0),
    )(*placed)


def far_offset():
    return 2 * lax.rem(lax.axis_index("blk"), 2)


def copy_all(pairs, sems):
    copies = [pltpu.make_async_copy(*pair, sems.at[i]) for i, pair in enumerate(pairs)]
    for copy in copies:
        copy.start()
    for copy in copies:
        copy.wait()


def half_rows(basis, group, half):
    return basis.at[0, 0, pl.ds(pl.multiple_of(group * half, half), half)]


def first_kernel(sketch, first, sems):
    copy_all([(sketch.at[:, pl.ds(0, first.shape[1])], first)], sems)


def cut_kernel(begun, sketch, basis, lent, second, sems):
    del begun
    theirs = half_rows(basis, 1 - lax.axis_index("group"), lent.shape[0])
    width = second.shape[1]
    columns = pl.ds(sketch.shape[1] - width, width)
    copy_all([(theirs, lent), (sketch.at[:, columns], second)], sems)


def stage_kernel(begun, sketch, tiles, basis, own, staged, kept, sems):
    del begun
    ours = half_rows(basis, lax.axis_index("group"), kept.shape[0])
    copy_all([(sketch, own), (tiles.at[0, 0, :, 0], staged), (ours, kept)], sems)


def local_kernel(row_blocks, owner_route, tiles, own, near, hit, miss, stays):
    far = far_offset()
    owner = owner_route[row_blocks[far]]
    own_hits = owner_route[row_blocks[1]] == owner
    near_hits = owner_route[row_blocks[2 - far]] == owner
    step = 256
    for place in range(0, own.shape[1], step):
        columns = pl.ds(place, step)
        first = jnp.dot(tiles[1], own[:, columns], preferred_element_type=jnp.float32)
        second = jnp.dot(tiles[2 - far], near[:, columns], preferred_element_type=jnp.float32)
        hit[:, columns] = jnp.where(own_hits, first, 0.0) + jnp.where(near_hits, second, 0.0)
        miss[:, columns] = (
            jnp.where(own_hits, 0.0, first) + jnp.where(near_hits, 0.0, second)
        ).astype(jnp.bfloat16)
    stays[...] = jnp.full(stays.shape, jnp.where(owner == lax.axis_index("group"), 1.0, 0.0))


def turn_kernel(kept, lent, miss, stays, hit_turned, missed):
    stay = stays[:, pl.ds(0, kept.shape[0])] > 0.0
    ours, theirs = kept[...].T, lent[...].T
    hit_turned[...] = jnp.where(stay, ours, theirs)
    missed[...] = jnp.dot(
        jnp.where(stay, theirs, ours), miss[...], preferred_element_type=jnp.float32
    )


def far_kernel(start, tiles, far, hit, hit_turned, missed, stays, kept, sent):
    columns = pl.ds(start, far.shape[1])
    product = jnp.dot(tiles[far_offset()], far[...], preferred_element_type=jnp.float32)
    sampled = (hit[:, columns] + product).astype(jnp.bfloat16)
    made = jnp.dot(hit_turned[...], sampled, preferred_element_type=jnp.float32)
    stay = stays[:, columns] > 0.0
    other = missed[:, columns]
    sent[...] = jnp.where(stay, other, made).astype(jnp.bfloat16)
    kept[...] = jnp.where(stay, made, other)


def join_kernel(start, kept, received, *rest):
    out, total, sems = rest[-3:]
    total[...] = kept[...] + received[...].astype(jnp.float32)
    copy_all([(total, out.at[:, pl.ds(start, total.shape[1])])], sems)


def paired_body(sketch, far_tiles, row_blocks, owner_route, cluster_basis):
    panels, columns = sketch.shape
    offsets, rows = far_tiles.shape[2], far_tiles.shape[4]
    half, rank = cluster_basis.shape[2] // 2, cluster_basis.shape[3]
    widths = [columns * share // sum(SHARES) for share in SHARES]
    starts = [sum(widths[:i]) for i in range(len(widths))]
    product = 2 * rows * panels * columns
    short, wide = sketch.dtype, jnp.float32
    copies = pltpu.SemaphoreType.DMA
    first = call(
        first_kernel,
        on_chip((panels, widths[0]), short),
        (),
        0,
        hbm=(sketch,),
        scratch=(copies((1,)),),
    )
    lent, second = call(
        cut_kernel,
        (on_chip((half, rank), short), on_chip((panels, widths[1]), short)),
        (first,),
        0,
        hbm=(sketch, cluster_basis),
        scratch=(copies((2,)),),
    )
    own, tiles, kept = call(
        stage_kernel,
        (
            on_chip((panels, columns), short),
            on_chip((offsets, rows, panels), short),
            on_chip((half, rank), short),
        ),
        (lent,),
        0,
        hbm=(sketch, far_tiles, cluster_basis),
        scratch=(copies((3,)),),
    )
    lent = from_behind(lent, "group", 1)
    fars = [swap_far(part) for part in (first, second)]
    near = swap_near(sketch)
    hit, miss, stays = call(
        local_kernel,
        (
            on_chip((rows, columns), wide),
            on_chip((rows, columns), short),
            on_chip((1, columns), wide),
        ),
        (tiles, own, near),
        2 * product,
        scalars=(row_blocks.reshape(-1), owner_route.reshape(-1)),
    )
    hit_turned, missed = call(
        turn_kernel,
        (on_chip((rank, half), short), on_chip((rank, columns), wide)),
        (kept, lent, miss, stays),
        product // 2,
    )
    out = None
    for i, (start, width) in enumerate(zip(starts, widths)):
        kept, sent = call(
            functools.partial(far_kernel, start),
            (on_chip((rank, width), wide), on_chip((rank, width), short)),
            (tiles, fars[i], hit, hit_turned, missed, stays),
            2 * product * width // columns,
        )
        out = call(
            functools.partial(join_kernel, start),
            pltpu.HBM((rank, columns), wide),
            (kept, from_behind(sent, "group", 1)),
            1 << 16,
            hbm=() if out is None else (out,),
            scratch=(on_chip((rank, width), wide), copies((1,))),
            to_hbm=True,
            alias=out is not None,
        )
    return out[None, None]


def contribute(summed, far_tiles, row_blocks, offset, current):
    product = jnp.einsum(
        "trk,kc->trc", far_tiles[0, 0, offset], current, preferred_element_type=jnp.float32
    )
    return summed.at[row_blocks[0, 0, offset]].add(product)


def ring_body(sketch, far_tiles, row_blocks, owner_route, cluster_basis):
    offsets = far_tiles.shape[2]
    radius = (offsets - 1) // 2
    groups = lax.axis_size("group")
    tile_rows = far_tiles.shape[4]
    columns = sketch.shape[1]
    summed = jnp.zeros((groups, tile_rows, columns), jnp.float32)
    for offset in range(offsets):
        current = from_behind(sketch, "blk", radius - offset) if offset != radius else sketch
        summed = contribute(summed, far_tiles, row_blocks, offset, current)
    sampled = summed.astype(jnp.bfloat16)
    ordered = jnp.zeros_like(sampled).at[owner_route[0, 0]].set(sampled)
    received = lax.all_to_all(ordered, "group", split_axis=0, concat_axis=0, tiled=True)
    stacked = received.reshape(received.shape[0] * received.shape[1], received.shape[2])
    coefficients = lax.dot_general(
        cluster_basis[0, 0], stacked, TRANSPOSED, preferred_element_type=jnp.float32
    )
    return coefficients[None, None]


def body(sketch, far_tiles, row_blocks, owner_route, cluster_basis):
    small = cluster_basis.shape[3] < far_tiles.shape[4]
    paired = lax.axis_size("group") == 2 and lax.axis_size("blk") % 2 == 0
    if small and paired and far_tiles.shape[2:4] == (3, 1):
        return paired_body(sketch, far_tiles, row_blocks, owner_route, cluster_basis)
    return ring_body(sketch, far_tiles, row_blocks, owner_route, cluster_basis)


def solution(mesh):
    placed = (
        P("blk", None),
        P("blk", "group", None, None, None, None),
        P("blk", "group", None, None),
        P("blk", "group", None),
        P("blk", "group", None, None),
    )
    return jax.shard_map(
        body, mesh=mesh, in_specs=placed, out_specs=P("blk", "group", None, None), check_vma=False
    )
```

```python
import functools

import jax
import jax.numpy as jnp
from jax import lax
from jax.experimental import pallas as pl
from jax.experimental.pallas import tpu as pltpu
from jax.sharding import PartitionSpec as P

SHARES = (2, 1)
TRANSPOSED = (((0,), (0,)), ((), ()))


def from_behind(array, axis, by):
    devices = lax.axis_size(axis)
    return lax.ppermute(array, axis, [(i, (i + by) % devices) for i in range(devices)])


def swap_near(array):
    devices = lax.axis_size("blk")
    return lax.ppermute(array, "blk", [(i, i ^ 1) for i in range(devices)])


def swap_far(array):
    devices = lax.axis_size("blk")
    return lax.ppermute(
        array, "blk", [(i, (i + 1 if i % 2 else i - 1) % devices) for i in range(devices)]
    )


def on_chip(shape, dtype):
    return pltpu.VMEM(shape, dtype)


def call(kernel, out_shape, arrays, flops, scalars=(), hbm=(), scratch=(), to_hbm=False, alias=False):
    scalar, vector, main = (
        pl.BlockSpec(memory_space=m) for m in (pltpu.SMEM, pltpu.VMEM, pltpu.HBM)
    )
    placed = list(scalars)
    placed += [pltpu.with_memory_space_constraint(x, pltpu.VMEM) for x in arrays]
    placed += [pltpu.with_memory_space_constraint(x, pltpu.HBM) for x in hbm]
    target = main if to_hbm else vector
    return pl.pallas_call(
        kernel,
        out_shape=out_shape,
        in_specs=[scalar] * len(scalars) + [vector] * len(arrays) + [main] * len(hbm),
        out_specs=tuple(target for _ in out_shape) if isinstance(out_shape, tuple) else target,
        scratch_shapes=list(scratch),
        input_output_aliases={len(placed) - 1: 0} if alias else {},
        compiler_params=pltpu.CompilerParams(vmem_limit_bytes=16 << 20),
        cost_estimate=pl.CostEstimate(flops=flops, bytes_accessed=1 << 20, transcendentals=0),
    )(*placed)


def far_offset():
    return 2 * lax.rem(lax.axis_index("blk"), 2)


def copy_all(pairs, sems):
    copies = [pltpu.make_async_copy(*pair, sems.at[i]) for i, pair in enumerate(pairs)]
    for copy in copies:
        copy.start()
    for copy in copies:
        copy.wait()


def half_rows(basis, group, half):
    return basis.at[0, 0, pl.ds(pl.multiple_of(group * half, half), half)]


def first_kernel(sketch, basis, lent, first, sems):
    theirs = half_rows(basis, 1 - lax.axis_index("group"), lent.shape[0])
    copy_all([(sketch.at[:, pl.ds(0, first.shape[1])], first), (theirs, lent)], sems)


def second_kernel(begun, sketch, second, sems):
    del begun
    width = second.shape[1]
    copy_all([(sketch.at[:, pl.ds(sketch.shape[1] - width, width)], second)], sems)


def stage_kernel(begun, sketch, tiles, basis, own, staged, kept, sems):
    del begun
    ours = half_rows(basis, lax.axis_index("group"), kept.shape[0])
    copy_all([(sketch, own), (tiles.at[0, 0, :, 0], staged), (ours, kept)], sems)


def local_kernel(row_blocks, owner_route, tiles, own, near, hit, miss, stays):
    far = far_offset()
    owner = owner_route[row_blocks[far]]
    own_hits = owner_route[row_blocks[1]] == owner
    near_hits = owner_route[row_blocks[2 - far]] == owner
    step = 256
    for place in range(0, own.shape[1], step):
        columns = pl.ds(place, step)
        first = jnp.dot(tiles[1], own[:, columns], preferred_element_type=jnp.float32)
        second = jnp.dot(tiles[2 - far], near[:, columns], preferred_element_type=jnp.float32)
        hit[:, columns] = jnp.where(own_hits, first, 0.0) + jnp.where(near_hits, second, 0.0)
        miss[:, columns] = (
            jnp.where(own_hits, 0.0, first) + jnp.where(near_hits, 0.0, second)
        ).astype(jnp.bfloat16)
    stays[...] = jnp.full(stays.shape, jnp.where(owner == lax.axis_index("group"), 1.0, 0.0))


def turn_kernel(kept, lent, miss, stays, hit_turned, missed):
    stay = stays[:, pl.ds(0, kept.shape[0])] > 0.0
    ours, theirs = kept[...].T, lent[...].T
    hit_turned[...] = jnp.where(stay, ours, theirs)
    missed[...] = jnp.dot(
        jnp.where(stay, theirs, ours), miss[...], preferred_element_type=jnp.float32
    )


def far_kernel(start, tiles, far, hit, hit_turned, missed, stays, kept, sent):
    columns = pl.ds(start, far.shape[1])
    product = jnp.dot(tiles[far_offset()], far[...], preferred_element_type=jnp.float32)
    sampled = (hit[:, columns] + product).astype(jnp.bfloat16)
    made = jnp.dot(hit_turned[...], sampled, preferred_element_type=jnp.float32)
    stay = stays[:, columns] > 0.0
    other = missed[:, columns]
    sent[...] = jnp.where(stay, other, made).astype(jnp.bfloat16)
    kept[...] = jnp.where(stay, made, other)


def join_kernel(start, kept, received, *rest):
    out, total, sems = rest[-3:]
    total[...] = kept[...] + received[...].astype(jnp.float32)
    copy_all([(total, out.at[:, pl.ds(start, total.shape[1])])], sems)


def paired_body(sketch, far_tiles, row_blocks, owner_route, cluster_basis):
    panels, columns = sketch.shape
    offsets, rows = far_tiles.shape[2], far_tiles.shape[4]
    half, rank = cluster_basis.shape[2] // 2, cluster_basis.shape[3]
    widths = [columns * share // sum(SHARES) for share in SHARES]
    starts = [sum(widths[:i]) for i in range(len(widths))]
    product = 2 * rows * panels * columns
    short, wide = sketch.dtype, jnp.float32
    copies = pltpu.SemaphoreType.DMA
    lent, first = call(
        first_kernel,
        (on_chip((half, rank), short), on_chip((panels, widths[0]), short)),
        (),
        0,
        hbm=(sketch, cluster_basis),
        scratch=(copies((2,)),),
    )
    second = call(
        second_kernel,
        on_chip((panels, widths[1]), short),
        (first,),
        0,
        hbm=(sketch,),
        scratch=(copies((1,)),),
    )
    own, tiles, kept = call(
        stage_kernel,
        (
            on_chip((panels, columns), short),
            on_chip((offsets, rows, panels), short),
            on_chip((half, rank), short),
        ),
        (second,),
        0,
        hbm=(sketch, far_tiles, cluster_basis),
        scratch=(copies((3,)),),
    )
    lent = from_behind(lent, "group", 1)
    fars = [swap_far(part) for part in (first, second)]
    near = swap_near(sketch)
    hit, miss, stays = call(
        local_kernel,
        (
            on_chip((rows, columns), wide),
            on_chip((rows, columns), short),
            on_chip((1, columns), wide),
        ),
        (tiles, own, near),
        2 * product,
        scalars=(row_blocks.reshape(-1), owner_route.reshape(-1)),
    )
    hit_turned, missed = call(
        turn_kernel,
        (on_chip((rank, half), short), on_chip((rank, columns), wide)),
        (kept, lent, miss, stays),
        product // 2,
    )
    out = None
    for i, (start, width) in enumerate(zip(starts, widths)):
        kept, sent = call(
            functools.partial(far_kernel, start),
            (on_chip((rank, width), wide), on_chip((rank, width), short)),
            (tiles, fars[i], hit, hit_turned, missed, stays),
            2 * product * width // columns,
        )
        out = call(
            functools.partial(join_kernel, start),
            pltpu.HBM((rank, columns), wide),
            (kept, from_behind(sent, "group", 1)),
            1 << 16,
            hbm=() if out is None else (out,),
            scratch=(on_chip((rank, width), wide), copies((1,))),
            to_hbm=True,
            alias=out is not None,
        )
    return out[None, None]


def contribute(summed, far_tiles, row_blocks, offset, current):
    product = jnp.einsum(
        "trk,kc->trc", far_tiles[0, 0, offset], current, preferred_element_type=jnp.float32
    )
    return summed.at[row_blocks[0, 0, offset]].add(product)


def ring_body(sketch, far_tiles, row_blocks, owner_route, cluster_basis):
    offsets = far_tiles.shape[2]
    radius = (offsets - 1) // 2
    groups = lax.axis_size("group")
    tile_rows = far_tiles.shape[4]
    columns = sketch.shape[1]
    summed = jnp.zeros((groups, tile_rows, columns), jnp.float32)
    for offset in range(offsets):
        current = from_behind(sketch, "blk", radius - offset) if offset != radius else sketch
        summed = contribute(summed, far_tiles, row_blocks, offset, current)
    sampled = summed.astype(jnp.bfloat16)
    ordered = jnp.zeros_like(sampled).at[owner_route[0, 0]].set(sampled)
    received = lax.all_to_all(ordered, "group", split_axis=0, concat_axis=0, tiled=True)
    stacked = received.reshape(received.shape[0] * received.shape[1], received.shape[2])
    coefficients = lax.dot_general(
        cluster_basis[0, 0], stacked, TRANSPOSED, preferred_element_type=jnp.float32
    )
    return coefficients[None, None]


def body(sketch, far_tiles, row_blocks, owner_route, cluster_basis):
    small = cluster_basis.shape[3] < far_tiles.shape[4]
    paired = lax.axis_size("group") == 2 and lax.axis_size("blk") % 2 == 0
    if small and paired and far_tiles.shape[2:4] == (3, 1):
        return paired_body(sketch, far_tiles, row_blocks, owner_route, cluster_basis)
    return ring_body(sketch, far_tiles, row_blocks, owner_route, cluster_basis)


def solution(mesh):
    placed = (
        P("blk", None),
        P("blk", "group", None, None, None, None),
        P("blk", "group", None, None),
        P("blk", "group", None),
        P("blk", "group", None, None),
    )
    return jax.shard_map(
        body, mesh=mesh, in_specs=placed, out_specs=P("blk", "group", None, None), check_vma=False
    )
```

```python
import functools

import jax
import jax.numpy as jnp
from jax import lax
from jax.experimental import pallas as pl
from jax.experimental.pallas import tpu as pltpu
from jax.sharding import PartitionSpec as P

SHARES = (2, 1)
TRANSPOSED = (((0,), (0,)), ((), ()))


def from_behind(array, axis, by):
    devices = lax.axis_size(axis)
    return lax.ppermute(array, axis, [(i, (i + by) % devices) for i in range(devices)])


def swap_near(array):
    devices = lax.axis_size("blk")
    return lax.ppermute(array, "blk", [(i, i ^ 1) for i in range(devices)])


def swap_far(array):
    devices = lax.axis_size("blk")
    return lax.ppermute(
        array, "blk", [(i, (i + 1 if i % 2 else i - 1) % devices) for i in range(devices)]
    )


def on_chip(shape, dtype):
    return pltpu.VMEM(shape, dtype)


def call(kernel, out_shape, arrays, flops, scalars=(), hbm=(), scratch=(), to_hbm=False, alias=False):
    scalar, vector, main = (
        pl.BlockSpec(memory_space=m) for m in (pltpu.SMEM, pltpu.VMEM, pltpu.HBM)
    )
    placed = list(scalars)
    placed += [pltpu.with_memory_space_constraint(x, pltpu.VMEM) for x in arrays]
    placed += [pltpu.with_memory_space_constraint(x, pltpu.HBM) for x in hbm]
    target = main if to_hbm else vector
    return pl.pallas_call(
        kernel,
        out_shape=out_shape,
        in_specs=[scalar] * len(scalars) + [vector] * len(arrays) + [main] * len(hbm),
        out_specs=tuple(target for _ in out_shape) if isinstance(out_shape, tuple) else target,
        scratch_shapes=list(scratch),
        input_output_aliases={len(placed) - 1: 0} if alias else {},
        compiler_params=pltpu.CompilerParams(vmem_limit_bytes=16 << 20),
        cost_estimate=pl.CostEstimate(flops=flops, bytes_accessed=1 << 20, transcendentals=0),
    )(*placed)


def far_offset():
    return 2 * lax.rem(lax.axis_index("blk"), 2)


def copy_all(pairs, sems):
    copies = [pltpu.make_async_copy(*pair, sems.at[i]) for i, pair in enumerate(pairs)]
    for copy in copies:
        copy.start()
    for copy in copies:
        copy.wait()


def half_rows(basis, group, half):
    return basis.at[0, 0, pl.ds(pl.multiple_of(group * half, half), half)]


def row_blocks_of(array, count):
    rows = array.shape[0] // count
    return [pl.ds(i * rows, rows) for i in range(count)]


def cut_kernel(sketch, basis, lent, first, second, sems):
    theirs = half_rows(basis, 1 - lax.axis_index("group"), lent.shape[0])
    early, late = pl.ds(0, first.shape[1]), pl.ds(first.shape[1], second.shape[1])
    pairs = [(sketch.at[:, early], first)]
    pairs += [(theirs, lent), (sketch.at[:, late], second)]
    copy_all(pairs, sems)


def stage_kernel(begun, sketch, tiles, basis, own, staged, kept, sems):
    del begun
    ours = half_rows(basis, lax.axis_index("group"), kept.shape[0])
    copy_all([(sketch, own), (tiles.at[0, 0, :, 0], staged), (ours, kept)], sems)


def local_kernel(row_blocks, owner_route, tiles, own, near, hit, miss, stays):
    far = far_offset()
    owner = owner_route[row_blocks[far]]
    own_hits = owner_route[row_blocks[1]] == owner
    near_hits = owner_route[row_blocks[2 - far]] == owner
    step = 256
    for place in range(0, own.shape[1], step):
        columns = pl.ds(place, step)
        first = jnp.dot(tiles[1], own[:, columns], preferred_element_type=jnp.float32)
        second = jnp.dot(tiles[2 - far], near[:, columns], preferred_element_type=jnp.float32)
        hit[:, columns] = jnp.where(own_hits, first, 0.0) + jnp.where(near_hits, second, 0.0)
        miss[:, columns] = (
            jnp.where(own_hits, 0.0, first) + jnp.where(near_hits, 0.0, second)
        ).astype(jnp.bfloat16)
    stays[...] = jnp.full(stays.shape, jnp.where(owner == lax.axis_index("group"), 1.0, 0.0))


def turn_kernel(kept, lent, miss, stays, hit_turned, missed):
    stay = stays[:, pl.ds(0, kept.shape[0])] > 0.0
    ours, theirs = kept[...].T, lent[...].T
    hit_turned[...] = jnp.where(stay, ours, theirs)
    missed[...] = jnp.dot(
        jnp.where(stay, theirs, ours), miss[...], preferred_element_type=jnp.float32
    )


def far_kernel(start, tiles, far, hit, hit_turned, missed, stays, kept, sent):
    columns = pl.ds(start, far.shape[1])
    offset = far_offset()
    sampled = []
    for rows in row_blocks_of(hit, 2):
        product = jnp.dot(tiles[offset, rows], far[...], preferred_element_type=jnp.float32)
        sampled.append((hit[rows, columns] + product).astype(jnp.bfloat16))
    made = jnp.dot(
        hit_turned[...], jnp.concatenate(sampled), preferred_element_type=jnp.float32
    )
    stay = stays[:, columns] > 0.0
    other = missed[:, columns]
    sent[...] = jnp.where(stay, other, made).astype(jnp.bfloat16)
    kept[...] = jnp.where(stay, made, other)


def join_kernel(start, kept, received, *rest):
    out, total, sems = rest[-3:]
    columns = pl.ds(start, total.shape[1])
    under_way = []
    for i, rows in enumerate(row_blocks_of(total, 2)):
        total[rows] = kept[rows] + received[rows].astype(jnp.float32)
        copy = pltpu.make_async_copy(total.at[rows], out.at[rows, columns], sems.at[i])
        copy.start()
        under_way.append(copy)
    for copy in under_way:
        copy.wait()


def paired_body(sketch, far_tiles, row_blocks, owner_route, cluster_basis):
    panels, columns = sketch.shape
    offsets, rows = far_tiles.shape[2], far_tiles.shape[4]
    half, rank = cluster_basis.shape[2] // 2, cluster_basis.shape[3]
    widths = [columns * share // sum(SHARES) for share in SHARES]
    starts = [sum(widths[:i]) for i in range(len(widths))]
    product = 2 * rows * panels * columns
    short, wide = sketch.dtype, jnp.float32
    copies = pltpu.SemaphoreType.DMA
    lent, *parts = call(
        cut_kernel,
        (on_chip((half, rank), short), *(on_chip((panels, width), short) for width in widths)),
        (),
        0,
        hbm=(sketch, cluster_basis),
        scratch=(copies((3,)),),
    )
    own, tiles, kept = call(
        stage_kernel,
        (
            on_chip((panels, columns), short),
            on_chip((offsets, rows, panels), short),
            on_chip((half, rank), short),
        ),
        (parts[0],),
        0,
        hbm=(sketch, far_tiles, cluster_basis),
        scratch=(copies((3,)),),
    )
    lent = from_behind(lent, "group", 1)
    fars = [swap_far(part) for part in parts]
    near = swap_near(sketch)
    hit, miss, stays = call(
        local_kernel,
        (
            on_chip((rows, columns), wide),
            on_chip((rows, columns), short),
            on_chip((1, columns), wide),
        ),
        (tiles, own, near),
        2 * product,
        scalars=(row_blocks.reshape(-1), owner_route.reshape(-1)),
    )
    hit_turned, missed = call(
        turn_kernel,
        (on_chip((rank, half), short), on_chip((rank, columns), wide)),
        (kept, lent, miss, stays),
        product // 2,
    )
    out = None
    for i, (start, width) in enumerate(zip(starts, widths)):
        kept, sent = call(
            functools.partial(far_kernel, start),
            (on_chip((rank, width), wide), on_chip((rank, width), short)),
            (tiles, fars[i], hit, hit_turned, missed, stays),
            2 * product * width // columns,
        )
        out = call(
            functools.partial(join_kernel, start),
            pltpu.HBM((rank, columns), wide),
            (kept, from_behind(sent, "group", 1)),
            1 << 16,
            hbm=() if out is None else (out,),
            scratch=(on_chip((rank, width), wide), copies((2,))),
            to_hbm=True,
            alias=out is not None,
        )
    return out[None, None]


def contribute(summed, far_tiles, row_blocks, offset, current):
    product = jnp.einsum(
        "trk,kc->trc", far_tiles[0, 0, offset], current, preferred_element_type=jnp.float32
    )
    return summed.at[row_blocks[0, 0, offset]].add(product)


def ring_body(sketch, far_tiles, row_blocks, owner_route, cluster_basis):
    offsets = far_tiles.shape[2]
    radius = (offsets - 1) // 2
    groups = lax.axis_size("group")
    tile_rows = far_tiles.shape[4]
    columns = sketch.shape[1]
    summed = jnp.zeros((groups, tile_rows, columns), jnp.float32)
    for offset in range(offsets):
        current = from_behind(sketch, "blk", radius - offset) if offset != radius else sketch
        summed = contribute(summed, far_tiles, row_blocks, offset, current)
    sampled = summed.astype(jnp.bfloat16)
    ordered = jnp.zeros_like(sampled).at[owner_route[0, 0]].set(sampled)
    received = lax.all_to_all(ordered, "group", split_axis=0, concat_axis=0, tiled=True)
    stacked = received.reshape(received.shape[0] * received.shape[1], received.shape[2])
    coefficients = lax.dot_general(
        cluster_basis[0, 0], stacked, TRANSPOSED, preferred_element_type=jnp.float32
    )
    return coefficients[None, None]


def body(sketch, far_tiles, row_blocks, owner_route, cluster_basis):
    small = cluster_basis.shape[3] < far_tiles.shape[4]
    paired = lax.axis_size("group") == 2 and lax.axis_size("blk") % 2 == 0
    if small and paired and far_tiles.shape[2:4] == (3, 1):
        return paired_body(sketch, far_tiles, row_blocks, owner_route, cluster_basis)
    return ring_body(sketch, far_tiles, row_blocks, owner_route, cluster_basis)


def solution(mesh):
    placed = (
        P("blk", None),
        P("blk", "group", None, None, None, None),
        P("blk", "group", None, None),
        P("blk", "group", None),
        P("blk", "group", None, None),
    )
    return jax.shard_map(
        body, mesh=mesh, in_specs=placed, out_specs=P("blk", "group", None, None), check_vma=False
    )
```
